256 devices in a mesh: ctx: 16 (over y, x), exp: 16 (over z, core).
Axes of the slice: x: 4, y: 4, z: 8, core: 2. Of those that a mesh axis runs over, the one named last changes fastest.
Arguments:
- tokens: bfloat16 [128, 4096], P('exp', 'ctx'), may hold values from -4.2 to 4.2, as said below
- attn_gain: float32 [4096], P('ctx'), may hold values from 0.1 to 1.9
- w_qkv: bfloat16 [4096, 5120], P('ctx'), may hold values from -0.09375 to 0.09375
- w_out: bfloat16 [4096, 4096], P(None, 'ctx'), may hold values from -0.09375 to 0.09375
- k_cache: bfloat16 [128, 2048, 512], P('exp', 'ctx'), may hold values from -480 to 480
- value_cache: bfloat16 [128, 2048, 512], P('exp', 'ctx'), may hold values from -24 to 24
- lengths: int32 [128], P('exp'), may hold values from 1 to 2047
- moe_gain: float32 [4096], P('ctx'), may hold values from 0.1 to 1.9
- routes: int32 [128, 8], P('exp'), may hold values from 0 to 63, all different within a row; in each aligned block of 8 rows (0 to 7, 8 to 15, ...) at most 2 rows name the same one
- gates: float32 [128, 8], P('exp'), may hold values from 0.05 to 0.3
- w_in: bfloat16 [64, 4096, 1536], P('exp', 'ctx'), may hold values from -0.09375 to 0.09375
- w_down: bfloat16 [64, 768, 4096], P('exp', None, 'ctx'), may hold values from -0.21875 to 0.21875
Outputs:
- context: bfloat16 [128, 4096], P('exp')
- layer_out: bfloat16 [128, 4096], P('exp', 'ctx')
The draws below stay inside these ranges and needn't reach their ends.
Inputs may be any that keep to these rules, and one draw needn't show every extreme that they name: Among the 64 routes of the tokens of one index of exp, at most 2 name one expert, and in every draw some expert is named exactly 2 times there. `tokens`: residual features.
All inputs are finite; a program needn't handle non-finite values.
Results may differ from the reference program's by a relative error of at most 0.04.
Values may be sent and summed in bfloat16 or wider, within the bound.
No kernel may reach another device: no remote copies, remote signals or barrier semaphores. Data moves between devices by JAX's collectives and lax.ppermute only.
A program may use at most 64 MiB of HBM per device.

```python
import math
import jax
import jax.numpy as jnp
import numpy as np
from jax import lax

D = 4096
QUERY_HEADS = 32
KEY_VALUE_HEADS = 4
HEAD_DIMENSION = 128
FFE = 768
TOPK = 8
B_EXP = 8
EXPERTS = 64
BATCH_SEQUENCES = 128
CACHE_POSITIONS = 2048
CAP = 2
QKV = 5120
N_EXP = 16


def draw_k_cache(key, part):
    key = jax.random.fold_in(key, 11)
    base_key = jax.random.fold_in(key, 0)
    array_shape = (BATCH_SEQUENCES, CACHE_POSITIONS, KEY_VALUE_HEADS * HEAD_DIMENSION)
    base = jnp.clip(jax.random.normal(base_key, array_shape, jnp.float32), -6.0, 6.0) * 1.5
    return base.astype(jnp.bfloat16)


def column_scales(key, low, high):
    place = jnp.arange(D).astype(jnp.float32) / (D - 1)
    rough = jax.random.uniform(key, (D,), jnp.float32, -0.15, 0.15)
    return jnp.exp(jnp.log(low) + (jnp.log(high) - jnp.log(low)) * place + rough)


def draw_tokens(key, part):
    key = jax.random.fold_in(key, 5)
    value_key, scale_key = jax.random.split(key, 2)
    spread = column_scales(scale_key, 0.4, 1.2)
    base = jnp.clip(jax.random.normal(value_key, (BATCH_SEQUENCES, D), jnp.float32), -3.0, 3.0)
    values = jnp.clip(base * spread[None, :], -4.2, 4.2)
    return values.astype(jnp.bfloat16)


def place_ends(array, stream_key, least, largest):
    longest = array.shape.index(max(array.shape))
    spots = []
    for shift in (0, 1):
        where = [jax.random.randint(jax.random.fold_in(stream_key, axis), (), 0, length) for axis, length in enumerate(array.shape)]
        where[longest] = (where[longest] + shift) % array.shape[longest]
        spots.append(tuple(where))
    return array.at[spots[0]].set(least).at[spots[1]].set(largest)


def steps_of(own_key, shape, pieces, least, largest):
    level = 1.0
    for axis_at, blocks in pieces:
        steps = jax.random.uniform(jax.random.fold_in(jax.random.fold_in(own_key, 6), axis_at), (blocks,), jnp.float32, least / len(pieces), largest / len(pieces))
        level = level * jnp.repeat(jnp.exp(steps), shape[axis_at] // blocks).reshape((-1,) + (1,) * (len(shape) - 1 - axis_at))
    return level


def assign_block(key, own, number, rows, amount, top, reach, skew):
    ranking = jax.random.permutation(key, amount)
    crowded, ordinary = portions_of(amount, rows * top, reach, skew, True), portions_of(amount, rows * top, reach, skew, False)
    places = jnp.arange(amount)

    def named(tallies, rotation):
        used = int((tallies > 0).sum())
        fixed = max(1, used // 4)
        shifted = fixed + (places - fixed + rotation * (used - fixed)) % max(1, amount - fixed)
        return jnp.zeros((amount,), jnp.int32).at[ranking[jnp.where(places < fixed, places, shifted)]].set(jnp.asarray(tallies, jnp.int32))

    tallies = jnp.where(number % 4 == 0, named(crowded, number // 4), named(ordinary, number - number // 4 - 1))
    mixed = jax.random.permutation(jax.random.fold_in(own, 3), amount)
    donor, receiver = mixed[0:amount // 2 * 2:2], mixed[1:amount // 2 * 2:2]
    slack = jnp.minimum(tallies[donor] - 1, reach - tallies[receiver]) // 2
    slack = jnp.where((donor == ranking[0]) | (receiver == ranking[0]) | (tallies[receiver] == 0), 0, jnp.maximum(slack, 0))
    shifted = jax.random.randint(jax.random.fold_in(own, 4), (amount // 2,), 0, 1 << 20) % (slack + 1)
    tallies = tallies.at[donor].add(-shifted).at[receiver].add(shifted)
    members = jnp.searchsorted(jnp.cumsum(tallies), jnp.arange(rows * top), side="right").astype(jnp.int32)
    listing = members.reshape(top, rows).T
    listing = listing[jax.random.permutation(jax.random.fold_in(own, 1), rows)]
    rotation = jax.random.randint(jax.random.fold_in(own, 2), (rows, 1), 0, top)
    return jnp.take_along_axis(listing, (jnp.arange(top)[None, :] + rotation) % top, axis=1)


def portions_of(number_of, total, most, skew, full):
    weights = [(1 << 20) // math.isqrt(rank ** skew) + 1 for rank in range(1, number_of + 1)]
    largest = most if full else min(most, max(-(-total // number_of), total * weights[0] // sum(weights)))
    least = 1 if total - largest >= number_of - 1 else 0
    given, surplus = [largest] + [least] * (number_of - 1), total - largest - least * (number_of - 1)
    while surplus > 0:
        candidates = [i for i in range(1, number_of) if given[i] < largest] or [i for i in range(1, number_of) if given[i] < most]
        mass, budget = sum([weights[i] for i in candidates]), surplus
        for i in candidates:
            addition = min(most - given[i], max(1, budget * weights[i] // mass), surplus)
            given[i] = given[i] + addition
            surplus = surplus - addition
    return np.array(given)


def normal_values(own_key, extent, scale, limit, cuts=(), kind=jnp.bfloat16):
    level = steps_of(own_key, extent, cuts, -0.22, 0.18) if cuts else 1.0
    array = jax.random.normal(own_key, extent, jnp.float32) * scale * level
    return jnp.minimum(jnp.maximum(array, -limit), limit).astype(kind)


def setup_inputs(seed: int = 0) -> dict:
    key_list = jax.random.split(jax.random.key(seed), 13)
    tokens = draw_tokens(jax.random.fold_in(key_list[12], 71), 0)
    attn_gain = jnp.clip(1.0 + 0.18 * jax.random.normal(key_list[1], (D,), jnp.float32), 0.1, 1.9)
    w_qkv = normal_values(key_list[2], (D, QKV), D ** -0.5, 0.09375, ((0, 16),))
    w_out = normal_values(key_list[3], (QUERY_HEADS * HEAD_DIMENSION, D), (QUERY_HEADS * HEAD_DIMENSION) ** -0.5, 0.09375, ((1, 16),))
    k_cache = draw_k_cache(jax.random.fold_in(key_list[12], 71), 0)
    value_cache = normal_values(key_list[5], (BATCH_SEQUENCES, CACHE_POSITIONS, KEY_VALUE_HEADS * HEAD_DIMENSION), 4.0, 24.0, ((0, 16), (1, 16)))
    lengths = place_ends(jax.random.randint(key_list[6], (BATCH_SEQUENCES,), 1, CACHE_POSITIONS), jax.random.fold_in(key_list[6], 1), 1, CACHE_POSITIONS - 1).astype(jnp.int32)
    moe_gain = jnp.clip(1.0 + 0.18 * jax.random.normal(key_list[7], (D,), jnp.float32), 0.1, 1.9)
    routes_keys = jax.random.split(jax.random.fold_in(key_list[8], 1), BATCH_SEQUENCES // B_EXP)
    routes_turns = jax.random.permutation(jax.random.fold_in(key_list[8], 3), BATCH_SEQUENCES // B_EXP)
    routes = jax.vmap(lambda own, number: assign_block(jax.random.fold_in(key_list[8], 2), own, number, B_EXP, EXPERTS, TOPK, CAP, 2))(routes_keys, routes_turns).reshape((BATCH_SEQUENCES, TOPK))
    gates = jnp.clip(0.05 + 0.25 * jax.random.uniform(key_list[9], (BATCH_SEQUENCES, TOPK), jnp.float32) ** steps_of(key_list[9], (BATCH_SEQUENCES, TOPK), ((0, 16),), -0.2, 0.2), 0.05, 0.3)
    w_in = normal_values(key_list[10], (EXPERTS, D, 2 * FFE), D ** -0.5, 0.09375, ((0, 16), (1, 16)))
    w_down = normal_values(key_list[11], (EXPERTS, FFE, D), FFE ** -0.5, 0.21875, ((0, 16), (2, 16)))
    return dict(tokens=tokens, attn_gain=attn_gain, w_qkv=w_qkv, w_out=w_out, k_cache=k_cache, value_cache=value_cache, lengths=lengths, moe_gain=moe_gain, routes=routes, gates=gates, w_in=w_in, w_down=w_down)


def apply_rotary(vec, pos):
    half = vec.shape[-1] // 2
    freq = jnp.exp(-jnp.log(1000000.0) * jnp.arange(half).astype(jnp.float32) / half)
    angle = pos.astype(jnp.float32)[:, None] * freq[None, :]
    cosine = jnp.cos(angle)[:, None, :]
    sine = jnp.sin(angle)[:, None, :]
    lower = vec[..., :half]
    upper = vec[..., half:]
    return jnp.concatenate([lower * cosine - upper * sine, upper * cosine + lower * sine], -1)

def reference(tokens, attn_gain, w_qkv, w_out, k_cache, value_cache, lengths, moe_gain, routes, gates, w_in, w_down):
    query_group = QUERY_HEADS // KEY_VALUE_HEADS
    scale = 1.0 / jnp.sqrt(jnp.float32(HEAD_DIMENSION))
    xf = tokens.astype(jnp.float32)
    scaled = (xf * attn_gain).astype(jnp.bfloat16)
    msq = lax.optimization_barrier(jnp.mean(xf * xf, -1, keepdims=True))
    projection_matrix = jnp.dot(scaled, w_qkv, preferred_element_type=jnp.float32) * lax.rsqrt(msq + 1e-06)
    query = apply_rotary(projection_matrix[:, :QUERY_HEADS * HEAD_DIMENSION].reshape(BATCH_SEQUENCES, QUERY_HEADS, HEAD_DIMENSION), lengths)
    fresh_key = apply_rotary(projection_matrix[:, QUERY_HEADS * HEAD_DIMENSION:QUERY_HEADS * HEAD_DIMENSION + KEY_VALUE_HEADS * HEAD_DIMENSION].reshape(BATCH_SEQUENCES, KEY_VALUE_HEADS, HEAD_DIMENSION), lengths)
    fresh_value = projection_matrix[:, QUERY_HEADS * HEAD_DIMENSION + KEY_VALUE_HEADS * HEAD_DIMENSION:].reshape(BATCH_SEQUENCES, KEY_VALUE_HEADS, HEAD_DIMENSION)

    def attend(items):
        single_query, single_key, single_value, length, kn_one, vn_one = items
        grouped_queries = single_query.reshape(KEY_VALUE_HEADS, query_group, HEAD_DIMENSION)
        cached_keys = single_key.astype(jnp.float32).reshape(CACHE_POSITIONS, KEY_VALUE_HEADS, HEAD_DIMENSION)
        cached_values = single_value.astype(jnp.float32).reshape(CACHE_POSITIONS, KEY_VALUE_HEADS, HEAD_DIMENSION)
        scores = jnp.einsum('hgd,lhd->hgl', grouped_queries, cached_keys) * scale
        live = jnp.arange(CACHE_POSITIONS) < length
        scores = jnp.where(live[None, None, :], scores, -1e+30)
        s_new = jnp.einsum('hgd,hd->hg', grouped_queries, kn_one) * scale
        top = jnp.maximum(lax.optimization_barrier(jnp.max(scores, -1)), s_new)
        weights = jnp.where(live[None, None, :], jnp.exp(scores - top[..., None]), 0.0)
        w_new = jnp.exp(s_new - top)
        total = lax.optimization_barrier(jnp.sum(weights, -1)) + w_new
        acc = jnp.einsum('hgl,lhd->hgd', weights, cached_values) + w_new[..., None] * vn_one[:, None, :]
        return (acc / total[..., None]).reshape(QUERY_HEADS * HEAD_DIMENSION)
    context = lax.map(attend, (query, k_cache, value_cache, lengths, fresh_key, fresh_value)).astype(jnp.bfloat16)
    attn_out = jnp.dot(context, w_out, preferred_element_type=jnp.float32)
    resid = (xf + attn_out).astype(jnp.bfloat16)
    rf = resid.astype(jnp.float32)
    ms2 = lax.optimization_barrier(jnp.mean(rf * rf, -1, keepdims=True))
    normed = (rf * lax.rsqrt(ms2 + 1e-06) * moe_gain).astype(jnp.bfloat16)
    per_dev = routes.reshape(N_EXP, B_EXP * TOPK)
    onehot = (per_dev[..., None] == jnp.arange(EXPERTS)[None, None, :]).astype(jnp.int32)
    rank = lax.optimization_barrier(jnp.sum((jnp.cumsum(onehot, 1) - onehot) * onehot, -1))
    source = jnp.arange(N_EXP).astype(jnp.int32)[:, None]
    column = (source * CAP + rank).reshape(-1).astype(jnp.int32)
    flat_ids = per_dev.reshape(-1).astype(jnp.int32)
    token_of = (jnp.arange(BATCH_SEQUENCES * TOPK) // TOPK).astype(jnp.int32)
    table = jnp.zeros((EXPERTS, N_EXP * CAP), jnp.int32).at[flat_ids, column].set(token_of)

    def expert(items):
        rows_idx, w_one, d_one = items
        rows = normed[rows_idx]
        gate_up = jnp.dot(rows, w_one, preferred_element_type=jnp.float32)
        act = (jax.nn.silu(gate_up[:, :FFE]) * gate_up[:, FFE:]).astype(jnp.bfloat16)
        return jnp.dot(act, d_one, preferred_element_type=jnp.float32).astype(jnp.bfloat16)
    outputs = lax.map(expert, (table, w_in, w_down))
    picked = outputs[flat_ids, column].astype(jnp.float32).reshape(BATCH_SEQUENCES, TOPK, D)
    moe = lax.optimization_barrier(jnp.sum(picked * gates[..., None], 1))
    layer_out = (rf + moe).astype(jnp.bfloat16)
    return (context, layer_out)
```

```python
import functools

import jax
import jax.numpy as jnp
from jax import lax
from jax.experimental import pallas as pl
from jax.experimental.pallas import tpu as pltpu
from jax.sharding import PartitionSpec as P

D = 4096
QUERY_HEADS = 32
KEY_VALUE_HEADS = 4
HEAD_DIMENSION = 128
AXES = ("ctx", "exp")


def exchange(value, stage, n_ctx, n_exp):
    side = 4
    got = []
    for step in range(1, side):
        pairs = []
        for i in range(n_ctx):
            for e in range(n_exp):
                j = i ^ step if (e & 1) == stage else i ^ (side * step)
                pairs.append((i * n_exp + e, j * n_exp + e))
        got.append(lax.ppermute(value, AXES, pairs))
    return got


def rotation(pos, size):
    half = size // 2
    freq = jnp.exp(-jnp.log(1000000.0) * jnp.arange(half).astype(jnp.float32) / half)
    angle = pos.astype(jnp.float32)[:, None] * freq[None, :]
    cosine, sine = jnp.cos(angle), jnp.sin(angle)
    return jnp.concatenate([cosine, cosine], -1), jnp.concatenate([-sine, sine], -1)


def lane_ids():
    return lax.broadcasted_iota(jnp.int32, (QUERY_HEADS, 128), 1)


def spread(log, seqs):
    log = jnp.where(lane_ids() < seqs, log, 0.0)
    high = log.astype(jnp.bfloat16).astype(jnp.float32)
    rest = log - high
    middle = rest.astype(jnp.bfloat16).astype(jnp.float32)
    low = rest - middle
    terms = high + pltpu.roll(middle, seqs, 1) + pltpu.roll(low, 2 * seqs, 1)
    return terms.astype(jnp.bfloat16)


def gather_terms(block, seqs):
    terms = block.astype(jnp.float32)
    return (terms + pltpu.roll(terms, 128 - seqs, 1)) + pltpu.roll(terms, 128 - 2 * seqs, 1)


def halves(value):
    high = value.astype(jnp.bfloat16).astype(jnp.float32)
    lane = lax.broadcasted_iota(jnp.int32, (value.shape[0], 128), 1)
    return jnp.where(lane < 64, high, value - high).astype(jnp.bfloat16)


def project_kernel(tokens_hbm, gain_hbm, w_hbm, out, tokens, gain, w_ref, small, sems):
    f32, bf16 = jnp.float32, jnp.bfloat16
    chunks = sems.shape[0]
    cols = w_hbm.shape[1]
    width = cols // chunks
    copies = [
        pltpu.make_async_copy(
            w_hbm.at[:, pl.ds(c * width, width)], w_ref.at[:, pl.ds(c * width, width)], sems.at[c]
        )
        for c in range(chunks)
    ]
    first = [
        pltpu.make_async_copy(tokens_hbm, tokens, small.at[0]),
        pltpu.make_async_copy(gain_hbm, gain, small.at[1]),
    ]
    for copy in first + copies:
        copy.start()
    for copy in first:
        copy.wait()
    xf = tokens[...].astype(f32)
    scaled = (xf * gain[...]).astype(bf16)
    out[:, cols:] = halves(jnp.sum(xf * xf, 1, keepdims=True))
    for c, copy in enumerate(copies):
        copy.wait()
        at = slice(c * width, (c + 1) * width)
        out[:, at] = jnp.dot(scaled, w_ref[:, at], preferred_element_type=f32).astype(bf16)


def load_kernel(after, k_hbm, v_hbm, w_hbm, k_out, v_out, w_out, sems):
    copies = [
        pltpu.make_async_copy(source, target, sems.at[i])
        for i, (source, target) in enumerate(((k_hbm, k_out), (v_hbm, v_out), (w_hbm, w_out)))
    ]
    for copy in copies:
        copy.start()
    for copy in copies:
        copy.wait()


def add_kernel(m0, m1, m2, m3, after, out):
    f32, bf16 = jnp.float32, jnp.bfloat16
    cols = out.shape[1] - 128

    def total(at):
        p, q, r, s = (m[:, at].astype(f32) for m in (m0, m1, m2, m3))
        return (p + q) + (r + s)

    out[:, :cols] = total(slice(0, cols)).astype(bf16)
    squares = total(slice(cols, cols + 128))
    out[:, cols:] = halves((squares + pltpu.roll(squares, 64, 1))[:, :1])


def attend_kernel(seqs, m0, m1, m2, m3, cosine, sine, live_ref, owns, k_ref, v_ref, out, rows):
    f32, bf16 = jnp.float32, jnp.bfloat16
    qh, kvh, hd = QUERY_HEADS, KEY_VALUE_HEADS, HEAD_DIMENSION
    group = qh // kvh
    positions = k_ref.shape[1]

    def share(h):
        p, q, r, s = (m[:, h * hd : (h + 1) * hd].astype(f32) for m in (m0, m1, m2, m3))
        return (p + q) + (r + s)

    squares = share(qh + 2 * kvh)
    norm = lax.rsqrt((squares + pltpu.roll(squares, 64, 1)) / D + 1e-06)
    cos, sin = cosine[...] * norm, sine[...] * norm
    scale = hd**-0.5
    cos_q, sin_q = cos * scale, sin * scale
    for h in range(qh):
        v = share(h)
        rows[h * seqs : (h + 1) * seqs, :] = v * cos_q + pltpu.roll(v, hd // 2, 1) * sin_q
    for h in range(qh, qh + kvh):
        v = share(h)
        rows[h * seqs : (h + 1) * seqs, :] = v * cos + pltpu.roll(v, hd // 2, 1) * sin
    for h in range(qh + kvh, qh + 2 * kvh):
        rows[h * seqs : (h + 1) * seqs, :] = share(h) * norm

    def grouped(first, b):
        at = [(first + g) * seqs + b for g in range(kvh)]
        return jnp.concatenate(
            [jnp.broadcast_to(rows[i : i + 1, :], (group, hd)) for i in at], 0
        )

    owns_new = jnp.broadcast_to(owns[0:1, :], (qh, 128))[:, :1] > 0.5
    zero = jnp.zeros((group, hd), f32)
    lanes = lane_ids()
    logs = jnp.zeros((qh, 128), f32)
    for b in range(seqs):
        q = rows[pl.ds(b, qh, stride=seqs), :]
        fresh = jnp.where(owns_new, jnp.sum(q * grouped(qh, b), 1, keepdims=True), -1e30)
        wide = jnp.concatenate(
            [
                jnp.concatenate(
                    [q[g * group : (g + 1) * group] if c == g else zero for c in range(kvh)], 1
                )
                for g in range(kvh)
            ],
            0,
        )
        high = wide.astype(bf16)
        low = (wide - high.astype(f32)).astype(bf16)
        both = lax.dot_general(
            jnp.concatenate([high, low], 0),
            k_ref[b],
            (((1,), (1,)), ((), ())),
            preferred_element_type=f32,
        )
        live = jnp.broadcast_to(live_ref[b : b + 1, :], (qh, positions)) > 0.5
        s = jnp.where(live, both[:qh] + both[qh:], -1e30)
        top = jnp.maximum(jnp.max(s, 1, keepdims=True), fresh)
        p = jnp.where(live, jnp.exp(s - top), 0.0)
        p_new = jnp.where(owns_new, jnp.exp(fresh - top), 0.0)
        total = jnp.sum(p, 1, keepdims=True) + p_new
        acc = jnp.dot(p.astype(bf16), v_ref[b], preferred_element_type=f32)
        acc = jnp.concatenate(
            [acc[g * group : (g + 1) * group, g * hd : (g + 1) * hd] for g in range(kvh)], 0
        )
        some = total > 0
        safe = jnp.where(some, total, 1.0)
        out[b * qh : (b + 1) * qh, :] = ((acc + p_new * grouped(qh + kvh, b)) / safe).astype(bf16)
        log = jnp.where(some, top + jnp.log(safe), -1e30)
        logs = jnp.where(lanes == b, log, logs)
    out[seqs * qh : (seqs + 1) * qh, :] = spread(logs, seqs)


def merged(seqs, parts):
    qh = QUERY_HEADS
    logs = [gather_terms(p[seqs * qh : (seqs + 1) * qh, :], seqs) for p in parts]
    top = jnp.maximum(jnp.maximum(logs[0], logs[1]), jnp.maximum(logs[2], logs[3]))
    weights = [jnp.exp(v - top) for v in logs]
    total = (weights[0] + weights[1]) + (weights[2] + weights[3])
    shares = [w / total for w in weights]
    values = []
    for b in range(seqs):
        v = [
            p[b * qh : (b + 1) * qh, :].astype(jnp.float32) * w[:, b : b + 1]
            for p, w in zip(parts, shares)
        ]
        values.append((v[0] + v[1]) + (v[2] + v[3]))
    return values, top + jnp.log(total)


def merge_kernel(seqs, p0, p1, p2, p3, out):
    qh = QUERY_HEADS
    values, log = merged(seqs, (p0, p1, p2, p3))
    for b in range(seqs):
        out[b * qh : (b + 1) * qh, :] = values[b].astype(jnp.bfloat16)
    out[seqs * qh : (seqs + 1) * qh, :] = spread(log, seqs)


def finish_kernel(seqs, p0, p1, p2, p3, tokens, placing, w_ref, context, resid, outgoing, rows):
    f32, bf16 = jnp.float32, jnp.bfloat16
    qh = QUERY_HEADS
    values, _ = merged(seqs, (p0, p1, p2, p3))
    for b in range(seqs):
        rows[pl.ds(b, qh, stride=seqs), :] = values[b]
    whole = jnp.concatenate([rows[h * seqs : (h + 1) * seqs, :] for h in range(qh)], 1).astype(bf16)
    context[...] = whole
    attn = jnp.dot(whole, w_ref[...], preferred_element_type=f32)
    after = (tokens[...].astype(f32) + attn).astype(bf16)
    resid[...] = after
    padded = jnp.concatenate(
        [after.astype(f32), jnp.zeros((placing.shape[1] - seqs, after.shape[1]), f32)], 0
    ).astype(bf16)
    outgoing[...] = jnp.dot(placing[...], padded, preferred_element_type=f32).astype(bf16)


def own_rows(capacity, per_source, n_rows, width, j):
    row = lax.broadcasted_iota(jnp.int32, (n_rows, width), 0)
    return lax.rem(row, per_source) // capacity == j


def gate_up_kernel(capacity, x_ref, gain, w_ref, out):
    f32, bf16 = jnp.float32, jnp.bfloat16
    n_rows, width = x_ref.shape
    experts, _, cols = w_ref.shape
    xf = x_ref[...].astype(f32)
    out[:, cols:] = halves(jnp.sum(xf * xf, 1, keepdims=True))
    gained = xf * gain[...]
    blocks = [
        jnp.where(own_rows(capacity, experts * capacity, n_rows, width, j), gained, 0.0).astype(bf16)
        for j in range(experts)
    ]
    step = 256
    for c in range(0, cols, step):
        total = jnp.dot(blocks[0], w_ref[0, :, c : c + step], preferred_element_type=f32)
        for j in range(1, experts):
            total += jnp.dot(blocks[j], w_ref[j, :, c : c + step], preferred_element_type=f32)
        out[:, c : c + step] = total.astype(bf16)


def activate_kernel(shares, out):
    f32, bf16 = jnp.float32, jnp.bfloat16
    hidden = out.shape[2]

    def total(at):
        terms = [shares[i, :, at].astype(f32) for i in range(shares.shape[0])]
        while len(terms) > 1:
            terms = [p + q for p, q in zip(terms[::2], terms[1::2])]
        return terms[0]

    squares = total(slice(2 * hidden, 2 * hidden + 128))
    norm = lax.rsqrt((squares + pltpu.roll(squares, 64, 1)) / D + 1e-06)[:, :1]
    gate = total(slice(0, hidden)) * norm
    up = total(slice(hidden, 2 * hidden)) * norm
    act = (gate / (1.0 + jnp.exp(-gate)) * up).astype(bf16)
    for i in range(out.shape[0]):
        out[i] = act


def down_kernel(capacity, x_ref, w_ref, out):
    f32 = jnp.float32
    n_rows, width = x_ref.shape
    experts = w_ref.shape[0]
    xf = x_ref[...].astype(f32)
    total = None
    for j in range(experts):
        mine = own_rows(capacity, experts * capacity, n_rows, width, j)
        block = jnp.where(mine, xf, 0.0).astype(jnp.bfloat16)
        part = jnp.dot(block, w_ref[j], preferred_element_type=f32)
        total = part if total is None else total + part
    out[...] = total.astype(jnp.bfloat16)


def combine_kernel(resid, weighting, returned, out):
    f32, bf16 = jnp.float32, jnp.bfloat16
    weights = weighting[...]
    seqs = weights.shape[0]
    high = weights.astype(bf16).astype(f32)
    rest = weights - high
    middle = rest.astype(bf16).astype(f32)
    low = rest - middle
    stack = jnp.concatenate([high, middle, low, jnp.zeros_like(low)], 0).astype(bf16)
    sums = jnp.dot(stack, returned[...], preferred_element_type=f32)
    moe = (sums[:seqs] + sums[seqs : 2 * seqs]) + sums[2 * seqs : 3 * seqs]
    out[...] = (resid[...].astype(f32) + moe).astype(bf16)


VM = pl.BlockSpec(memory_space=pltpu.VMEM)
ANY = pl.BlockSpec(memory_space=pl.ANY)
HBM = pl.BlockSpec(memory_space=pltpu.HBM)


def shape(dims, dtype=jnp.bfloat16):
    return jax.ShapeDtypeStruct(dims, dtype)


def call(kernel, name, out, inputs, specs, scratch=(), mib=8):
    return pl.pallas_call(
        kernel,
        out_shape=out,
        in_specs=specs,
        out_specs=jax.tree.map(lambda _: VM, out),
        scratch_shapes=list(scratch),
        compiler_params=pltpu.CompilerParams(vmem_limit_bytes=mib << 20),
        name=name,
    )(*inputs)


def local(
    tokens,
    attn_gain,
    w_qkv,
    w_out,
    k_cache,
    value_cache,
    lengths,
    moe_gain,
    routes,
    gates,
    w_in,
    w_down,
):
    f32, bf16 = jnp.float32, jnp.bfloat16
    seqs, slice_width = tokens.shape
    hd = HEAD_DIMENSION
    hidden = w_down.shape[1]
    local_exp = w_in.shape[0]
    n_ctx, n_exp = lax.axis_size("ctx"), lax.axis_size("exp")
    experts_all = local_exp * n_exp
    top_k = routes.shape[1]
    capacity = 2 * seqs * top_k // experts_all
    per_source = local_exp * capacity

    cols = w_qkv.shape[1]
    message = call(
        project_kernel,
        "project",
        shape((seqs, cols + 128)),
        (tokens, attn_gain[None], w_qkv),
        [HBM] * 3,
        [
            pltpu.VMEM(tokens.shape, bf16),
            pltpu.VMEM((1, slice_width), f32),
            pltpu.VMEM(w_qkv.shape, bf16),
            pltpu.SemaphoreType.DMA((2,)),
            pltpu.SemaphoreType.DMA((10,)),
        ],
        mib=62,
    )
    got = exchange(message, 0, n_ctx, n_exp)
    keys, values, w_near = call(
        load_kernel,
        "load",
        (shape(k_cache.shape), shape(value_cache.shape), shape(w_out.shape)),
        (message, k_cache, value_cache, w_out),
        [ANY] + [HBM] * 3,
        [pltpu.SemaphoreType.DMA((3,))],
    )
    message = call(
        add_kernel,
        "add",
        shape(message.shape),
        (message, *got, w_near),
        [VM] * 4 + [ANY],
    )
    shares = [message] + exchange(message, 1, n_ctx, n_exp)
    cosine, sine = rotation(lengths, hd)
    positions = k_cache.shape[1]
    first = lax.axis_index("ctx")
    where_pos = first * positions + jnp.arange(positions)
    live = (where_pos[None, :] < lengths[:, None]).astype(f32)
    owns = jnp.broadcast_to((first == 0).astype(f32), (seqs, 128))

    flat_ids = routes.reshape(-1)
    onehot = (flat_ids[:, None] == jnp.arange(experts_all)[None, :]).astype(jnp.int32)
    rank = jnp.sum((jnp.cumsum(onehot, 0) - onehot) * onehot, -1)
    slot_index = flat_ids * capacity + rank
    select = (slot_index[:, None] == jnp.arange(experts_all * capacity)[None, :]).astype(f32)
    token_map = (jnp.arange(seqs * top_k)[:, None] // top_k == jnp.arange(seqs)[None, :]).astype(f32)
    placing = jnp.dot(select.T, token_map, precision=lax.Precision.HIGHEST).astype(bf16)
    placing = jnp.pad(placing, ((0, 0), (0, 128 - seqs)))
    weighting = jnp.dot(
        token_map.T, select * gates.reshape(-1)[:, None], precision=lax.Precision.HIGHEST
    )

    part = call(
        functools.partial(attend_kernel, seqs),
        "attend",
        shape(((seqs + 1) * QUERY_HEADS, hd)),
        (*shares, cosine, sine, live, owns, keys, values),
        [VM] * 10,
        [pltpu.VMEM((cols // hd * seqs, hd), f32)],
    )
    part = call(
        functools.partial(merge_kernel, seqs),
        "merge",
        shape(part.shape),
        [part] + exchange(part, 0, n_ctx, n_exp),
        [VM] * 4,
    )
    context, resid, outgoing = call(
        functools.partial(finish_kernel, seqs),
        "finish",
        (
            shape((seqs, QUERY_HEADS * hd)),
            shape(tokens.shape),
            shape((placing.shape[0], slice_width)),
        ),
        [part] + exchange(part, 1, n_ctx, n_exp) + [tokens, placing, w_near],
        [VM] * 7,
        [pltpu.VMEM((QUERY_HEADS * seqs, hd), f32)],
    )

    n_rows = n_exp * per_source
    rows = lax.all_to_all(
        outgoing.reshape(n_exp, per_source, slice_width), "exp", split_axis=0, concat_axis=0, tiled=True
    )
    message = call(
        functools.partial(gate_up_kernel, capacity),
        "gate_up",
        shape((n_rows, 2 * hidden + 128)),
        (rows.reshape(n_rows, slice_width), moe_gain[None], w_in),
        [VM] * 3,
    )
    sums = lax.all_to_all(
        message.reshape(n_ctx, n_rows // n_ctx, 2 * hidden + 128),
        "ctx",
        split_axis=0,
        concat_axis=0,
        tiled=True,
    )
    act = call(
        activate_kernel, "activate", shape((n_ctx, n_rows // n_ctx, hidden)), (sums,), [VM]
    )
    act = lax.all_to_all(act, "ctx", split_axis=0, concat_axis=0, tiled=True)
    expert_out = call(
        functools.partial(down_kernel, capacity),
        "down",
        shape((n_rows, slice_width)),
        (act.reshape(n_rows, hidden), w_down),
        [VM] * 2,
    )
    returned = lax.all_to_all(
        expert_out.reshape(n_exp, per_source, slice_width), "exp", split_axis=0, concat_axis=0, tiled=True
    )
    layer_out = call(
        combine_kernel,
        "combine",
        shape(tokens.shape),
        (resid, weighting, returned.reshape(n_rows, slice_width)),
        [VM] * 3,
    )
    return (context, layer_out)


def solution(mesh):
    placed = (
        P("exp", "ctx"),
        P("ctx"),
        P("ctx", None),
        P(None, "ctx"),
        P("exp", "ctx", None),
        P("exp", "ctx", None),
        P("exp"),
        P("ctx"),
        P("exp", None),
        P("exp", None),
        P("exp", "ctx", None),
        P("exp", None, "ctx"),
    )
    return jax.shard_map(
        local,
        mesh=mesh,
        in_specs=placed,
        out_specs=(P("exp", None), P("exp", "ctx")),
        check_vma=False,
    )
```

```python
import functools

import jax
import jax.numpy as jnp
from jax import lax
from jax.experimental import pallas as pl
from jax.experimental.pallas import tpu as pltpu
from jax.sharding import PartitionSpec as P

D = 4096
QUERY_HEADS = 32
KEY_VALUE_HEADS = 4
HEAD_DIMENSION = 128
AXES = ("ctx", "exp")


def exchange(value, stage, n_ctx, n_exp):
    side = 4
    got = []
    for step in range(1, side):
        pairs = []
        for i in range(n_ctx):
            for e in range(n_exp):
                j = i ^ step if (e & 1) == stage else i ^ (side * step)
                pairs.append((i * n_exp + e, j * n_exp + e))
        sent = value[step - 1] if isinstance(value, (list, tuple)) else value
        got.append(lax.ppermute(sent, AXES, pairs))
    return got


def rotation(pos, size):
    half = size // 2
    freq = jnp.exp(-jnp.log(1000000.0) * jnp.arange(half).astype(jnp.float32) / half)
    angle = pos.astype(jnp.float32)[:, None] * freq[None, :]
    cosine, sine = jnp.cos(angle), jnp.sin(angle)
    return jnp.concatenate([cosine, cosine], -1), jnp.concatenate([-sine, sine], -1)


def lane_ids():
    return lax.broadcasted_iota(jnp.int32, (QUERY_HEADS, 128), 1)


def spread(log, seqs):
    log = jnp.where(lane_ids() < seqs, log, 0.0)
    high = log.astype(jnp.bfloat16).astype(jnp.float32)
    rest = log - high
    middle = rest.astype(jnp.bfloat16).astype(jnp.float32)
    low = rest - middle
    terms = high + pltpu.roll(middle, seqs, 1) + pltpu.roll(low, 2 * seqs, 1)
    return terms.astype(jnp.bfloat16)


def gather_terms(block, seqs):
    terms = block.astype(jnp.float32)
    return (terms + pltpu.roll(terms, 128 - seqs, 1)) + pltpu.roll(terms, 128 - 2 * seqs, 1)


def halves(value):
    high = value.astype(jnp.bfloat16).astype(jnp.float32)
    lane = lax.broadcasted_iota(jnp.int32, (value.shape[0], 128), 1)
    return jnp.where(lane < 64, high, value - high).astype(jnp.bfloat16)


def project_kernel(tokens_hbm, gain_hbm, w_hbm, out, tokens, gain, w_ref, small, sems):
    f32, bf16 = jnp.float32, jnp.bfloat16
    chunks = sems.shape[0]
    cols = w_hbm.shape[1]
    width = cols // chunks
    copies = [
        pltpu.make_async_copy(
            w_hbm.at[:, pl.ds(c * width, width)], w_ref.at[:, pl.ds(c * width, width)], sems.at[c]
        )
        for c in range(chunks)
    ]
    first = [
        pltpu.make_async_copy(tokens_hbm, tokens, small.at[0]),
        pltpu.make_async_copy(gain_hbm, gain, small.at[1]),
    ]
    for copy in first + copies:
        copy.start()
    for copy in first:
        copy.wait()
    xf = tokens[...].astype(f32)
    scaled = (xf * gain[...]).astype(bf16)
    out[:, cols:] = halves(jnp.sum(xf * xf, 1, keepdims=True))
    for c, copy in enumerate(copies):
        copy.wait()
        at = slice(c * width, (c + 1) * width)
        out[:, at] = jnp.dot(scaled, w_ref[:, at], preferred_element_type=f32).astype(bf16)


def load_kernel(after, *refs):
    count = len(refs) // 2
    sems = refs[-1]
    copies = [
        pltpu.make_async_copy(refs[i], refs[count + i], sems.at[i]) for i in range(count)
    ]
    for copy in copies:
        copy.start()
    for copy in copies:
        copy.wait()


def add_kernel(m0, m1, m2, m3, *rest):
    f32, bf16 = jnp.float32, jnp.bfloat16
    out = rest[-1]
    cols = out.shape[1] - 128

    def total(at):
        p, q, r, s = (m[:, at].astype(f32) for m in (m0, m1, m2, m3))
        return (p + q) + (r + s)

    out[:, :cols] = total(slice(0, cols)).astype(bf16)
    squares = total(slice(cols, cols + 128))
    out[:, cols:] = halves((squares + pltpu.roll(squares, 64, 1))[:, :1])


def attend_kernel(
    seqs, m0, m1, m2, m3, cosine, sine, live_ref, owns, k_ref, v_ref, after, out, rows
):
    f32, bf16 = jnp.float32, jnp.bfloat16
    qh, kvh, hd = QUERY_HEADS, KEY_VALUE_HEADS, HEAD_DIMENSION
    group = qh // kvh
    positions = k_ref.shape[1]

    def share(h):
        p, q, r, s = (m[:, h * hd : (h + 1) * hd].astype(f32) for m in (m0, m1, m2, m3))
        return (p + q) + (r + s)

    squares = share(qh + 2 * kvh)
    norm = lax.rsqrt((squares + pltpu.roll(squares, 64, 1)) / D + 1e-06)
    cos, sin = cosine[...] * norm, sine[...] * norm
    scale = hd**-0.5
    cos_q, sin_q = cos * scale, sin * scale
    for h in range(qh):
        v = share(h)
        rows[h * seqs : (h + 1) * seqs, :] = v * cos_q + pltpu.roll(v, hd // 2, 1) * sin_q
    for h in range(qh, qh + kvh):
        v = share(h)
        rows[h * seqs : (h + 1) * seqs, :] = v * cos + pltpu.roll(v, hd // 2, 1) * sin
    for h in range(qh + kvh, qh + 2 * kvh):
        rows[h * seqs : (h + 1) * seqs, :] = share(h) * norm

    def grouped(first, b):
        at = [(first + g) * seqs + b for g in range(kvh)]
        return jnp.concatenate(
            [jnp.broadcast_to(rows[i : i + 1, :], (group, hd)) for i in at], 0
        )

    owns_new = jnp.broadcast_to(owns[0:1, :], (qh, 128))[:, :1] > 0.5
    zero = jnp.zeros((group, hd), f32)
    lanes = lane_ids()
    logs = jnp.zeros((qh, 128), f32)
    scores, fresh = [], []
    for b in range(seqs):
        q = rows[pl.ds(b, qh, stride=seqs), :]
        fresh.append(jnp.where(owns_new, jnp.sum(q * grouped(qh, b), 1, keepdims=True), -1e30))
        wide = jnp.concatenate(
            [
                jnp.concatenate(
                    [q[g * group : (g + 1) * group] if c == g else zero for c in range(kvh)], 1
                )
                for g in range(kvh)
            ],
            0,
        )
        high = wide.astype(bf16)
        low = (wide - high.astype(f32)).astype(bf16)
        both = lax.dot_general(
            jnp.concatenate([high, low], 0),
            k_ref[b],
            (((1,), (1,)), ((), ())),
            preferred_element_type=f32,
        )
        scores.append(both[:qh] + both[qh:])
    tops, weights, news, totals = [], [], [], []
    for b in range(seqs):
        live = jnp.broadcast_to(live_ref[b : b + 1, :], (qh, positions)) > 0.5
        s = jnp.where(live, scores[b], -1e30)
        top = jnp.maximum(jnp.max(s, 1, keepdims=True), fresh[b])
        p = jnp.where(live, jnp.exp(s - top), 0.0)
        p_new = jnp.where(owns_new, jnp.exp(fresh[b] - top), 0.0)
        tops.append(top)
        weights.append(p.astype(bf16))
        news.append(p_new)
        totals.append(jnp.sum(p, 1, keepdims=True) + p_new)
    for b in range(seqs):
        acc = jnp.dot(weights[b], v_ref[b], preferred_element_type=f32)
        acc = jnp.concatenate(
            [acc[g * group : (g + 1) * group, g * hd : (g + 1) * hd] for g in range(kvh)], 0
        )
        some = totals[b] > 0
        safe = jnp.where(some, totals[b], 1.0)
        value = (acc + news[b] * grouped(qh + kvh, b)) / safe
        out[b * qh : (b + 1) * qh, :] = value.astype(bf16)
        log = jnp.where(some, tops[b] + jnp.log(safe), -1e30)
        logs = jnp.where(lanes == b, log, logs)
    out[seqs * qh : (seqs + 1) * qh, :] = spread(logs, seqs)


def merged(seqs, parts):
    qh = QUERY_HEADS
    logs = [gather_terms(p[seqs * qh : (seqs + 1) * qh, :], seqs) for p in parts]
    top = jnp.maximum(jnp.maximum(logs[0], logs[1]), jnp.maximum(logs[2], logs[3]))
    weights = [jnp.exp(v - top) for v in logs]
    total = (weights[0] + weights[1]) + (weights[2] + weights[3])
    shares = [w / total for w in weights]
    values = []
    for b in range(seqs):
        v = [
            p[b * qh : (b + 1) * qh, :].astype(jnp.float32) * w[:, b : b + 1]
            for p, w in zip(parts, shares)
        ]
        values.append((v[0] + v[1]) + (v[2] + v[3]))
    return values, top + jnp.log(total)


def merge_kernel(seqs, p0, p1, p2, p3, after, out):
    qh = QUERY_HEADS
    values, log = merged(seqs, (p0, p1, p2, p3))
    for b in range(seqs):
        out[b * qh : (b + 1) * qh, :] = values[b].astype(jnp.bfloat16)
    out[seqs * qh : (seqs + 1) * qh, :] = spread(log, seqs)


def finish_kernel(seqs, p0, p1, p2, p3, tokens, placing, w_ref, context, resid, outgoing, rows):
    f32, bf16 = jnp.float32, jnp.bfloat16
    qh = QUERY_HEADS
    values, _ = merged(seqs, (p0, p1, p2, p3))
    for b in range(seqs):
        rows[pl.ds(b, qh, stride=seqs), :] = values[b]
    whole = jnp.concatenate([rows[h * seqs : (h + 1) * seqs, :] for h in range(qh)], 1).astype(bf16)
    context[...] = whole
    attn = jnp.dot(whole, w_ref[...], preferred_element_type=f32)
    after = (tokens[...].astype(f32) + attn).astype(bf16)
    resid[...] = after
    padded = jnp.concatenate(
        [after.astype(f32), jnp.zeros((placing.shape[1] - seqs, after.shape[1]), f32)], 0
    ).astype(bf16)
    outgoing[...] = jnp.dot(placing[...], padded, preferred_element_type=f32).astype(bf16)


def own_rows(capacity, per_source, n_rows, width, j):
    row = lax.broadcasted_iota(jnp.int32, (n_rows, width), 0)
    return lax.rem(row, per_source) // capacity == j


def gate_up_kernel(capacity, place, x_ref, gain, w_ref, *outs):
    f32, bf16 = jnp.float32, jnp.bfloat16
    n_rows, width = x_ref.shape
    experts, _, cols = w_ref.shape
    part = n_rows // len(outs)
    xf = jnp.concatenate(
        [
            x_ref[pl.ds(pl.multiple_of((place[0] ^ s) * part, part), part), :]
            for s in range(len(outs))
        ],
        0,
    ).astype(f32)
    squares = halves(jnp.sum(xf * xf, 1, keepdims=True))
    gained = xf * gain[...]
    blocks = [
        jnp.where(own_rows(capacity, experts * capacity, n_rows, width, j), gained, 0.0).astype(bf16)
        for j in range(experts)
    ]
    for s, out in enumerate(outs):
        out[:, cols:] = squares[s * part : (s + 1) * part]
    step = 256
    for c in range(0, cols, step):
        total = jnp.dot(blocks[0], w_ref[0, :, c : c + step], preferred_element_type=f32)
        for j in range(1, experts):
            total += jnp.dot(blocks[j], w_ref[j, :, c : c + step], preferred_element_type=f32)
        total = total.astype(bf16)
        for s, out in enumerate(outs):
            out[:, c : c + step] = total[s * part : (s + 1) * part]


def activate_kernel(m0, m1, m2, m3, out):
    f32, bf16 = jnp.float32, jnp.bfloat16
    hidden = out.shape[1]

    def total(at):
        p, q, r, s = (m[:, at].astype(f32) for m in (m0, m1, m2, m3))
        return (p + q) + (r + s)

    squares = total(slice(2 * hidden, 2 * hidden + 128))
    norm = lax.rsqrt((squares + pltpu.roll(squares, 64, 1)) / D + 1e-06)[:, :1]
    gate = total(slice(0, hidden)) * norm
    up = total(slice(hidden, 2 * hidden)) * norm
    out[...] = (gate / (1.0 + jnp.exp(-gate)) * up).astype(bf16)


def down_kernel(capacity, place, x0, x1, x2, x3, w_ref, out):
    f32 = jnp.float32
    xf = jnp.concatenate([x[...].astype(f32) for x in (x0, x1, x2, x3)], 0)
    n_rows, width = xf.shape
    part = n_rows // 4
    experts = w_ref.shape[0]
    total = None
    for j in range(experts):
        mine = own_rows(capacity, experts * capacity, n_rows, width, j)
        block = jnp.where(mine, xf, 0.0).astype(jnp.bfloat16)
        share = jnp.dot(block, w_ref[j], preferred_element_type=f32)
        total = share if total is None else total + share
    total = total.astype(jnp.bfloat16)
    for s in range(4):
        at = pl.ds(pl.multiple_of((place[0] ^ s) * part, part), part)
        out[at, :] = total[s * part : (s + 1) * part]


def combine_kernel(resid, weighting, returned, out):
    f32, bf16 = jnp.float32, jnp.bfloat16
    weights = weighting[...]
    seqs = weights.shape[0]
    high = weights.astype(bf16).astype(f32)
    rest = weights - high
    middle = rest.astype(bf16).astype(f32)
    low = rest - middle
    stack = jnp.concatenate([high, middle, low, jnp.zeros_like(low)], 0).astype(bf16)
    sums = jnp.dot(stack, returned[...], preferred_element_type=f32)
    moe = (sums[:seqs] + sums[seqs : 2 * seqs]) + sums[2 * seqs : 3 * seqs]
    out[...] = (resid[...].astype(f32) + moe).astype(bf16)


VM = pl.BlockSpec(memory_space=pltpu.VMEM)
ANY = pl.BlockSpec(memory_space=pl.ANY)
HBM = pl.BlockSpec(memory_space=pltpu.HBM)
SM = pl.BlockSpec(memory_space=pltpu.SMEM)


def shape(dims, dtype=jnp.bfloat16):
    return jax.ShapeDtypeStruct(dims, dtype)


def call(kernel, name, out, inputs, specs, scratch=(), mib=8):
    return pl.pallas_call(
        kernel,
        out_shape=out,
        in_specs=specs,
        out_specs=jax.tree.map(lambda _: VM, out),
        scratch_shapes=list(scratch),
        compiler_params=pltpu.CompilerParams(vmem_limit_bytes=mib << 20),
        name=name,
    )(*inputs)


def load(after, *arrays):
    kept = [pltpu.with_memory_space_constraint(a, pltpu.HBM) for a in arrays]
    return call(
        load_kernel,
        "load",
        tuple(pltpu.VMEM(a.shape, a.dtype) for a in arrays),
        (after, *kept),
        [ANY] + [HBM] * len(arrays),
        [pltpu.SemaphoreType.DMA((len(arrays),))],
    )


def local(
    tokens,
    attn_gain,
    w_qkv,
    w_out,
    k_cache,
    value_cache,
    lengths,
    moe_gain,
    routes,
    gates,
    w_in,
    w_down,
):
    f32, bf16 = jnp.float32, jnp.bfloat16
    seqs, slice_width = tokens.shape
    hd = HEAD_DIMENSION
    hidden = w_down.shape[1]
    local_exp = w_in.shape[0]
    n_ctx, n_exp = lax.axis_size("ctx"), lax.axis_size("exp")
    experts_all = local_exp * n_exp
    top_k = routes.shape[1]
    capacity = 2 * seqs * top_k // experts_all
    per_source = local_exp * capacity

    cols = w_qkv.shape[1]
    message = call(
        project_kernel,
        "project",
        pltpu.VMEM((seqs, cols + 128), bf16),
        [
            pltpu.with_memory_space_constraint(a, pltpu.HBM)
            for a in (tokens, attn_gain[None], w_qkv)
        ],
        [HBM] * 3,
        [
            pltpu.VMEM(tokens.shape, bf16),
            pltpu.VMEM((1, slice_width), f32),
            pltpu.VMEM(w_qkv.shape, bf16),
            pltpu.SemaphoreType.DMA((2,)),
            pltpu.SemaphoreType.DMA((10,)),
        ],
    )
    got = exchange(message, 0, n_ctx, n_exp)
    keys, values = load(message, k_cache, value_cache)
    message = call(
        add_kernel, "add", shape(message.shape), (message, *got, keys), [VM] * 4 + [ANY]
    )
    shares = [message] + exchange(message, 1, n_ctx, n_exp)
    (w_near,) = load(message, w_out)
    cosine, sine = rotation(lengths, hd)
    positions = k_cache.shape[1]
    first = lax.axis_index("ctx")
    where_pos = first * positions + jnp.arange(positions)
    live = (where_pos[None, :] < lengths[:, None]).astype(f32)
    owns = jnp.broadcast_to((first == 0).astype(f32), (seqs, 128))

    flat_ids = routes.reshape(-1)
    onehot = (flat_ids[:, None] == jnp.arange(experts_all)[None, :]).astype(jnp.int32)
    rank = jnp.sum((jnp.cumsum(onehot, 0) - onehot) * onehot, -1)
    slot_index = flat_ids * capacity + rank
    select = (slot_index[:, None] == jnp.arange(experts_all * capacity)[None, :]).astype(f32)
    token_map = (jnp.arange(seqs * top_k)[:, None] // top_k == jnp.arange(seqs)[None, :]).astype(f32)
    placing = jnp.dot(select.T, token_map, precision=lax.Precision.HIGHEST).astype(bf16)
    placing = jnp.pad(placing, ((0, 0), (0, 128 - seqs)))
    weighting = jnp.dot(
        token_map.T, select * gates.reshape(-1)[:, None], precision=lax.Precision.HIGHEST
    )

    part = call(
        functools.partial(attend_kernel, seqs),
        "attend",
        shape(((seqs + 1) * QUERY_HEADS, hd)),
        (*shares, cosine, sine, live, owns, keys, values, w_near),
        [VM] * 10 + [ANY],
        [pltpu.VMEM((cols // hd * seqs, hd), f32)],
    )
    parts = [part] + exchange(part, 0, n_ctx, n_exp)
    (w_in_near,) = load(part, w_in)
    part = call(
        functools.partial(merge_kernel, seqs),
        "merge",
        shape(part.shape),
        parts + [w_in_near],
        [VM] * 4 + [ANY],
    )
    context, resid, outgoing = call(
        functools.partial(finish_kernel, seqs),
        "finish",
        (
            shape((seqs, QUERY_HEADS * hd)),
            shape(tokens.shape),
            shape((placing.shape[0], slice_width)),
        ),
        [part] + exchange(part, 1, n_ctx, n_exp) + [tokens, placing, w_near],
        [VM] * 7,
        [pltpu.VMEM((QUERY_HEADS * seqs, hd), f32)],
    )

    n_rows = n_exp * per_source
    rows = lax.all_to_all(
        outgoing.reshape(n_exp, per_source, slice_width), "exp", split_axis=0, concat_axis=0, tiled=True
    )
    side = 4
    place = jnp.where(lax.axis_index("exp") & 1, first >> 2, first & 3)[None]
    wide = 2 * hidden + 128
    sent = call(
        functools.partial(gate_up_kernel, capacity),
        "gate_up",
        (shape((n_rows // side, wide)),) * side,
        (place, rows.reshape(n_rows, slice_width), moe_gain[None], w_in_near),
        [SM] + [VM] * 3,
    )
    got = [sent[0]] + exchange(sent[1:], 0, n_ctx, n_exp)
    total = call(add_kernel, "add_rows", shape(got[0].shape), got, [VM] * 4)
    act = call(
        activate_kernel,
        "activate",
        shape((n_rows // side, hidden)),
        [total] + exchange(total, 1, n_ctx, n_exp),
        [VM] * 4,
    )
    expert_out = call(
        functools.partial(down_kernel, capacity),
        "down",
        shape((n_rows, slice_width)),
        [place, act] + exchange(act, 0, n_ctx, n_exp) + [w_down],
        [SM] + [VM] * 5,
    )
    returned = lax.all_to_all(
        expert_out.reshape(n_exp, per_source, slice_width), "exp", split_axis=0, concat_axis=0, tiled=True
    )
    layer_out = call(
        combine_kernel,
        "combine",
        shape(tokens.shape),
        (resid, weighting, returned.reshape(n_rows, slice_width)),
        [VM] * 3,
    )
    return (context, layer_out)


def solution(mesh):
    placed = (
        P("exp", "ctx"),
        P("ctx"),
        P("ctx", None),
        P(None, "ctx"),
        P("exp", "ctx", None),
        P("exp", "ctx", None),
        P("exp"),
        P("ctx"),
        P("exp", None),
        P("exp", None),
        P("exp", "ctx", None),
        P("exp", None, "ctx"),
    )
    return jax.shard_map(
        local,
        mesh=mesh,
        in_specs=placed,
        out_specs=(P("exp", None), P("exp", "ctx")),
        check_vma=False,
    )
```

```python
import functools

import jax
import jax.numpy as jnp
from jax import lax
from jax.experimental import pallas as pl
from jax.experimental.pallas import tpu as pltpu
from jax.sharding import PartitionSpec as P

D = 4096
QUERY_HEADS = 32
KEY_VALUE_HEADS = 4
HEAD_DIMENSION = 128
AXES = ("ctx", "exp")


def exchange(value, stage, n_ctx, n_exp):
    side = 4
    got = []
    for step in range(1, side):
        pairs = []
        for i in range(n_ctx):
            for e in range(n_exp):
                j = i ^ step if (e & 1) == stage else i ^ (side * step)
                pairs.append((i * n_exp + e, j * n_exp + e))
        sent = value[step - 1] if isinstance(value, (list, tuple)) else value
        got.append(lax.ppermute(sent, AXES, pairs))
    return got


def rotation(pos, size):
    half = size // 2
    freq = jnp.exp(-jnp.log(1000000.0) * jnp.arange(half).astype(jnp.float32) / half)
    angle = pos.astype(jnp.float32)[:, None] * freq[None, :]
    cosine, sine = jnp.cos(angle), jnp.sin(angle)
    return jnp.concatenate([cosine, cosine], -1), jnp.concatenate([-sine, sine], -1)


def lane_ids():
    return lax.broadcasted_iota(jnp.int32, (QUERY_HEADS, 128), 1)


def spread(log, seqs):
    log = jnp.where(lane_ids() < seqs, log, 0.0)
    high = log.astype(jnp.bfloat16).astype(jnp.float32)
    rest = log - high
    middle = rest.astype(jnp.bfloat16).astype(jnp.float32)
    low = rest - middle
    terms = high + pltpu.roll(middle, seqs, 1) + pltpu.roll(low, 2 * seqs, 1)
    return terms.astype(jnp.bfloat16)


def gather_terms(block, seqs):
    terms = block.astype(jnp.float32)
    return (terms + pltpu.roll(terms, 128 - seqs, 1)) + pltpu.roll(terms, 128 - 2 * seqs, 1)


def halves(value):
    high = value.astype(jnp.bfloat16).astype(jnp.float32)
    lane = lax.broadcasted_iota(jnp.int32, (value.shape[0], 128), 1)
    return jnp.where(lane < 64, high, value - high).astype(jnp.bfloat16)


def prepare_kernel(lengths, routes, gates, after, live, owns, placing, weighting):
    f32 = jnp.float32
    seqs, top_k = routes.shape
    lane = lax.broadcasted_iota(jnp.int32, (seqs, 128), 1)
    row = lax.broadcasted_iota(jnp.int32, (seqs, 128), 0)
    first = lax.axis_index("ctx")
    limits = jnp.zeros((seqs, 128), jnp.int32)
    for b in range(seqs):
        limits = jnp.where(row == b, lengths[b], limits)
    live[...] = jnp.where(lane + first * 128 < limits, 1.0, 0.0)
    owns[...] = jnp.where(lane * 0 + first == 0, 1.0, 0.0)
    named = jnp.zeros((seqs, 128), f32)
    weights = jnp.zeros((seqs, 128), f32)
    for k in range(top_k):
        hit = jnp.broadcast_to(routes[:, k : k + 1], (seqs, 128)) == lane // 2
        named += jnp.where(hit, 1.0, 0.0)
        weights += jnp.where(hit, jnp.broadcast_to(gates[:, k : k + 1], (seqs, 128)), 0.0)
    earlier = jnp.zeros((1, 128), f32)
    ranks = []
    for b in range(seqs):
        ranks.append(earlier)
        earlier = earlier + named[b : b + 1]
    rank = jnp.concatenate(ranks, 0)
    chosen = (named > 0.5) & (jnp.abs(rank - (lane % 2).astype(f32)) < 0.5)
    weighting[...] = jnp.where(chosen, weights, 0.0)
    square = jnp.concatenate(
        [jnp.where(chosen, 1.0, 0.0), jnp.zeros((128 - seqs, 128), f32)], 0
    )
    placing[...] = square.T.astype(jnp.bfloat16)


def line_place():
    first = lax.axis_index("ctx")
    return jnp.where(lax.axis_index("exp") % 2 == 1, first // 4, first % 4)


def project_kernel(tokens_hbm, gain_hbm, w_hbm, out, tokens, gain, w_ref, small, sems):
    f32, bf16 = jnp.float32, jnp.bfloat16
    chunks = sems.shape[0]
    cols = w_hbm.shape[1]
    width = cols // chunks
    copies = [
        pltpu.make_async_copy(
            w_hbm.at[:, pl.ds(c * width, width)], w_ref.at[:, pl.ds(c * width, width)], sems.at[c]
        )
        for c in range(chunks)
    ]
    first = [
        pltpu.make_async_copy(tokens_hbm, tokens, small.at[0]),
        pltpu.make_async_copy(gain_hbm, gain, small.at[1]),
    ]
    for copy in first + copies:
        copy.start()
    for copy in first:
        copy.wait()
    xf = tokens[...].astype(f32)
    scaled = (xf * gain[...]).astype(bf16)
    out[:, cols:] = halves(jnp.sum(xf * xf, 1, keepdims=True))
    for c, copy in enumerate(copies):
        copy.wait()
        at = slice(c * width, (c + 1) * width)
        out[:, at] = jnp.dot(scaled, w_ref[:, at], preferred_element_type=f32).astype(bf16)


def load_kernel(after, *refs):
    count = len(refs) // 2
    sems = refs[-1]
    copies = [
        pltpu.make_async_copy(refs[i], refs[count + i], sems.at[i]) for i in range(count)
    ]
    for copy in copies:
        copy.start()
    for copy in copies:
        copy.wait()


def add_kernel(m0, m1, m2, m3, *rest):
    f32, bf16 = jnp.float32, jnp.bfloat16
    out = rest[-1]
    cols = out.shape[1] - 128

    def total(at):
        p, q, r, s = (m[:, at].astype(f32) for m in (m0, m1, m2, m3))
        return (p + q) + (r + s)

    out[:, :cols] = total(slice(0, cols)).astype(bf16)
    squares = total(slice(cols, cols + 128))
    out[:, cols:] = halves((squares + pltpu.roll(squares, 64, 1))[:, :1])


def attend_kernel(
    seqs, m0, m1, m2, m3, cosine, sine, live_ref, owns, k_ref, v_ref, after, out, rows
):
    f32, bf16 = jnp.float32, jnp.bfloat16
    qh, kvh, hd = QUERY_HEADS, KEY_VALUE_HEADS, HEAD_DIMENSION
    group = qh // kvh
    positions = k_ref.shape[1]

    def share(h):
        p, q, r, s = (m[:, h * hd : (h + 1) * hd].astype(f32) for m in (m0, m1, m2, m3))
        return (p + q) + (r + s)

    squares = share(qh + 2 * kvh)
    norm = lax.rsqrt((squares + pltpu.roll(squares, 64, 1)) / D + 1e-06)
    cos, sin = cosine[...] * norm, sine[...] * norm
    scale = hd**-0.5
    cos_q, sin_q = cos * scale, sin * scale
    for h in range(qh):
        v = share(h)
        rows[h * seqs : (h + 1) * seqs, :] = v * cos_q + pltpu.roll(v, hd // 2, 1) * sin_q
    for h in range(qh, qh + kvh):
        v = share(h)
        rows[h * seqs : (h + 1) * seqs, :] = v * cos + pltpu.roll(v, hd // 2, 1) * sin
    for h in range(qh + kvh, qh + 2 * kvh):
        rows[h * seqs : (h + 1) * seqs, :] = share(h) * norm

    def grouped(first, b):
        at = [(first + g) * seqs + b for g in range(kvh)]
        return jnp.concatenate(
            [jnp.broadcast_to(rows[i : i + 1, :], (group, hd)) for i in at], 0
        )

    owns_new = jnp.broadcast_to(owns[0:1, :], (qh, 128))[:, :1] > 0.5
    zero = jnp.zeros((group, hd), f32)
    lanes = lane_ids()
    logs = jnp.zeros((qh, 128), f32)
    scores, fresh = [], []
    for b in range(seqs):
        q = rows[pl.ds(b, qh, stride=seqs), :]
        fresh.append(jnp.where(owns_new, jnp.sum(q * grouped(qh, b), 1, keepdims=True), -1e30))
        wide = jnp.concatenate(
            [
                jnp.concatenate(
                    [q[g * group : (g + 1) * group] if c == g else zero for c in range(kvh)], 1
                )
                for g in range(kvh)
            ],
            0,
        )
        high = wide.astype(bf16)
        low = (wide - high.astype(f32)).astype(bf16)
        both = lax.dot_general(
            jnp.concatenate([high, low], 0),
            k_ref[b],
            (((1,), (1,)), ((), ())),
            preferred_element_type=f32,
        )
        scores.append(both[:qh] + both[qh:])
    tops, weights, news, totals = [], [], [], []
    for b in range(seqs):
        live = jnp.broadcast_to(live_ref[b : b + 1, :], (qh, positions)) > 0.5
        s = jnp.where(live, scores[b], -1e30)
        top = jnp.maximum(jnp.max(s, 1, keepdims=True), fresh[b])
        p = jnp.where(live, jnp.exp(s - top), 0.0)
        p_new = jnp.where(owns_new, jnp.exp(fresh[b] - top), 0.0)
        tops.append(top)
        weights.append(p.astype(bf16))
        news.append(p_new)
        totals.append(jnp.sum(p, 1, keepdims=True) + p_new)
    for b in range(seqs):
        acc = jnp.dot(weights[b], v_ref[b], preferred_element_type=f32)
        acc = jnp.concatenate(
            [acc[g * group : (g + 1) * group, g * hd : (g + 1) * hd] for g in range(kvh)], 0
        )
        some = totals[b] > 0
        safe = jnp.where(some, totals[b], 1.0)
        value = (acc + news[b] * grouped(qh + kvh, b)) / safe
        out[b * qh : (b + 1) * qh, :] = value.astype(bf16)
        log = jnp.where(some, tops[b] + jnp.log(safe), -1e30)
        logs = jnp.where(lanes == b, log, logs)
    out[seqs * qh : (seqs + 1) * qh, :] = spread(logs, seqs)


def merged(seqs, parts):
    qh = QUERY_HEADS
    logs = [gather_terms(p[seqs * qh : (seqs + 1) * qh, :], seqs) for p in parts]
    top = jnp.maximum(jnp.maximum(logs[0], logs[1]), jnp.maximum(logs[2], logs[3]))
    weights = [jnp.exp(v - top) for v in logs]
    total = (weights[0] + weights[1]) + (weights[2] + weights[3])
    shares = [w / total for w in weights]
    values = []
    for b in range(seqs):
        v = [
            p[b * qh : (b + 1) * qh, :].astype(jnp.float32) * w[:, b : b + 1]
            for p, w in zip(parts, shares)
        ]
        values.append((v[0] + v[1]) + (v[2] + v[3]))
    return values, top + jnp.log(total)


def merge_kernel(seqs, p0, p1, p2, p3, after, out):
    qh = QUERY_HEADS
    values, log = merged(seqs, (p0, p1, p2, p3))
    for b in range(seqs):
        out[b * qh : (b + 1) * qh, :] = values[b].astype(jnp.bfloat16)
    out[seqs * qh : (seqs + 1) * qh, :] = spread(log, seqs)


def finish_kernel(seqs, p0, p1, p2, p3, tokens, placing, w_ref, context, resid, outgoing, rows):
    f32, bf16 = jnp.float32, jnp.bfloat16
    qh = QUERY_HEADS
    values, _ = merged(seqs, (p0, p1, p2, p3))
    for b in range(seqs):
        rows[pl.ds(b, qh, stride=seqs), :] = values[b]
    whole = jnp.concatenate([rows[h * seqs : (h + 1) * seqs, :] for h in range(qh)], 1).astype(bf16)
    context[...] = whole
    attn = jnp.dot(whole, w_ref[...], preferred_element_type=f32)
    after = (tokens[...].astype(f32) + attn).astype(bf16)
    resid[...] = after
    padded = jnp.concatenate(
        [after.astype(f32), jnp.zeros((placing.shape[1] - seqs, after.shape[1]), f32)], 0
    ).astype(bf16)
    outgoing[...] = jnp.dot(placing[...], padded, preferred_element_type=f32).astype(bf16)


def own_rows(capacity, per_source, n_rows, width, j):
    row = lax.broadcasted_iota(jnp.int32, (n_rows, width), 0)
    return lax.rem(row, per_source) // capacity == j


def gate_up_kernel(capacity, x_ref, gain, w_ref, *outs):
    f32, bf16 = jnp.float32, jnp.bfloat16
    n_rows, width = x_ref.shape
    experts, _, cols = w_ref.shape
    part = n_rows // len(outs)
    place = line_place()
    xf = jnp.concatenate(
        [
            x_ref[pl.ds(pl.multiple_of((place ^ s) * part, part), part), :]
            for s in range(len(outs))
        ],
        0,
    ).astype(f32)
    squares = halves(jnp.sum(xf * xf, 1, keepdims=True))
    gained = xf * gain[...]
    blocks = [
        jnp.where(own_rows(capacity, experts * capacity, n_rows, width, j), gained, 0.0).astype(bf16)
        for j in range(experts)
    ]
    for s, out in enumerate(outs):
        out[:, cols:] = squares[s * part : (s + 1) * part]
    step = 256
    for c in range(0, cols, step):
        total = jnp.dot(blocks[0], w_ref[0, :, c : c + step], preferred_element_type=f32)
        for j in range(1, experts):
            total += jnp.dot(blocks[j], w_ref[j, :, c : c + step], preferred_element_type=f32)
        total = total.astype(bf16)
        for s, out in enumerate(outs):
            out[:, c : c + step] = total[s * part : (s + 1) * part]


def activate_kernel(m0, m1, m2, m3, out):
    f32, bf16 = jnp.float32, jnp.bfloat16
    hidden = out.shape[1]

    def total(at):
        p, q, r, s = (m[:, at].astype(f32) for m in (m0, m1, m2, m3))
        return (p + q) + (r + s)

    squares = total(slice(2 * hidden, 2 * hidden + 128))
    norm = lax.rsqrt((squares + pltpu.roll(squares, 64, 1)) / D + 1e-06)[:, :1]
    gate = total(slice(0, hidden)) * norm
    up = total(slice(hidden, 2 * hidden)) * norm
    out[...] = (gate / (1.0 + jnp.exp(-gate)) * up).astype(bf16)


def down_kernel(capacity, x0, x1, x2, x3, w_ref, out):
    f32 = jnp.float32
    xf = jnp.concatenate([x[...].astype(f32) for x in (x0, x1, x2, x3)], 0)
    n_rows, width = xf.shape
    part = n_rows // 4
    experts = w_ref.shape[0]
    total = None
    for j in range(experts):
        mine = own_rows(capacity, experts * capacity, n_rows, width, j)
        block = jnp.where(mine, xf, 0.0).astype(jnp.bfloat16)
        share = jnp.dot(block, w_ref[j], preferred_element_type=f32)
        total = share if total is None else total + share
    total = total.astype(jnp.bfloat16)
    place = line_place()
    for s in range(4):
        at = pl.ds(pl.multiple_of((place ^ s) * part, part), part)
        out[at, :] = total[s * part : (s + 1) * part]


def combine_kernel(resid, weighting, returned, out):
    f32, bf16 = jnp.float32, jnp.bfloat16
    weights = weighting[...]
    seqs = weights.shape[0]
    high = weights.astype(bf16).astype(f32)
    rest = weights - high
    middle = rest.astype(bf16).astype(f32)
    low = rest - middle
    stack = jnp.concatenate([high, middle, low, jnp.zeros_like(low)], 0).astype(bf16)
    sums = jnp.dot(stack, returned[...], preferred_element_type=f32)
    moe = (sums[:seqs] + sums[seqs : 2 * seqs]) + sums[2 * seqs : 3 * seqs]
    out[...] = (resid[...].astype(f32) + moe).astype(bf16)


VM = pl.BlockSpec(memory_space=pltpu.VMEM)
ANY = pl.BlockSpec(memory_space=pl.ANY)
HBM = pl.BlockSpec(memory_space=pltpu.HBM)
SM = pl.BlockSpec(memory_space=pltpu.SMEM)


def shape(dims, dtype=jnp.bfloat16):
    return jax.ShapeDtypeStruct(dims, dtype)


def call(kernel, name, out, inputs, specs, scratch=(), mib=8):
    return pl.pallas_call(
        kernel,
        out_shape=out,
        in_specs=specs,
        out_specs=jax.tree.map(lambda _: VM, out),
        scratch_shapes=list(scratch),
        compiler_params=pltpu.CompilerParams(vmem_limit_bytes=mib << 20),
        name=name,
    )(*inputs)


def near(array):
    return pltpu.with_memory_space_constraint(array, pltpu.VMEM)


def load(after, *arrays):
    kept = [pltpu.with_memory_space_constraint(a, pltpu.HBM) for a in arrays]
    return call(
        load_kernel,
        "load",
        tuple(pltpu.VMEM(a.shape, a.dtype) for a in arrays),
        (near(after), *kept),
        [VM] + [HBM] * len(arrays),
        [pltpu.SemaphoreType.DMA((len(arrays),))],
    )


def local(
    tokens,
    attn_gain,
    w_qkv,
    w_out,
    k_cache,
    value_cache,
    lengths,
    moe_gain,
    routes,
    gates,
    w_in,
    w_down,
):
    f32, bf16 = jnp.float32, jnp.bfloat16
    seqs, slice_width = tokens.shape
    hd = HEAD_DIMENSION
    hidden = w_down.shape[1]
    local_exp = w_in.shape[0]
    n_ctx, n_exp = lax.axis_size("ctx"), lax.axis_size("exp")
    experts_all = local_exp * n_exp
    top_k = routes.shape[1]
    capacity = 2 * seqs * top_k // experts_all
    per_source = local_exp * capacity

    cols = w_qkv.shape[1]
    message = call(
        project_kernel,
        "project",
        pltpu.VMEM((seqs, cols + 128), bf16),
        [
            pltpu.with_memory_space_constraint(a, pltpu.HBM)
            for a in (tokens, attn_gain[None], w_qkv)
        ],
        [HBM] * 3,
        [
            pltpu.VMEM(tokens.shape, bf16),
            pltpu.VMEM((1, slice_width), f32),
            pltpu.VMEM(w_qkv.shape, bf16),
            pltpu.SemaphoreType.DMA((2,)),
            pltpu.SemaphoreType.DMA((2,)),
        ],
    )
    got = exchange(message, 0, n_ctx, n_exp)
    keys, values = load(message, k_cache, value_cache)
    live, owns, placing, weighting = call(
        prepare_kernel,
        "prepare",
        (
            pltpu.VMEM((seqs, 128), f32),
            pltpu.VMEM((seqs, 128), f32),
            pltpu.VMEM((128, 128), bf16),
            pltpu.VMEM((seqs, 128), f32),
        ),
        (lengths, routes, gates, near(message)),
        [SM] + [VM] * 3,
    )
    cosine, sine = rotation(lengths, hd)
    message = call(
        add_kernel,
        "add",
        shape(message.shape),
        (message, *got, near(keys), near(placing), cosine),
        [VM] * 7,
    )
    shares = [message] + exchange(message, 1, n_ctx, n_exp)
    (w_near,) = load(message, w_out)

    part = call(
        functools.partial(attend_kernel, seqs),
        "attend",
        shape(((seqs + 1) * QUERY_HEADS, hd)),
        (*shares, cosine, sine, near(live), near(owns), near(keys), near(values), near(w_near)),
        [VM] * 11,
        [pltpu.VMEM((cols // hd * seqs, hd), f32)],
    )
    parts = [part] + exchange(part, 0, n_ctx, n_exp)
    (w_in_near,) = load(part, w_in)
    part = call(
        functools.partial(merge_kernel, seqs),
        "merge",
        shape(part.shape),
        parts + [near(w_in_near)],
        [VM] * 5,
    )
    context, resid, outgoing = call(
        functools.partial(finish_kernel, seqs),
        "finish",
        (
            pltpu.VMEM((seqs, QUERY_HEADS * hd), bf16),
            shape(tokens.shape),
            shape((placing.shape[0], slice_width)),
        ),
        [part] + exchange(part, 1, n_ctx, n_exp) + [tokens, near(placing), near(w_near)],
        [VM] * 7,
        [pltpu.VMEM((QUERY_HEADS * seqs, hd), f32)],
    )

    n_rows = n_exp * per_source
    rows = lax.all_to_all(
        outgoing.reshape(n_exp, per_source, slice_width), "exp", split_axis=0, concat_axis=0, tiled=True
    )
    side = 4
    wide = 2 * hidden + 128
    sent = call(
        functools.partial(gate_up_kernel, capacity),
        "gate_up",
        (shape((n_rows // side, wide)),) * side,
        (rows.reshape(n_rows, slice_width), moe_gain[None], near(w_in_near)),
        [VM] * 3,
    )
    got = [sent[0]] + exchange(sent[1:], 0, n_ctx, n_exp)
    w_down_near, context = pl.pallas_call(
        load_kernel,
        out_shape=(pltpu.VMEM(w_down.shape, bf16), shape(context.shape)),
        in_specs=[VM, HBM, VM],
        out_specs=(VM, HBM),
        scratch_shapes=[pltpu.SemaphoreType.DMA((2,))],
        compiler_params=pltpu.CompilerParams(vmem_limit_bytes=8 << 20),
        name="settle",
    )(near(sent[0]), pltpu.with_memory_space_constraint(w_down, pltpu.HBM), near(context))
    total = call(
        add_kernel, "add_rows", shape(got[0].shape), got + [near(w_down_near)], [VM] * 5
    )
    act = call(
        activate_kernel,
        "activate",
        shape((n_rows // side, hidden)),
        [total] + exchange(total, 1, n_ctx, n_exp),
        [VM] * 4,
    )
    expert_out = call(
        functools.partial(down_kernel, capacity),
        "down",
        shape((n_rows, slice_width)),
        [act] + exchange(act, 0, n_ctx, n_exp) + [near(w_down_near)],
        [VM] * 5,
    )
    returned = lax.all_to_all(
        expert_out.reshape(n_exp, per_source, slice_width), "exp", split_axis=0, concat_axis=0, tiled=True
    )
    layer_out = call(
        combine_kernel,
        "combine",
        shape(tokens.shape),
        (resid, near(weighting), returned.reshape(n_rows, slice_width)),
        [VM] * 3,
    )
    return (context, layer_out)


def solution(mesh):
    placed = (
        P("exp", "ctx"),
        P("ctx"),
        P("ctx", None),
        P(None, "ctx"),
        P("exp", "ctx", None),
        P("exp", "ctx", None),
        P("exp"),
        P("ctx"),
        P("exp", None),
        P("exp", None),
        P("exp", "ctx", None),
        P("exp", None, "ctx"),
    )
    return jax.shard_map(
        local,
        mesh=mesh,
        in_specs=placed,
        out_specs=(P("exp", None), P("exp", "ctx")),
        check_vma=False,
    )
```

```python
import functools

import jax
import jax.numpy as jnp
from jax import lax
from jax.experimental import pallas as pl
from jax.experimental.pallas import tpu as pltpu
from jax.sharding import PartitionSpec as P

D = 4096
QUERY_HEADS = 32
KEY_VALUE_HEADS = 4
HEAD_DIMENSION = 128
AXES = ("ctx", "exp")


def exchange(value, stage, n_ctx, n_exp):
    side = 4
    got = {}
    for step in (2, 3, 1) if isinstance(value, (list, tuple)) else (1, 3, 2):
        pairs = []
        for i in range(n_ctx):
            for e in range(n_exp):
                j = i ^ step if (e & 1) == stage else i ^ (side * step)
                pairs.append((i * n_exp + e, j * n_exp + e))
        sent = value[step - 1] if isinstance(value, (list, tuple)) else value
        got[step] = lax.ppermute(sent, AXES, pairs)
    return [got[step] for step in range(1, side)]


def rotation(pos, size):
    half = size // 2
    freq = jnp.exp(-jnp.log(1000000.0) * jnp.arange(half).astype(jnp.float32) / half)
    angle = pos.astype(jnp.float32)[:, None] * freq[None, :]
    cosine, sine = jnp.cos(angle), jnp.sin(angle)
    return jnp.concatenate([cosine, cosine], -1), jnp.concatenate([-sine, sine], -1)


def lane_ids():
    return lax.broadcasted_iota(jnp.int32, (QUERY_HEADS, 128), 1)


def spread(log, seqs):
    log = jnp.where(lane_ids() < seqs, log, 0.0)
    high = log.astype(jnp.bfloat16).astype(jnp.float32)
    rest = log - high
    middle = rest.astype(jnp.bfloat16).astype(jnp.float32)
    low = rest - middle
    terms = high + pltpu.roll(middle, seqs, 1) + pltpu.roll(low, 2 * seqs, 1)
    return terms.astype(jnp.bfloat16)


def gather_terms(block, seqs):
    terms = block.astype(jnp.float32)
    return (terms + pltpu.roll(terms, 128 - seqs, 1)) + pltpu.roll(terms, 128 - 2 * seqs, 1)


def halves(value):
    high = value.astype(jnp.bfloat16).astype(jnp.float32)
    lane = lax.broadcasted_iota(jnp.int32, (value.shape[0], 128), 1)
    return jnp.where(lane < 64, high, value - high).astype(jnp.bfloat16)


def prepare_kernel(lengths, routes, gates, after, live, owns, placing, weighting):
    f32 = jnp.float32
    seqs, top_k = routes.shape
    lane = lax.broadcasted_iota(jnp.int32, (seqs, 128), 1)
    row = lax.broadcasted_iota(jnp.int32, (seqs, 128), 0)
    first = lax.axis_index("ctx")
    limits = jnp.zeros((seqs, 128), jnp.int32)
    for b in range(seqs):
        limits = jnp.where(row == b, lengths[b], limits)
    live[...] = jnp.where(lane + first * 128 < limits, 1.0, 0.0)
    owns[...] = jnp.where(lane * 0 + first == 0, 1.0, 0.0)
    named = jnp.zeros((seqs, 128), f32)
    weights = jnp.zeros((seqs, 128), f32)
    for k in range(top_k):
        hit = jnp.broadcast_to(routes[:, k : k + 1], (seqs, 128)) == lane // 2
        named += jnp.where(hit, 1.0, 0.0)
        weights += jnp.where(hit, jnp.broadcast_to(gates[:, k : k + 1], (seqs, 128)), 0.0)
    earlier = jnp.zeros((1, 128), f32)
    ranks = []
    for b in range(seqs):
        ranks.append(earlier)
        earlier = earlier + named[b : b + 1]
    rank = jnp.concatenate(ranks, 0)
    chosen = (named > 0.5) & (jnp.abs(rank - (lane % 2).astype(f32)) < 0.5)
    weighting[...] = jnp.where(chosen, weights, 0.0)
    square = jnp.concatenate(
        [jnp.where(chosen, 1.0, 0.0), jnp.zeros((128 - seqs, 128), f32)], 0
    )
    placing[...] = square.T.astype(jnp.bfloat16)


def line_place():
    first = lax.axis_index("ctx")
    return jnp.where(lax.axis_index("exp") % 2 == 1, first // 4, first % 4)


def project_kernel(tokens_hbm, gain_hbm, w_hbm, out, tokens, gain, w_ref, small, sems):
    f32, bf16 = jnp.float32, jnp.bfloat16
    chunks = sems.shape[0]
    cols = w_hbm.shape[1]
    width = cols // chunks
    copies = [
        pltpu.make_async_copy(
            w_hbm.at[:, pl.ds(c * width, width)], w_ref.at[:, pl.ds(c * width, width)], sems.at[c]
        )
        for c in range(chunks)
    ]
    first = [
        pltpu.make_async_copy(tokens_hbm, tokens, small.at[0]),
        pltpu.make_async_copy(gain_hbm, gain, small.at[1]),
    ]
    for copy in first + copies:
        copy.start()
    for copy in first:
        copy.wait()
    xf = tokens[...].astype(f32)
    scaled = (xf * gain[...]).astype(bf16)
    out[:, cols:] = halves(jnp.sum(xf * xf, 1, keepdims=True))
    for c, copy in enumerate(copies):
        copy.wait()
        at = slice(c * width, (c + 1) * width)
        out[:, at] = jnp.dot(scaled, w_ref[:, at], preferred_element_type=f32).astype(bf16)


def load_kernel(after, *refs):
    count = len(refs) // 2
    sems = refs[-1]
    copies = [
        pltpu.make_async_copy(refs[i], refs[count + i], sems.at[i]) for i in range(count)
    ]
    for copy in copies:
        copy.start()
    for copy in copies:
        copy.wait()


def add_kernel(m0, m1, m2, m3, *rest):
    f32, bf16 = jnp.float32, jnp.bfloat16
    out = rest[-1]
    cols = out.shape[1] - 128

    def total(at):
        p, q, r, s = (m[:, at].astype(f32) for m in (m0, m1, m2, m3))
        return (p + q) + (r + s)

    out[:, :cols] = total(slice(0, cols)).astype(bf16)
    squares = total(slice(cols, cols + 128))
    out[:, cols:] = halves((squares + pltpu.roll(squares, 64, 1))[:, :1])


def attend_kernel(
    seqs, m0, m1, m2, m3, cosine, sine, live_ref, owns, k_ref, v_ref, after, out, rows
):
    f32, bf16 = jnp.float32, jnp.bfloat16
    qh, kvh, hd = QUERY_HEADS, KEY_VALUE_HEADS, HEAD_DIMENSION
    group = qh // kvh
    positions = k_ref.shape[1]

    def share(h):
        p, q, r, s = (m[:, h * hd : (h + 1) * hd].astype(f32) for m in (m0, m1, m2, m3))
        return (p + q) + (r + s)

    squares = share(qh + 2 * kvh)
    norm = lax.rsqrt((squares + pltpu.roll(squares, 64, 1)) / D + 1e-06)
    cos, sin = cosine[...] * norm, sine[...] * norm
    scale = hd**-0.5
    cos_q, sin_q = cos * scale, sin * scale
    for h in range(qh):
        v = share(h)
        rows[h * seqs : (h + 1) * seqs, :] = v * cos_q + pltpu.roll(v, hd // 2, 1) * sin_q
    for h in range(qh, qh + kvh):
        v = share(h)
        rows[h * seqs : (h + 1) * seqs, :] = v * cos + pltpu.roll(v, hd // 2, 1) * sin
    for h in range(qh + kvh, qh + 2 * kvh):
        rows[h * seqs : (h + 1) * seqs, :] = share(h) * norm

    def grouped(first, b):
        at = [(first + g) * seqs + b for g in range(kvh)]
        return jnp.concatenate(
            [jnp.broadcast_to(rows[i : i + 1, :], (group, hd)) for i in at], 0
        )

    owns_new = jnp.broadcast_to(owns[0:1, :], (qh, 128))[:, :1] > 0.5
    zero = jnp.zeros((group, hd), f32)
    lanes = lane_ids()
    logs = jnp.zeros((qh, 128), f32)
    scores, fresh = [], []
    for b in range(seqs):
        q = rows[pl.ds(b, qh, stride=seqs), :]
        fresh.append(jnp.where(owns_new, jnp.sum(q * grouped(qh, b), 1, keepdims=True), -1e30))
        wide = jnp.concatenate(
            [
                jnp.concatenate(
                    [q[g * group : (g + 1) * group] if c == g else zero for c in range(kvh)], 1
                )
                for g in range(kvh)
            ],
            0,
        )
        high = wide.astype(bf16)
        low = (wide - high.astype(f32)).astype(bf16)
        both = lax.dot_general(
            jnp.concatenate([high, low], 0),
            k_ref[b],
            (((1,), (1,)), ((), ())),
            preferred_element_type=f32,
        )
        scores.append(both[:qh] + both[qh:])
    tops, weights, news, totals = [], [], [], []
    for b in range(seqs):
        live = jnp.broadcast_to(live_ref[b : b + 1, :], (qh, positions)) > 0.5
        s = jnp.where(live, scores[b], -1e30)
        top = jnp.maximum(jnp.max(s, 1, keepdims=True), fresh[b])
        p = jnp.where(live, jnp.exp(s - top), 0.0)
        p_new = jnp.where(owns_new, jnp.exp(fresh[b] - top), 0.0)
        tops.append(top)
        weights.append(p.astype(bf16))
        news.append(p_new)
        totals.append(jnp.sum(p, 1, keepdims=True) + p_new)
    for b in range(seqs):
        acc = jnp.dot(weights[b], v_ref[b], preferred_element_type=f32)
        acc = jnp.concatenate(
            [acc[g * group : (g + 1) * group, g * hd : (g + 1) * hd] for g in range(kvh)], 0
        )
        some = totals[b] > 0
        safe = jnp.where(some, totals[b], 1.0)
        value = (acc + news[b] * grouped(qh + kvh, b)) / safe
        out[b * qh : (b + 1) * qh, :] = value.astype(bf16)
        log = jnp.where(some, tops[b] + jnp.log(safe), -1e30)
        logs = jnp.where(lanes == b, log, logs)
    out[seqs * qh : (seqs + 1) * qh, :] = spread(logs, seqs)


def merged(seqs, parts):
    qh = QUERY_HEADS
    logs = [gather_terms(p[seqs * qh : (seqs + 1) * qh, :], seqs) for p in parts]
    top = jnp.maximum(jnp.maximum(logs[0], logs[1]), jnp.maximum(logs[2], logs[3]))
    weights = [jnp.exp(v - top) for v in logs]
    total = (weights[0] + weights[1]) + (weights[2] + weights[3])
    shares = [w / total for w in weights]
    values = []
    for b in range(seqs):
        v = [
            p[b * qh : (b + 1) * qh, :].astype(jnp.float32) * w[:, b : b + 1]
            for p, w in zip(parts, shares)
        ]
        values.append((v[0] + v[1]) + (v[2] + v[3]))
    return values, top + jnp.log(total)


def merge_kernel(seqs, p0, p1, p2, p3, after, out):
    qh = QUERY_HEADS
    values, log = merged(seqs, (p0, p1, p2, p3))
    for b in range(seqs):
        out[b * qh : (b + 1) * qh, :] = values[b].astype(jnp.bfloat16)
    out[seqs * qh : (seqs + 1) * qh, :] = spread(log, seqs)


def finish_kernel(seqs, p0, p1, p2, p3, tokens, placing, w_ref, context, resid, outgoing, rows):
    f32, bf16 = jnp.float32, jnp.bfloat16
    qh = QUERY_HEADS
    values, _ = merged(seqs, (p0, p1, p2, p3))
    for b in range(seqs):
        rows[pl.ds(b, qh, stride=seqs), :] = values[b]
    whole = jnp.concatenate([rows[h * seqs : (h + 1) * seqs, :] for h in range(qh)], 1).astype(bf16)
    context[...] = whole
    attn = jnp.dot(whole, w_ref[...], preferred_element_type=f32)
    after = (tokens[...].astype(f32) + attn).astype(bf16)
    resid[...] = after
    padded = jnp.concatenate(
        [after.astype(f32), jnp.zeros((placing.shape[1] - seqs, after.shape[1]), f32)], 0
    ).astype(bf16)
    outgoing[...] = jnp.dot(placing[...], padded, preferred_element_type=f32).astype(bf16)


def own_rows(capacity, per_source, n_rows, width, j):
    row = lax.broadcasted_iota(jnp.int32, (n_rows, width), 0)
    return lax.rem(row, per_source) // capacity == j


def gate_up_kernel(capacity, x_ref, gain, w_ref, *outs):
    f32, bf16 = jnp.float32, jnp.bfloat16
    n_rows, width = x_ref.shape
    experts, _, cols = w_ref.shape
    part = n_rows // len(outs)
    place = line_place()
    xf = jnp.concatenate(
        [
            x_ref[pl.ds(pl.multiple_of((place ^ s) * part, part), part), :]
            for s in range(len(outs))
        ],
        0,
    ).astype(f32)
    squares = halves(jnp.sum(xf * xf, 1, keepdims=True))
    gained = xf * gain[...]
    blocks = [
        jnp.where(own_rows(capacity, experts * capacity, n_rows, width, j), gained, 0.0).astype(bf16)
        for j in range(experts)
    ]
    for s, out in enumerate(outs):
        out[:, cols:] = squares[s * part : (s + 1) * part]
    step = 256
    for c in range(0, cols, step):
        total = jnp.dot(blocks[0], w_ref[0, :, c : c + step], preferred_element_type=f32)
        for j in range(1, experts):
            total += jnp.dot(blocks[j], w_ref[j, :, c : c + step], preferred_element_type=f32)
        total = total.astype(bf16)
        for s, out in enumerate(outs):
            out[:, c : c + step] = total[s * part : (s + 1) * part]


def activate_kernel(m0, m1, m2, m3, out):
    f32, bf16 = jnp.float32, jnp.bfloat16
    hidden = out.shape[1]

    def total(at):
        p, q, r, s = (m[:, at].astype(f32) for m in (m0, m1, m2, m3))
        return (p + q) + (r + s)

    squares = total(slice(2 * hidden, 2 * hidden + 128))
    norm = lax.rsqrt((squares + pltpu.roll(squares, 64, 1)) / D + 1e-06)[:, :1]
    gate = total(slice(0, hidden)) * norm
    up = total(slice(hidden, 2 * hidden)) * norm
    out[...] = (gate / (1.0 + jnp.exp(-gate)) * up).astype(bf16)


def down_kernel(capacity, x0, x1, x2, x3, w_ref, out):
    f32 = jnp.float32
    xf = jnp.concatenate([x[...].astype(f32) for x in (x0, x1, x2, x3)], 0)
    n_rows, width = xf.shape
    part = n_rows // 4
    experts = w_ref.shape[0]
    total = None
    for j in range(experts):
        mine = own_rows(capacity, experts * capacity, n_rows, width, j)
        block = jnp.where(mine, xf, 0.0).astype(jnp.bfloat16)
        share = jnp.dot(block, w_ref[j], preferred_element_type=f32)
        total = share if total is None else total + share
    total = total.astype(jnp.bfloat16)
    place = line_place()
    for s in range(4):
        at = pl.ds(pl.multiple_of((place ^ s) * part, part), part)
        out[at, :] = total[s * part : (s + 1) * part]


def combine_kernel(resid, weighting, returned, out):
    f32, bf16 = jnp.float32, jnp.bfloat16
    weights = weighting[...]
    seqs = weights.shape[0]
    high = weights.astype(bf16).astype(f32)
    rest = weights - high
    middle = rest.astype(bf16).astype(f32)
    low = rest - middle
    stack = jnp.concatenate([high, middle, low, jnp.zeros_like(low)], 0).astype(bf16)
    sums = jnp.dot(stack, returned[...], preferred_element_type=f32)
    moe = (sums[:seqs] + sums[seqs : 2 * seqs]) + sums[2 * seqs : 3 * seqs]
    out[...] = (resid[...].astype(f32) + moe).astype(bf16)


VM = pl.BlockSpec(memory_space=pltpu.VMEM)
ANY = pl.BlockSpec(memory_space=pl.ANY)
HBM = pl.BlockSpec(memory_space=pltpu.HBM)
SM = pl.BlockSpec(memory_space=pltpu.SMEM)


def shape(dims, dtype=jnp.bfloat16):
    return jax.ShapeDtypeStruct(dims, dtype)


def call(kernel, name, out, inputs, specs, scratch=(), mib=8):
    return pl.pallas_call(
        kernel,
        out_shape=out,
        in_specs=specs,
        out_specs=jax.tree.map(lambda _: VM, out),
        scratch_shapes=list(scratch),
        compiler_params=pltpu.CompilerParams(vmem_limit_bytes=mib << 20),
        name=name,
    )(*inputs)


def near(array):
    return pltpu.with_memory_space_constraint(array, pltpu.VMEM)


def load(after, *arrays):
    kept = [pltpu.with_memory_space_constraint(a, pltpu.HBM) for a in arrays]
    return call(
        load_kernel,
        "load",
        tuple(pltpu.VMEM(a.shape, a.dtype) for a in arrays),
        (near(after), *kept),
        [VM] + [HBM] * len(arrays),
        [pltpu.SemaphoreType.DMA((len(arrays),))],
    )


def local(
    tokens,
    attn_gain,
    w_qkv,
    w_out,
    k_cache,
    value_cache,
    lengths,
    moe_gain,
    routes,
    gates,
    w_in,
    w_down,
):
    f32, bf16 = jnp.float32, jnp.bfloat16
    seqs, slice_width = tokens.shape
    hd = HEAD_DIMENSION
    hidden = w_down.shape[1]
    local_exp = w_in.shape[0]
    n_ctx, n_exp = lax.axis_size("ctx"), lax.axis_size("exp")
    experts_all = local_exp * n_exp
    top_k = routes.shape[1]
    capacity = 2 * seqs * top_k // experts_all
    per_source = local_exp * capacity

    cols = w_qkv.shape[1]
    message = call(
        project_kernel,
        "project",
        pltpu.VMEM((seqs, cols + 128), bf16),
        [
            pltpu.with_memory_space_constraint(a, pltpu.HBM)
            for a in (tokens, attn_gain[None], w_qkv)
        ],
        [HBM] * 3,
        [
            pltpu.VMEM(tokens.shape, bf16),
            pltpu.VMEM((1, slice_width), f32),
            pltpu.VMEM(w_qkv.shape, bf16),
            pltpu.SemaphoreType.DMA((2,)),
            pltpu.SemaphoreType.DMA((2,)),
        ],
    )
    got = exchange(message, 0, n_ctx, n_exp)
    keys, values = load(message, k_cache, value_cache)
    live, owns, placing, weighting = call(
        prepare_kernel,
        "prepare",
        (
            pltpu.VMEM((seqs, 128), f32),
            pltpu.VMEM((seqs, 128), f32),
            pltpu.VMEM((128, 128), bf16),
            pltpu.VMEM((seqs, 128), f32),
        ),
        (lengths, routes, gates, near(message)),
        [SM] + [VM] * 3,
    )
    cosine, sine = rotation(lengths, hd)
    message = call(
        add_kernel,
        "add",
        shape(message.shape),
        (message, *got, near(keys), near(placing), cosine),
        [VM] * 7,
    )
    shares = [message] + exchange(message, 1, n_ctx, n_exp)
    (w_near,) = load(message, w_out)

    part = call(
        functools.partial(attend_kernel, seqs),
        "attend",
        shape(((seqs + 1) * QUERY_HEADS, hd)),
        (*shares, cosine, sine, near(live), near(owns), near(keys), near(values), near(w_near)),
        [VM] * 11,
        [pltpu.VMEM((cols // hd * seqs, hd), f32)],
    )
    parts = [part] + exchange(part, 0, n_ctx, n_exp)
    (w_in_near,) = load(part, w_in)
    part = call(
        functools.partial(merge_kernel, seqs),
        "merge",
        shape(part.shape),
        parts + [near(w_in_near)],
        [VM] * 5,
    )
    context, resid, outgoing = call(
        functools.partial(finish_kernel, seqs),
        "finish",
        (
            pltpu.VMEM((seqs, QUERY_HEADS * hd), bf16),
            shape(tokens.shape),
            shape((placing.shape[0], slice_width)),
        ),
        [part] + exchange(part, 1, n_ctx, n_exp) + [tokens, near(placing), near(w_near)],
        [VM] * 7,
        [pltpu.VMEM((QUERY_HEADS * seqs, hd), f32)],
    )

    n_rows = n_exp * per_source
    rows = lax.all_to_all(
        outgoing.reshape(n_exp, per_source, slice_width), "exp", split_axis=0, concat_axis=0, tiled=True
    )
    side = 4
    wide = 2 * hidden + 128
    sent = call(
        functools.partial(gate_up_kernel, capacity),
        "gate_up",
        (shape((n_rows // side, wide)),) * side,
        (rows.reshape(n_rows, slice_width), moe_gain[None], near(w_in_near)),
        [VM] * 3,
    )
    got = [sent[0]] + exchange(sent[1:], 0, n_ctx, n_exp)
    w_down_near, context = pl.pallas_call(
        load_kernel,
        out_shape=(pltpu.VMEM(w_down.shape, bf16), shape(context.shape)),
        in_specs=[VM, HBM, VM],
        out_specs=(VM, HBM),
        scratch_shapes=[pltpu.SemaphoreType.DMA((2,))],
        compiler_params=pltpu.CompilerParams(vmem_limit_bytes=8 << 20),
        name="settle",
    )(near(sent[0]), pltpu.with_memory_space_constraint(w_down, pltpu.HBM), near(context))
    total = call(
        add_kernel, "add_rows", shape(got[0].shape), got + [near(w_down_near)], [VM] * 5
    )
    act = call(
        activate_kernel,
        "activate",
        shape((n_rows // side, hidden)),
        [total] + exchange(total, 1, n_ctx, n_exp),
        [VM] * 4,
    )
    expert_out = call(
        functools.partial(down_kernel, capacity),
        "down",
        shape((n_rows, slice_width)),
        [act] + exchange(act, 0, n_ctx, n_exp) + [near(w_down_near)],
        [VM] * 5,
    )
    returned = lax.all_to_all(
        expert_out.reshape(n_exp, per_source, slice_width), "exp", split_axis=0, concat_axis=0, tiled=True
    )
    layer_out = call(
        combine_kernel,
        "combine",
        shape(tokens.shape),
        (resid, near(weighting), returned.reshape(n_rows, slice_width)),
        [VM] * 3,
    )
    return (context, layer_out)


def solution(mesh):
    placed = (
        P("exp", "ctx"),
        P("ctx"),
        P("ctx", None),
        P(None, "ctx"),
        P("exp", "ctx", None),
        P("exp", "ctx", None),
        P("exp"),
        P("ctx"),
        P("exp", None),
        P("exp", None),
        P("exp", "ctx", None),
        P("exp", None, "ctx"),
    )
    return jax.shard_map(
        local,
        mesh=mesh,
        in_specs=placed,
        out_specs=(P("exp", None), P("exp", "ctx")),
        check_vma=False,
    )
```

```python
import functools

import jax
import jax.numpy as jnp
from jax import lax
from jax.experimental import pallas as pl
from jax.experimental.pallas import tpu as pltpu
from jax.sharding import PartitionSpec as P

D = 4096
QUERY_HEADS = 32
KEY_VALUE_HEADS = 4
HEAD_DIMENSION = 128
AXES = ("ctx", "exp")


def exchange(value, stage, n_ctx, n_exp):
    side = 4
    got = {}
    for step in (2, 3, 1) if isinstance(value, (list, tuple)) else (1, 3, 2):
        pairs = []
        for i in range(n_ctx):
            for e in range(n_exp):
                j = i ^ step if (e & 1) == stage else i ^ (side * step)
                pairs.append((i * n_exp + e, j * n_exp + e))
        sent = value[step - 1] if isinstance(value, (list, tuple)) else value
        got[step] = lax.ppermute(sent, AXES, pairs)
    return [got[step] for step in (1, 3, 2)]


def rotation(pos, size):
    half = size // 2
    freq = jnp.exp(-jnp.log(1000000.0) * jnp.arange(half).astype(jnp.float32) / half)
    angle = pos.astype(jnp.float32)[:, None] * freq[None, :]
    cosine, sine = jnp.cos(angle), jnp.sin(angle)
    return jnp.concatenate([cosine, cosine], -1), jnp.concatenate([-sine, sine], -1)


def lane_ids():
    return lax.broadcasted_iota(jnp.int32, (QUERY_HEADS, 128), 1)


def spread(log, seqs):
    log = jnp.where(lane_ids() < seqs, log, 0.0)
    high = log.astype(jnp.bfloat16).astype(jnp.float32)
    rest = log - high
    middle = rest.astype(jnp.bfloat16).astype(jnp.float32)
    low = rest - middle
    terms = high + pltpu.roll(middle, seqs, 1) + pltpu.roll(low, 2 * seqs, 1)
    return terms.astype(jnp.bfloat16)


def gather_terms(block, seqs):
    terms = block.astype(jnp.float32)
    return (terms + pltpu.roll(terms, 128 - seqs, 1)) + pltpu.roll(terms, 128 - 2 * seqs, 1)


def halves(value):
    high = value.astype(jnp.bfloat16).astype(jnp.float32)
    lane = lax.broadcasted_iota(jnp.int32, (value.shape[0], 128), 1)
    return jnp.where(lane < 64, high, value - high).astype(jnp.bfloat16)


def prepare_kernel(lengths, routes, gates, after, live, owns, placing, weighting):
    f32 = jnp.float32
    seqs, top_k = routes.shape
    lane = lax.broadcasted_iota(jnp.int32, (seqs, 128), 1)
    row = lax.broadcasted_iota(jnp.int32, (seqs, 128), 0)
    first = lax.axis_index("ctx")
    limits = jnp.zeros((seqs, 128), jnp.int32)
    for b in range(seqs):
        limits = jnp.where(row == b, lengths[b], limits)
    live[...] = jnp.where(lane + first * 128 < limits, 1.0, 0.0)
    owns[...] = jnp.where(lane * 0 + first == 0, 1.0, 0.0)
    named = jnp.zeros((seqs, 128), f32)
    weights = jnp.zeros((seqs, 128), f32)
    for k in range(top_k):
        hit = jnp.broadcast_to(routes[:, k : k + 1], (seqs, 128)) == lane // 2
        named += jnp.where(hit, 1.0, 0.0)
        weights += jnp.where(hit, jnp.broadcast_to(gates[:, k : k + 1], (seqs, 128)), 0.0)
    earlier = jnp.zeros((1, 128), f32)
    ranks = []
    for b in range(seqs):
        ranks.append(earlier)
        earlier = earlier + named[b : b + 1]
    rank = jnp.concatenate(ranks, 0)
    chosen = (named > 0.5) & (jnp.abs(rank - (lane % 2).astype(f32)) < 0.5)
    weighting[...] = jnp.where(chosen, weights, 0.0)
    square = jnp.concatenate(
        [jnp.where(chosen, 1.0, 0.0), jnp.zeros((128 - seqs, 128), f32)], 0
    )
    placing[...] = square.T.astype(jnp.bfloat16)


def line_place():
    first = lax.axis_index("ctx")
    return jnp.where(lax.axis_index("exp") % 2 == 1, first // 4, first % 4)


def project_kernel(tokens_hbm, gain_hbm, w_hbm, out, tokens, gain, w_ref, small, sems):
    f32, bf16 = jnp.float32, jnp.bfloat16
    chunks = sems.shape[0]
    cols = w_hbm.shape[1]
    width = cols // chunks
    copies = [
        pltpu.make_async_copy(
            w_hbm.at[:, pl.ds(c * width, width)], w_ref.at[:, pl.ds(c * width, width)], sems.at[c]
        )
        for c in range(chunks)
    ]
    first = [
        pltpu.make_async_copy(tokens_hbm, tokens, small.at[0]),
        pltpu.make_async_copy(gain_hbm, gain, small.at[1]),
    ]
    for copy in first + copies:
        copy.start()
    for copy in first:
        copy.wait()
    xf = tokens[...].astype(f32)
    scaled = (xf * gain[...]).astype(bf16)
    out[:, cols:] = halves(jnp.sum(xf * xf, 1, keepdims=True))
    for c, copy in enumerate(copies):
        copy.wait()
        at = slice(c * width, (c + 1) * width)
        out[:, at] = jnp.dot(scaled, w_ref[:, at], preferred_element_type=f32).astype(bf16)


def load_kernel(after, *refs):
    count = len(refs) // 2
    sems = refs[-1]
    copies = [
        pltpu.make_async_copy(refs[i], refs[count + i], sems.at[i]) for i in range(count)
    ]
    for copy in copies:
        copy.start()
    for copy in copies:
        copy.wait()


def add_kernel(m0, m1, m3, m2, *rest):
    f32, bf16 = jnp.float32, jnp.bfloat16
    out = rest[-1]
    cols = out.shape[1] - 128

    def total(at):
        p, q, r, s = (m[:, at].astype(f32) for m in (m0, m1, m2, m3))
        return (p + q) + (r + s)

    out[:, :cols] = total(slice(0, cols)).astype(bf16)
    squares = total(slice(cols, cols + 128))
    out[:, cols:] = halves((squares + pltpu.roll(squares, 64, 1))[:, :1])


def attend_kernel(
    seqs, m0, m1, m3, m2, cosine, sine, live_ref, owns, k_ref, v_ref, after, out, rows
):
    f32, bf16 = jnp.float32, jnp.bfloat16
    qh, kvh, hd = QUERY_HEADS, KEY_VALUE_HEADS, HEAD_DIMENSION
    group = qh // kvh
    positions = k_ref.shape[1]

    def share(h):
        p, q, r, s = (m[:, h * hd : (h + 1) * hd].astype(f32) for m in (m0, m1, m2, m3))
        return (p + q) + (r + s)

    squares = share(qh + 2 * kvh)
    norm = lax.rsqrt((squares + pltpu.roll(squares, 64, 1)) / D + 1e-06)
    cos, sin = cosine[...] * norm, sine[...] * norm
    scale = hd**-0.5
    cos_q, sin_q = cos * scale, sin * scale
    for h in range(qh):
        v = share(h)
        rows[h * seqs : (h + 1) * seqs, :] = v * cos_q + pltpu.roll(v, hd // 2, 1) * sin_q
    for h in range(qh, qh + kvh):
        v = share(h)
        rows[h * seqs : (h + 1) * seqs, :] = v * cos + pltpu.roll(v, hd // 2, 1) * sin
    for h in range(qh + kvh, qh + 2 * kvh):
        rows[h * seqs : (h + 1) * seqs, :] = share(h) * norm

    def grouped(first, b):
        at = [(first + g) * seqs + b for g in range(kvh)]
        return jnp.concatenate(
            [jnp.broadcast_to(rows[i : i + 1, :], (group, hd)) for i in at], 0
        )

    owns_new = jnp.broadcast_to(owns[0:1, :], (qh, 128))[:, :1] > 0.5
    zero = jnp.zeros((group, hd), f32)
    lanes = lane_ids()
    logs = jnp.zeros((qh, 128), f32)
    scores, fresh = [], []
    for b in range(seqs):
        q = rows[pl.ds(b, qh, stride=seqs), :]
        fresh.append(jnp.where(owns_new, jnp.sum(q * grouped(qh, b), 1, keepdims=True), -1e30))
        wide = jnp.concatenate(
            [
                jnp.concatenate(
                    [q[g * group : (g + 1) * group] if c == g else zero for c in range(kvh)], 1
                )
                for g in range(kvh)
            ],
            0,
        )
        high = wide.astype(bf16)
        low = (wide - high.astype(f32)).astype(bf16)
        both = lax.dot_general(
            jnp.concatenate([high, low], 0),
            k_ref[b],
            (((1,), (1,)), ((), ())),
            preferred_element_type=f32,
        )
        scores.append(both[:qh] + both[qh:])
    tops, weights, news, totals = [], [], [], []
    for b in range(seqs):
        live = jnp.broadcast_to(live_ref[b : b + 1, :], (qh, positions)) > 0.5
        s = jnp.where(live, scores[b], -1e30)
        top = jnp.maximum(jnp.max(s, 1, keepdims=True), fresh[b])
        p = jnp.where(live, jnp.exp(s - top), 0.0)
        p_new = jnp.where(owns_new, jnp.exp(fresh[b] - top), 0.0)
        tops.append(top)
        weights.append(p.astype(bf16))
        news.append(p_new)
        totals.append(jnp.sum(p, 1, keepdims=True) + p_new)
    for b in range(seqs):
        acc = jnp.dot(weights[b], v_ref[b], preferred_element_type=f32)
        acc = jnp.concatenate(
            [acc[g * group : (g + 1) * group, g * hd : (g + 1) * hd] for g in range(kvh)], 0
        )
        some = totals[b] > 0
        safe = jnp.where(some, totals[b], 1.0)
        value = (acc + news[b] * grouped(qh + kvh, b)) / safe
        out[b * qh : (b + 1) * qh, :] = value.astype(bf16)
        log = jnp.where(some, tops[b] + jnp.log(safe), -1e30)
        logs = jnp.where(lanes == b, log, logs)
    out[seqs * qh : (seqs + 1) * qh, :] = spread(logs, seqs)


def merged(seqs, parts):
    qh = QUERY_HEADS
    logs = [gather_terms(p[seqs * qh : (seqs + 1) * qh, :], seqs) for p in parts]
    top = jnp.maximum(jnp.maximum(logs[0], logs[1]), jnp.maximum(logs[2], logs[3]))
    weights = [jnp.exp(v - top) for v in logs]
    total = (weights[0] + weights[1]) + (weights[2] + weights[3])
    shares = [w / total for w in weights]
    values = []
    for b in range(seqs):
        v = [
            p[b * qh : (b + 1) * qh, :].astype(jnp.float32) * w[:, b : b + 1]
            for p, w in zip(parts, shares)
        ]
        values.append((v[0] + v[1]) + (v[2] + v[3]))
    return values, top + jnp.log(total)


def merge_kernel(seqs, p0, p1, p3, p2, after, out):
    qh = QUERY_HEADS
    values, log = merged(seqs, (p0, p1, p2, p3))
    for b in range(seqs):
        out[b * qh : (b + 1) * qh, :] = values[b].astype(jnp.bfloat16)
    out[seqs * qh : (seqs + 1) * qh, :] = spread(log, seqs)


def finish_kernel(seqs, p0, p1, p3, p2, tokens, placing, w_ref, context, resid, outgoing, rows):
    f32, bf16 = jnp.float32, jnp.bfloat16
    qh = QUERY_HEADS
    values, _ = merged(seqs, (p0, p1, p2, p3))
    for b in range(seqs):
        rows[pl.ds(b, qh, stride=seqs), :] = values[b]
    whole = jnp.concatenate([rows[h * seqs : (h + 1) * seqs, :] for h in range(qh)], 1).astype(bf16)
    context[...] = whole
    attn = jnp.dot(whole, w_ref[...], preferred_element_type=f32)
    after = (tokens[...].astype(f32) + attn).astype(bf16)
    resid[...] = after
    padded = jnp.concatenate(
        [after.astype(f32), jnp.zeros((placing.shape[1] - seqs, after.shape[1]), f32)], 0
    ).astype(bf16)
    outgoing[...] = jnp.dot(placing[...], padded, preferred_element_type=f32).astype(bf16)


def own_rows(capacity, per_source, n_rows, width, j):
    row = lax.broadcasted_iota(jnp.int32, (n_rows, width), 0)
    return lax.rem(row, per_source) // capacity == j


def gate_up_kernel(capacity, x_ref, gain, w_ref, *outs):
    f32, bf16 = jnp.float32, jnp.bfloat16
    n_rows, width = x_ref.shape
    experts, _, cols = w_ref.shape
    part = n_rows // len(outs)
    place = line_place()
    xf = jnp.concatenate(
        [
            x_ref[pl.ds(pl.multiple_of((place ^ s) * part, part), part), :]
            for s in range(len(outs))
        ],
        0,
    ).astype(f32)
    squares = halves(jnp.sum(xf * xf, 1, keepdims=True))
    gained = xf * gain[...]
    blocks = [
        jnp.where(own_rows(capacity, experts * capacity, n_rows, width, j), gained, 0.0).astype(bf16)
        for j in range(experts)
    ]
    for s, out in enumerate(outs):
        out[:, cols:] = squares[s * part : (s + 1) * part]
    step = 256
    for c in range(0, cols, step):
        total = jnp.dot(blocks[0], w_ref[0, :, c : c + step], preferred_element_type=f32)
        for j in range(1, experts):
            total += jnp.dot(blocks[j], w_ref[j, :, c : c + step], preferred_element_type=f32)
        total = total.astype(bf16)
        for s, out in enumerate(outs):
            out[:, c : c + step] = total[s * part : (s + 1) * part]


def activate_kernel(m0, m1, m3, m2, out):
    f32, bf16 = jnp.float32, jnp.bfloat16
    hidden = out.shape[1]

    def total(at):
        p, q, r, s = (m[:, at].astype(f32) for m in (m0, m1, m2, m3))
        return (p + q) + (r + s)

    squares = total(slice(2 * hidden, 2 * hidden + 128))
    norm = lax.rsqrt((squares + pltpu.roll(squares, 64, 1)) / D + 1e-06)[:, :1]
    gate = total(slice(0, hidden)) * norm
    up = total(slice(hidden, 2 * hidden)) * norm
    out[...] = (gate / (1.0 + jnp.exp(-gate)) * up).astype(bf16)


def down_kernel(capacity, x0, x1, x3, x2, w_ref, out):
    f32 = jnp.float32
    xf = jnp.concatenate([x[...].astype(f32) for x in (x0, x1, x2, x3)], 0)
    n_rows, width = xf.shape
    part = n_rows // 4
    experts = w_ref.shape[0]
    total = None
    for j in range(experts):
        mine = own_rows(capacity, experts * capacity, n_rows, width, j)
        block = jnp.where(mine, xf, 0.0).astype(jnp.bfloat16)
        share = jnp.dot(block, w_ref[j], preferred_element_type=f32)
        total = share if total is None else total + share
    total = total.astype(jnp.bfloat16)
    place = line_place()
    for s in range(4):
        at = pl.ds(pl.multiple_of((place ^ s) * part, part), part)
        out[at, :] = total[s * part : (s + 1) * part]


def combine_kernel(resid, weighting, returned, out):
    f32, bf16 = jnp.float32, jnp.bfloat16
    weights = weighting[...]
    seqs = weights.shape[0]
    high = weights.astype(bf16).astype(f32)
    rest = weights - high
    middle = rest.astype(bf16).astype(f32)
    low = rest - middle
    stack = jnp.concatenate([high, middle, low, jnp.zeros_like(low)], 0).astype(bf16)
    sums = jnp.dot(stack, returned[...], preferred_element_type=f32)
    moe = (sums[:seqs] + sums[seqs : 2 * seqs]) + sums[2 * seqs : 3 * seqs]
    out[...] = (resid[...].astype(f32) + moe).astype(bf16)


VM = pl.BlockSpec(memory_space=pltpu.VMEM)
ANY = pl.BlockSpec(memory_space=pl.ANY)
HBM = pl.BlockSpec(memory_space=pltpu.HBM)
SM = pl.BlockSpec(memory_space=pltpu.SMEM)


def shape(dims, dtype=jnp.bfloat16):
    return jax.ShapeDtypeStruct(dims, dtype)


def call(kernel, name, out, inputs, specs, scratch=(), mib=8):
    return pl.pallas_call(
        kernel,
        out_shape=out,
        in_specs=specs,
        out_specs=jax.tree.map(lambda _: VM, out),
        scratch_shapes=list(scratch),
        compiler_params=pltpu.CompilerParams(vmem_limit_bytes=mib << 20),
        name=name,
    )(*inputs)


def near(array):
    return pltpu.with_memory_space_constraint(array, pltpu.VMEM)


def load(after, *arrays):
    kept = [pltpu.with_memory_space_constraint(a, pltpu.HBM) for a in arrays]
    return call(
        load_kernel,
        "load",
        tuple(pltpu.VMEM(a.shape, a.dtype) for a in arrays),
        (near(after), *kept),
        [VM] + [HBM] * len(arrays),
        [pltpu.SemaphoreType.DMA((len(arrays),))],
    )


def local(
    tokens,
    attn_gain,
    w_qkv,
    w_out,
    k_cache,
    value_cache,
    lengths,
    moe_gain,
    routes,
    gates,
    w_in,
    w_down,
):
    f32, bf16 = jnp.float32, jnp.bfloat16
    seqs, slice_width = tokens.shape
    hd = HEAD_DIMENSION
    hidden = w_down.shape[1]
    local_exp = w_in.shape[0]
    n_ctx, n_exp = lax.axis_size("ctx"), lax.axis_size("exp")
    experts_all = local_exp * n_exp
    top_k = routes.shape[1]
    capacity = 2 * seqs * top_k // experts_all
    per_source = local_exp * capacity

    cols = w_qkv.shape[1]
    message = call(
        project_kernel,
        "project",
        pltpu.VMEM((seqs, cols + 128), bf16),
        [
            pltpu.with_memory_space_constraint(a, pltpu.HBM)
            for a in (tokens, attn_gain[None], w_qkv)
        ],
        [HBM] * 3,
        [
            pltpu.VMEM(tokens.shape, bf16),
            pltpu.VMEM((1, slice_width), f32),
            pltpu.VMEM(w_qkv.shape, bf16),
            pltpu.SemaphoreType.DMA((2,)),
            pltpu.SemaphoreType.DMA((2,)),
        ],
    )
    got = exchange(message, 0, n_ctx, n_exp)
    keys, values = load(message, k_cache, value_cache)
    live, owns, placing, weighting = call(
        prepare_kernel,
        "prepare",
        (
            pltpu.VMEM((seqs, 128), f32),
            pltpu.VMEM((seqs, 128), f32),
            pltpu.VMEM((128, 128), bf16),
            pltpu.VMEM((seqs, 128), f32),
        ),
        (lengths, routes, gates, near(message)),
        [SM] + [VM] * 3,
    )
    cosine, sine = rotation(lengths, hd)
    message = call(
        add_kernel,
        "add",
        shape(message.shape),
        (message, *got, near(keys), near(placing), cosine),
        [VM] * 7,
    )
    shares = [message] + exchange(message, 1, n_ctx, n_exp)
    (w_near,) = load(message, w_out)

    part = call(
        functools.partial(attend_kernel, seqs),
        "attend",
        shape(((seqs + 1) * QUERY_HEADS, hd)),
        (*shares, cosine, sine, near(live), near(owns), near(keys), near(values), near(w_near)),
        [VM] * 11,
        [pltpu.VMEM((cols // hd * seqs, hd), f32)],
    )
    parts = [part] + exchange(part, 0, n_ctx, n_exp)
    (w_in_near,) = load(part, w_in)
    part = call(
        functools.partial(merge_kernel, seqs),
        "merge",
        shape(part.shape),
        parts + [near(w_in_near)],
        [VM] * 5,
    )
    context, resid, outgoing = call(
        functools.partial(finish_kernel, seqs),
        "finish",
        (
            pltpu.VMEM((seqs, QUERY_HEADS * hd), bf16),
            shape(tokens.shape),
            shape((placing.shape[0], slice_width)),
        ),
        [part] + exchange(part, 1, n_ctx, n_exp) + [tokens, near(placing), near(w_near)],
        [VM] * 7,
        [pltpu.VMEM((QUERY_HEADS * seqs, hd), f32)],
    )

    n_rows = n_exp * per_source
    rows = lax.all_to_all(
        outgoing.reshape(n_exp, per_source, slice_width), "exp", split_axis=0, concat_axis=0, tiled=True
    )
    side = 4
    wide = 2 * hidden + 128
    sent = call(
        functools.partial(gate_up_kernel, capacity),
        "gate_up",
        (shape((n_rows // side, wide)),) * side,
        (rows.reshape(n_rows, slice_width), moe_gain[None], near(w_in_near)),
        [VM] * 3,
    )
    got = [sent[0]] + exchange(sent[1:], 0, n_ctx, n_exp)[::-1]
    w_down_near, context = pl.pallas_call(
        load_kernel,
        out_shape=(pltpu.VMEM(w_down.shape, bf16), shape(context.shape)),
        in_specs=[VM, HBM, VM],
        out_specs=(VM, HBM),
        scratch_shapes=[pltpu.SemaphoreType.DMA((2,))],
        compiler_params=pltpu.CompilerParams(vmem_limit_bytes=8 << 20),
        name="settle",
    )(near(sent[0]), pltpu.with_memory_space_constraint(w_down, pltpu.HBM), near(context))
    total = call(
        add_kernel, "add_rows", shape(got[0].shape), got + [near(w_down_near)], [VM] * 5
    )
    act = call(
        activate_kernel,
        "activate",
        shape((n_rows // side, hidden)),
        [total] + exchange(total, 1, n_ctx, n_exp),
        [VM] * 4,
    )
    expert_out = call(
        functools.partial(down_kernel, capacity),
        "down",
        shape((n_rows, slice_width)),
        [act] + exchange(act, 0, n_ctx, n_exp) + [near(w_down_near)],
        [VM] * 5,
    )
    returned = lax.all_to_all(
        expert_out.reshape(n_exp, per_source, slice_width), "exp", split_axis=0, concat_axis=0, tiled=True
    )
    layer_out = call(
        combine_kernel,
        "combine",
        shape(tokens.shape),
        (resid, near(weighting), returned.reshape(n_rows, slice_width)),
        [VM] * 3,
    )
    return (context, layer_out)


def solution(mesh):
    placed = (
        P("exp", "ctx"),
        P("ctx"),
        P("ctx", None),
        P(None, "ctx"),
        P("exp", "ctx", None),
        P("exp", "ctx", None),
        P("exp"),
        P("ctx"),
        P("exp", None),
        P("exp", None),
        P("exp", "ctx", None),
        P("exp", None, "ctx"),
    )
    return jax.shard_map(
        local,
        mesh=mesh,
        in_specs=placed,
        out_specs=(P("exp", None), P("exp", "ctx")),
        check_vma=False,
    )
```

```python
import functools

import jax
import jax.numpy as jnp
from jax import lax
from jax.experimental import pallas as pl
from jax.experimental.pallas import tpu as pltpu
from jax.sharding import PartitionSpec as P

D = 4096
QUERY_HEADS = 32
KEY_VALUE_HEADS = 4
HEAD_DIMENSION = 128
AXES = ("ctx", "exp")
SQUARES = 1024.0
SHARES = 16.0


def exchange(value, stage, n_ctx, n_exp):
    side = 4
    got = {}
    for step in (2, 3, 1) if isinstance(value, (list, tuple)) else (1, 3, 2):
        pairs = []
        for i in range(n_ctx):
            for e in range(n_exp):
                j = i ^ step if (e & 1) == stage else i ^ (side * step)
                pairs.append((i * n_exp + e, j * n_exp + e))
        sent = value[step - 1] if isinstance(value, (list, tuple)) else value
        got[step] = lax.ppermute(sent, AXES, pairs)
    return [got[step] for step in (1, 3, 2)]


def rotation(pos, size):
    half = size // 2
    freq = jnp.exp(-jnp.log(1000000.0) * jnp.arange(half).astype(jnp.float32) / half)
    angle = pos.astype(jnp.float32)[:, None] * freq[None, :]
    cosine, sine = jnp.cos(angle), jnp.sin(angle)
    return jnp.concatenate([cosine, cosine], -1), jnp.concatenate([-sine, sine], -1)


def lane_ids():
    return lax.broadcasted_iota(jnp.int32, (QUERY_HEADS, 128), 1)


def spread(log, seqs):
    log = jnp.where(lane_ids() < seqs, log, 0.0)
    high = log.astype(jnp.bfloat16).astype(jnp.float32)
    rest = log - high
    middle = rest.astype(jnp.bfloat16).astype(jnp.float32)
    low = rest - middle
    terms = high + pltpu.roll(middle, seqs, 1) + pltpu.roll(low, 2 * seqs, 1)
    return terms.astype(jnp.bfloat16)


def gather_terms(block, seqs):
    terms = block.astype(jnp.float32)
    return (terms + pltpu.roll(terms, 128 - seqs, 1)) + pltpu.roll(terms, 128 - 2 * seqs, 1)


def halves(value):
    high = value.astype(jnp.bfloat16).astype(jnp.float32)
    lane = lax.broadcasted_iota(jnp.int32, (value.shape[0], 128), 1)
    return jnp.where(lane < 64, high, value - high).astype(jnp.bfloat16)


def added(arrays):
    own, one, three, two = (a.astype(jnp.float32) for a in arrays)
    return (own + one) + (two + three)


def prepare_kernel(lengths, routes, gates, after, live, owns, placing, weighting):
    f32 = jnp.float32
    seqs, top_k = routes.shape
    lane = lax.broadcasted_iota(jnp.int32, (seqs, 128), 1)
    row = lax.broadcasted_iota(jnp.int32, (seqs, 128), 0)
    first = lax.axis_index("ctx")
    limits = jnp.zeros((seqs, 128), jnp.int32)
    for b in range(seqs):
        limits = jnp.where(row == b, lengths[b], limits)
    live[...] = jnp.where(lane + first * 128 < limits, 1.0, 0.0)
    owns[...] = jnp.where(lane * 0 + first == 0, 1.0, 0.0)
    named = jnp.zeros((seqs, 128), f32)
    weights = jnp.zeros((seqs, 128), f32)
    for k in range(top_k):
        hit = jnp.broadcast_to(routes[:, k : k + 1], (seqs, 128)) == lane // 2
        named += jnp.where(hit, 1.0, 0.0)
        weights += jnp.where(hit, jnp.broadcast_to(gates[:, k : k + 1], (seqs, 128)), 0.0)
    earlier = jnp.zeros((1, 128), f32)
    ranks = []
    for b in range(seqs):
        ranks.append(earlier)
        earlier = earlier + named[b : b + 1]
    rank = jnp.concatenate(ranks, 0)
    chosen = (named > 0.5) & (jnp.abs(rank - (lane % 2).astype(f32)) < 0.5)
    weighting[...] = jnp.where(chosen, weights, 0.0)
    square = jnp.concatenate(
        [jnp.where(chosen, 1.0, 0.0), jnp.zeros((128 - seqs, 128), f32)], 0
    )
    placing[...] = square.T.astype(jnp.bfloat16)


def line_place():
    first = lax.axis_index("ctx")
    return jnp.where(lax.axis_index("exp") % 2 == 1, first // 4, first % 4)


def project_kernel(tokens_hbm, gain_hbm, w_hbm, out, tokens, gain, w_ref, small, sems):
    f32, bf16 = jnp.float32, jnp.bfloat16
    chunks = sems.shape[0]
    cols = w_hbm.shape[1]
    width = cols // chunks
    copies = [
        pltpu.make_async_copy(
            w_hbm.at[:, pl.ds(c * width, width)], w_ref.at[:, pl.ds(c * width, width)], sems.at[c]
        )
        for c in range(chunks)
    ]
    first = [
        pltpu.make_async_copy(tokens_hbm, tokens, small.at[0]),
        pltpu.make_async_copy(gain_hbm, gain, small.at[1]),
    ]
    for copy in first + copies:
        copy.start()
    for copy in first:
        copy.wait()
    xf = tokens[...].astype(f32)
    scaled = (xf * gain[...]).astype(bf16)
    squares = jnp.sum(xf * xf, 1, keepdims=True) * (SQUARES / D)
    out[:, cols:] = halves(squares).astype(f32)
    for c, copy in enumerate(copies):
        copy.wait()
        at = slice(c * width, (c + 1) * width)
        out[:, at] = jnp.dot(scaled, w_ref[:, at], preferred_element_type=f32) * SHARES


def load_kernel(after, *refs):
    count = len(refs) // 2
    sems = refs[-1]
    copies = [
        pltpu.make_async_copy(refs[i], refs[count + i], sems.at[i]) for i in range(count)
    ]
    for copy in copies:
        copy.start()
    for copy in copies:
        copy.wait()


def add_kernel(m0, m1, m3, m2, *rest):
    f32, bf16 = jnp.float32, jnp.bfloat16
    out = rest[-1]
    cols = out.shape[1] - 128

    def total(at):
        p, q, r, s = (m[:, at].astype(f32) for m in (m0, m1, m2, m3))
        return (p + q) + (r + s)

    out[:, :cols] = total(slice(0, cols)).astype(bf16)
    squares = total(slice(cols, cols + 128))
    out[:, cols:] = halves((squares + pltpu.roll(squares, 64, 1))[:, :1])


def attend_kernel(
    seqs, shares, cosine, sine, live_ref, owns, k_ref, v_ref, after, out, rows
):
    f32, bf16 = jnp.float32, jnp.bfloat16
    qh, kvh, hd = QUERY_HEADS, KEY_VALUE_HEADS, HEAD_DIMENSION
    group = qh // kvh
    positions = k_ref.shape[1]

    def share(h):
        return shares[:, h * hd : (h + 1) * hd]

    squares = share(qh + 2 * kvh)
    norm = lax.rsqrt((squares + pltpu.roll(squares, 64, 1)) / SQUARES + 1e-06) / SHARES
    cos, sin = cosine[...] * norm, sine[...] * norm
    scale = hd**-0.5
    cos_q, sin_q = cos * scale, sin * scale
    for h in range(qh):
        v = share(h)
        rows[h * seqs : (h + 1) * seqs, :] = v * cos_q + pltpu.roll(v, hd // 2, 1) * sin_q
    for h in range(qh, qh + kvh):
        v = share(h)
        rows[h * seqs : (h + 1) * seqs, :] = v * cos + pltpu.roll(v, hd // 2, 1) * sin
    for h in range(qh + kvh, qh + 2 * kvh):
        rows[h * seqs : (h + 1) * seqs, :] = share(h) * norm

    def grouped(first, b):
        at = [(first + g) * seqs + b for g in range(kvh)]
        return jnp.concatenate(
            [jnp.broadcast_to(rows[i : i + 1, :], (group, hd)) for i in at], 0
        )

    owns_new = jnp.broadcast_to(owns[0:1, :], (qh, 128))[:, :1] > 0.5
    zero = jnp.zeros((group, hd), f32)
    lanes = lane_ids()
    logs = jnp.zeros((qh, 128), f32)
    scores, fresh = [], []
    for b in range(seqs):
        q = rows[pl.ds(b, qh, stride=seqs), :]
        fresh.append(jnp.where(owns_new, jnp.sum(q * grouped(qh, b), 1, keepdims=True), -1e30))
        wide = jnp.concatenate(
            [
                jnp.concatenate(
                    [q[g * group : (g + 1) * group] if c == g else zero for c in range(kvh)], 1
                )
                for g in range(kvh)
            ],
            0,
        )
        high = wide.astype(bf16)
        low = (wide - high.astype(f32)).astype(bf16)
        both = lax.dot_general(
            jnp.concatenate([high, low], 0),
            k_ref[b],
            (((1,), (1,)), ((), ())),
            preferred_element_type=f32,
        )
        scores.append(both[:qh] + both[qh:])
    tops, weights, news, totals = [], [], [], []
    for b in range(seqs):
        live = jnp.broadcast_to(live_ref[b : b + 1, :], (qh, positions)) > 0.5
        s = jnp.where(live, scores[b], -1e30)
        top = jnp.maximum(jnp.max(s, 1, keepdims=True), fresh[b])
        p = jnp.where(live, jnp.exp(s - top), 0.0)
        p_new = jnp.where(owns_new, jnp.exp(fresh[b] - top), 0.0)
        tops.append(top)
        weights.append(p.astype(bf16))
        news.append(p_new)
        totals.append(jnp.sum(p, 1, keepdims=True) + p_new)
    for b in range(seqs):
        acc = jnp.dot(weights[b], v_ref[b], preferred_element_type=f32)
        acc = jnp.concatenate(
            [acc[g * group : (g + 1) * group, g * hd : (g + 1) * hd] for g in range(kvh)], 0
        )
        some = totals[b] > 0
        safe = jnp.where(some, totals[b], 1.0)
        value = (acc + news[b] * grouped(qh + kvh, b)) / safe
        out[b * qh : (b + 1) * qh, :] = value.astype(bf16)
        log = jnp.where(some, tops[b] + jnp.log(safe), -1e30)
        logs = jnp.where(lanes == b, log, logs)
    out[seqs * qh : (seqs + 1) * qh, :] = spread(logs, seqs)


def merged(seqs, parts):
    qh = QUERY_HEADS
    logs = [gather_terms(p[seqs * qh : (seqs + 1) * qh, :], seqs) for p in parts]
    top = jnp.maximum(jnp.maximum(logs[0], logs[1]), jnp.maximum(logs[2], logs[3]))
    weights = [jnp.exp(v - top) for v in logs]
    total = (weights[0] + weights[1]) + (weights[2] + weights[3])
    shares = [w / total for w in weights]
    values = []
    for b in range(seqs):
        v = [
            p[b * qh : (b + 1) * qh, :].astype(jnp.float32) * w[:, b : b + 1]
            for p, w in zip(parts, shares)
        ]
        values.append((v[0] + v[1]) + (v[2] + v[3]))
    return values, top + jnp.log(total)


def merge_kernel(seqs, p0, p1, p3, p2, after, out):
    qh = QUERY_HEADS
    values, log = merged(seqs, (p0, p1, p2, p3))
    for b in range(seqs):
        out[b * qh : (b + 1) * qh, :] = values[b].astype(jnp.bfloat16)
    out[seqs * qh : (seqs + 1) * qh, :] = spread(log, seqs)


def finish_kernel(seqs, p0, p1, p3, p2, tokens, placing, w_ref, context, resid, outgoing, rows):
    f32, bf16 = jnp.float32, jnp.bfloat16
    qh = QUERY_HEADS
    values, _ = merged(seqs, (p0, p1, p2, p3))
    for b in range(seqs):
        rows[pl.ds(b, qh, stride=seqs), :] = values[b]
    whole = jnp.concatenate([rows[h * seqs : (h + 1) * seqs, :] for h in range(qh)], 1).astype(bf16)
    context[...] = whole
    attn = jnp.dot(whole, w_ref[...], preferred_element_type=f32)
    after = (tokens[...].astype(f32) + attn).astype(bf16)
    resid[...] = after
    padded = jnp.concatenate(
        [after.astype(f32), jnp.zeros((placing.shape[1] - seqs, after.shape[1]), f32)], 0
    ).astype(bf16)
    outgoing[...] = jnp.dot(placing[...], padded, preferred_element_type=f32).astype(bf16)


def own_rows(capacity, per_source, n_rows, width, j):
    row = lax.broadcasted_iota(jnp.int32, (n_rows, width), 0)
    return lax.rem(row, per_source) // capacity == j


def gate_up_kernel(capacity, x_ref, gain, w_ref, *outs):
    f32, bf16 = jnp.float32, jnp.bfloat16
    n_rows, width = x_ref.shape
    experts, _, cols = w_ref.shape
    part = n_rows // len(outs)
    place = line_place()
    xf = jnp.concatenate(
        [
            x_ref[pl.ds(pl.multiple_of((place ^ s) * part, part), part), :]
            for s in range(len(outs))
        ],
        0,
    ).astype(f32)
    squares = halves(jnp.sum(xf * xf, 1, keepdims=True))
    gained = xf * gain[...]
    blocks = [
        jnp.where(own_rows(capacity, experts * capacity, n_rows, width, j), gained, 0.0).astype(bf16)
        for j in range(experts)
    ]
    for s, out in enumerate(outs):
        out[:, cols:] = squares[s * part : (s + 1) * part]
    step = 256
    for c in range(0, cols, step):
        total = jnp.dot(blocks[0], w_ref[0, :, c : c + step], preferred_element_type=f32)
        for j in range(1, experts):
            total += jnp.dot(blocks[j], w_ref[j, :, c : c + step], preferred_element_type=f32)
        total = total.astype(bf16)
        for s, out in enumerate(outs):
            out[:, c : c + step] = total[s * part : (s + 1) * part]


def activate_kernel(m0, m1, m3, m2, out):
    f32, bf16 = jnp.float32, jnp.bfloat16
    hidden = out.shape[1]

    def total(at):
        p, q, r, s = (m[:, at].astype(f32) for m in (m0, m1, m2, m3))
        return (p + q) + (r + s)

    squares = total(slice(2 * hidden, 2 * hidden + 128))
    norm = lax.rsqrt((squares + pltpu.roll(squares, 64, 1)) / D + 1e-06)[:, :1]
    gate = total(slice(0, hidden)) * norm
    up = total(slice(hidden, 2 * hidden)) * norm
    out[...] = (gate / (1.0 + jnp.exp(-gate)) * up).astype(bf16)


def down_kernel(capacity, x0, x1, x3, x2, w_ref, out):
    f32 = jnp.float32
    xf = jnp.concatenate([x[...].astype(f32) for x in (x0, x1, x2, x3)], 0)
    n_rows, width = xf.shape
    part = n_rows // 4
    experts = w_ref.shape[0]
    total = None
    for j in range(experts):
        mine = own_rows(capacity, experts * capacity, n_rows, width, j)
        block = jnp.where(mine, xf, 0.0).astype(jnp.bfloat16)
        share = jnp.dot(block, w_ref[j], preferred_element_type=f32)
        total = share if total is None else total + share
    total = total.astype(jnp.bfloat16)
    place = line_place()
    for s in range(4):
        at = pl.ds(pl.multiple_of((place ^ s) * part, part), part)
        out[at, :] = total[s * part : (s + 1) * part]


def combine_kernel(resid, weighting, returned, out):
    f32, bf16 = jnp.float32, jnp.bfloat16
    weights = weighting[...]
    seqs = weights.shape[0]
    high = weights.astype(bf16).astype(f32)
    rest = weights - high
    middle = rest.astype(bf16).astype(f32)
    low = rest - middle
    stack = jnp.concatenate([high, middle, low, jnp.zeros_like(low)], 0).astype(bf16)
    sums = jnp.dot(stack, returned[...], preferred_element_type=f32)
    moe = (sums[:seqs] + sums[seqs : 2 * seqs]) + sums[2 * seqs : 3 * seqs]
    out[...] = (resid[...].astype(f32) + moe).astype(bf16)


VM = pl.BlockSpec(memory_space=pltpu.VMEM)
ANY = pl.BlockSpec(memory_space=pl.ANY)
HBM = pl.BlockSpec(memory_space=pltpu.HBM)
SM = pl.BlockSpec(memory_space=pltpu.SMEM)


def shape(dims, dtype=jnp.bfloat16):
    return jax.ShapeDtypeStruct(dims, dtype)


def call(kernel, name, out, inputs, specs, scratch=(), mib=8):
    return pl.pallas_call(
        kernel,
        out_shape=out,
        in_specs=specs,
        out_specs=jax.tree.map(lambda _: VM, out),
        scratch_shapes=list(scratch),
        compiler_params=pltpu.CompilerParams(vmem_limit_bytes=mib << 20),
        name=name,
    )(*inputs)


def near(array):
    return pltpu.with_memory_space_constraint(array, pltpu.VMEM)


def load(after, *arrays):
    kept = [pltpu.with_memory_space_constraint(a, pltpu.HBM) for a in arrays]
    return call(
        load_kernel,
        "load",
        tuple(pltpu.VMEM(a.shape, a.dtype) for a in arrays),
        (near(after), *kept),
        [VM] + [HBM] * len(arrays),
        [pltpu.SemaphoreType.DMA((len(arrays),))],
    )


def local(
    tokens,
    attn_gain,
    w_qkv,
    w_out,
    k_cache,
    value_cache,
    lengths,
    moe_gain,
    routes,
    gates,
    w_in,
    w_down,
):
    f32, bf16 = jnp.float32, jnp.bfloat16
    seqs, slice_width = tokens.shape
    hd = HEAD_DIMENSION
    hidden = w_down.shape[1]
    local_exp = w_in.shape[0]
    n_ctx, n_exp = lax.axis_size("ctx"), lax.axis_size("exp")
    experts_all = local_exp * n_exp
    top_k = routes.shape[1]
    capacity = 2 * seqs * top_k // experts_all
    per_source = local_exp * capacity

    cols = w_qkv.shape[1]
    message = call(
        project_kernel,
        "project",
        pltpu.VMEM((seqs, cols + 128), f32),
        [
            pltpu.with_memory_space_constraint(a, pltpu.HBM)
            for a in (tokens, attn_gain[None], w_qkv)
        ],
        [HBM] * 3,
        [
            pltpu.VMEM(tokens.shape, bf16),
            pltpu.VMEM((1, slice_width), f32),
            pltpu.VMEM(w_qkv.shape, bf16),
            pltpu.SemaphoreType.DMA((2,)),
            pltpu.SemaphoreType.DMA((2,)),
        ],
    )
    whole, message = message, lax.optimization_barrier(message.astype(jnp.float16))
    got = exchange(message, 0, n_ctx, n_exp)
    keys, values = load(whole, k_cache, value_cache)
    live, owns, placing, weighting = call(
        prepare_kernel,
        "prepare",
        (
            pltpu.VMEM((seqs, 128), f32),
            pltpu.VMEM((seqs, 128), f32),
            pltpu.VMEM((128, 128), bf16),
            pltpu.VMEM((seqs, 128), f32),
        ),
        (lengths, routes, gates, near(whole)),
        [SM] + [VM] * 3,
    )
    cosine, sine = rotation(lengths, hd)
    total = added([message] + got)
    message = lax.optimization_barrier(total.astype(jnp.float16))
    shares = added([message] + exchange(message, 1, n_ctx, n_exp))
    (w_near,) = load(total, w_out)

    part = call(
        functools.partial(attend_kernel, seqs),
        "attend",
        shape(((seqs + 1) * QUERY_HEADS, hd)),
        (shares, cosine, sine, near(live), near(owns), near(keys), near(values), near(w_near)),
        [VM] * 8,
        [pltpu.VMEM((cols // hd * seqs, hd), f32)],
    )
    parts = [part] + exchange(part, 0, n_ctx, n_exp)
    (w_in_near,) = load(part, w_in)
    part = call(
        functools.partial(merge_kernel, seqs),
        "merge",
        shape(part.shape),
        parts + [near(w_in_near)],
        [VM] * 5,
    )
    context, resid, outgoing = call(
        functools.partial(finish_kernel, seqs),
        "finish",
        (
            pltpu.VMEM((seqs, QUERY_HEADS * hd), bf16),
            shape(tokens.shape),
            shape((placing.shape[0], slice_width)),
        ),
        [part] + exchange(part, 1, n_ctx, n_exp) + [tokens, near(placing), near(w_near)],
        [VM] * 7,
        [pltpu.VMEM((QUERY_HEADS * seqs, hd), f32)],
    )

    n_rows = n_exp * per_source
    rows = lax.all_to_all(
        outgoing.reshape(n_exp, per_source, slice_width), "exp", split_axis=0, concat_axis=0, tiled=True
    )
    side = 4
    wide = 2 * hidden + 128
    sent = call(
        functools.partial(gate_up_kernel, capacity),
        "gate_up",
        (shape((n_rows // side, wide)),) * side,
        (rows.reshape(n_rows, slice_width), moe_gain[None], near(w_in_near)),
        [VM] * 3,
    )
    got = [sent[0]] + exchange(sent[1:], 0, n_ctx, n_exp)[::-1]
    w_down_near, context = pl.pallas_call(
        load_kernel,
        out_shape=(pltpu.VMEM(w_down.shape, bf16), shape(context.shape)),
        in_specs=[VM, HBM, VM],
        out_specs=(VM, HBM),
        scratch_shapes=[pltpu.SemaphoreType.DMA((2,))],
        compiler_params=pltpu.CompilerParams(vmem_limit_bytes=8 << 20),
        name="settle",
    )(near(sent[0]), pltpu.with_memory_space_constraint(w_down, pltpu.HBM), near(context))
    total = call(
        add_kernel, "add_rows", shape(got[0].shape), got + [near(w_down_near)], [VM] * 5
    )
    act = call(
        activate_kernel,
        "activate",
        shape((n_rows // side, hidden)),
        [total] + exchange(total, 1, n_ctx, n_exp),
        [VM] * 4,
    )
    expert_out = call(
        functools.partial(down_kernel, capacity),
        "down",
        shape((n_rows, slice_width)),
        [act] + exchange(act, 0, n_ctx, n_exp) + [near(w_down_near)],
        [VM] * 5,
    )
    returned = lax.all_to_all(
        expert_out.reshape(n_exp, per_source, slice_width), "exp", split_axis=0, concat_axis=0, tiled=True
    )
    layer_out = call(
        combine_kernel,
        "combine",
        shape(tokens.shape),
        (resid, near(weighting), returned.reshape(n_rows, slice_width)),
        [VM] * 3,
    )
    return (context, layer_out)


def solution(mesh):
    placed = (
        P("exp", "ctx"),
        P("ctx"),
        P("ctx", None),
        P(None, "ctx"),
        P("exp", "ctx", None),
        P("exp", "ctx", None),
        P("exp"),
        P("ctx"),
        P("exp", None),
        P("exp", None),
        P("exp", "ctx", None),
        P("exp", None, "ctx"),
    )
    return jax.shard_map(
        local,
        mesh=mesh,
        in_specs=placed,
        out_specs=(P("exp", None), P("exp", "ctx")),
        check_vma=False,
    )
```

```python
import functools

import jax
import jax.numpy as jnp
from jax import lax
from jax.experimental import pallas as pl
from jax.experimental.pallas import tpu as pltpu
from jax.sharding import PartitionSpec as P

D = 4096
QUERY_HEADS = 32
KEY_VALUE_HEADS = 4
HEAD_DIMENSION = 128
AXES = ("ctx", "exp")
SQUARES = 1024.0
SHARES = 16.0


def exchange(value, stage, n_ctx, n_exp):
    side = 4
    got = {}
    for step in (2, 3, 1) if isinstance(value, (list, tuple)) else (1, 3, 2):
        pairs = []
        for i in range(n_ctx):
            for e in range(n_exp):
                j = i ^ step if (e & 1) == stage else i ^ (side * step)
                pairs.append((i * n_exp + e, j * n_exp + e))
        sent = value[step - 1] if isinstance(value, (list, tuple)) else value
        got[step] = lax.ppermute(sent, AXES, pairs)
    return [got[step] for step in (1, 3, 2)]


def rotation(pos, size):
    half = size // 2
    freq = jnp.exp(-jnp.log(1000000.0) * jnp.arange(half).astype(jnp.float32) / half)
    angle = pos.astype(jnp.float32)[:, None] * freq[None, :]
    cosine, sine = jnp.cos(angle), jnp.sin(angle)
    return jnp.concatenate([cosine, cosine], -1), jnp.concatenate([-sine, sine], -1)


def lane_ids():
    return lax.broadcasted_iota(jnp.int32, (QUERY_HEADS, 128), 1)


def spread(log, seqs):
    log = jnp.where(lane_ids() < seqs, log, 0.0)
    high = log.astype(jnp.bfloat16).astype(jnp.float32)
    rest = log - high
    middle = rest.astype(jnp.bfloat16).astype(jnp.float32)
    low = rest - middle
    terms = high + pltpu.roll(middle, seqs, 1) + pltpu.roll(low, 2 * seqs, 1)
    return terms.astype(jnp.bfloat16)


def gather_terms(block, seqs):
    terms = block.astype(jnp.float32)
    return (terms + pltpu.roll(terms, 128 - seqs, 1)) + pltpu.roll(terms, 128 - 2 * seqs, 1)


def halves(value):
    high = value.astype(jnp.bfloat16).astype(jnp.float32)
    lane = lax.broadcasted_iota(jnp.int32, (value.shape[0], 128), 1)
    return jnp.where(lane < 64, high, value - high).astype(jnp.bfloat16)


def added(arrays):
    own, one, three, two = (a.astype(jnp.float32) for a in arrays)
    return (own + one) + (three + two)


def prepare_kernel(lengths, routes, gates, after, live, owns, placing, weighting):
    f32 = jnp.float32
    seqs, top_k = routes.shape
    lane = lax.broadcasted_iota(jnp.int32, (seqs, 128), 1)
    row = lax.broadcasted_iota(jnp.int32, (seqs, 128), 0)
    first = lax.axis_index("ctx")
    limits = jnp.zeros((seqs, 128), jnp.int32)
    for b in range(seqs):
        limits = jnp.where(row == b, lengths[b], limits)
    live[...] = jnp.where(lane + first * 128 < limits, 1.0, 0.0)
    owns[...] = jnp.where(lane * 0 + first == 0, 1.0, 0.0)
    named = jnp.zeros((seqs, 128), f32)
    weights = jnp.zeros((seqs, 128), f32)
    for k in range(top_k):
        hit = jnp.broadcast_to(routes[:, k : k + 1], (seqs, 128)) == lane // 2
        named += jnp.where(hit, 1.0, 0.0)
        weights += jnp.where(hit, jnp.broadcast_to(gates[:, k : k + 1], (seqs, 128)), 0.0)
    earlier = jnp.zeros((1, 128), f32)
    ranks = []
    for b in range(seqs):
        ranks.append(earlier)
        earlier = earlier + named[b : b + 1]
    rank = jnp.concatenate(ranks, 0)
    chosen = (named > 0.5) & (jnp.abs(rank - (lane % 2).astype(f32)) < 0.5)
    weighting[...] = jnp.where(chosen, weights, 0.0)
    square = jnp.concatenate(
        [jnp.where(chosen, 1.0, 0.0), jnp.zeros((128 - seqs, 128), f32)], 0
    )
    placing[...] = square.T.astype(jnp.bfloat16)


def line_place():
    first = lax.axis_index("ctx")
    return jnp.where(lax.axis_index("exp") % 2 == 1, first // 4, first % 4)


def project_kernel(tokens_hbm, gain_hbm, w_hbm, out, tokens, gain, w_ref, small, sems):
    f32, bf16 = jnp.float32, jnp.bfloat16
    chunks = sems.shape[0]
    cols = w_hbm.shape[1]
    width = cols // chunks
    copies = [
        pltpu.make_async_copy(
            w_hbm.at[:, pl.ds(c * width, width)], w_ref.at[:, pl.ds(c * width, width)], sems.at[c]
        )
        for c in range(chunks)
    ]
    first = [
        pltpu.make_async_copy(tokens_hbm, tokens, small.at[0]),
        pltpu.make_async_copy(gain_hbm, gain, small.at[1]),
    ]
    for copy in first + copies:
        copy.start()
    for copy in first:
        copy.wait()
    xf = tokens[...].astype(f32)
    scaled = (xf * gain[...]).astype(bf16)
    squares = jnp.sum(xf * xf, 1, keepdims=True) * (SQUARES / D)
    out[:, cols:] = halves(squares).astype(f32)
    for c, copy in enumerate(copies):
        copy.wait()
        at = slice(c * width, (c + 1) * width)
        out[:, at] = jnp.dot(scaled, w_ref[:, at], preferred_element_type=f32) * SHARES


def load_kernel(after, *refs):
    count = len(refs) // 2
    sems = refs[-1]
    copies = [
        pltpu.make_async_copy(refs[i], refs[count + i], sems.at[i]) for i in range(count)
    ]
    for copy in copies:
        copy.start()
    for copy in copies:
        copy.wait()


def add_kernel(m0, m1, m3, m2, *rest):
    f32, bf16 = jnp.float32, jnp.bfloat16
    out = rest[-1]
    cols = out.shape[1] - 128

    def total(at):
        p, q, r, s = (m[:, at].astype(f32) for m in (m0, m1, m2, m3))
        return (p + q) + (r + s)

    out[:, :cols] = total(slice(0, cols)).astype(bf16)
    squares = total(slice(cols, cols + 128))
    out[:, cols:] = halves((squares + pltpu.roll(squares, 64, 1))[:, :1])


def attend_kernel(
    seqs, shares, cosine, sine, live_ref, owns, k_ref, v_ref, after, out, rows
):
    f32, bf16 = jnp.float32, jnp.bfloat16
    qh, kvh, hd = QUERY_HEADS, KEY_VALUE_HEADS, HEAD_DIMENSION
    group = qh // kvh
    positions = k_ref.shape[1]

    def share(h):
        return shares[:, h * hd : (h + 1) * hd]

    squares = share(qh + 2 * kvh)
    norm = lax.rsqrt((squares + pltpu.roll(squares, 64, 1)) / SQUARES + 1e-06) / SHARES
    cos, sin = cosine[...] * norm, sine[...] * norm
    scale = hd**-0.5
    cos_q, sin_q = cos * scale, sin * scale
    for h in range(qh):
        v = share(h)
        rows[h * seqs : (h + 1) * seqs, :] = v * cos_q + pltpu.roll(v, hd // 2, 1) * sin_q
    for h in range(qh, qh + kvh):
        v = share(h)
        rows[h * seqs : (h + 1) * seqs, :] = v * cos + pltpu.roll(v, hd // 2, 1) * sin
    for h in range(qh + kvh, qh + 2 * kvh):
        rows[h * seqs : (h + 1) * seqs, :] = share(h) * norm

    def grouped(first, b):
        at = [(first + g) * seqs + b for g in range(kvh)]
        return jnp.concatenate(
            [jnp.broadcast_to(rows[i : i + 1, :], (group, hd)) for i in at], 0
        )

    owns_new = jnp.broadcast_to(owns[0:1, :], (qh, 128))[:, :1] > 0.5
    zero = jnp.zeros((group, hd), f32)
    lanes = lane_ids()
    logs = jnp.zeros((qh, 128), f32)
    scores, fresh = [], []
    for b in range(seqs):
        q = rows[pl.ds(b, qh, stride=seqs), :]
        fresh.append(jnp.where(owns_new, jnp.sum(q * grouped(qh, b), 1, keepdims=True), -1e30))
        wide = jnp.concatenate(
            [
                jnp.concatenate(
                    [q[g * group : (g + 1) * group] if c == g else zero for c in range(kvh)], 1
                )
                for g in range(kvh)
            ],
            0,
        )
        high = wide.astype(bf16)
        low = (wide - high.astype(f32)).astype(bf16)
        both = lax.dot_general(
            jnp.concatenate([high, low], 0),
            k_ref[b],
            (((1,), (1,)), ((), ())),
            preferred_element_type=f32,
        )
        scores.append(both[:qh] + both[qh:])
    tops, weights, news, totals = [], [], [], []
    for b in range(seqs):
        live = jnp.broadcast_to(live_ref[b : b + 1, :], (qh, positions)) > 0.5
        s = jnp.where(live, scores[b], -1e30)
        top = jnp.maximum(jnp.max(s, 1, keepdims=True), fresh[b])
        p = jnp.where(live, jnp.exp(s - top), 0.0)
        p_new = jnp.where(owns_new, jnp.exp(fresh[b] - top), 0.0)
        tops.append(top)
        weights.append(p.astype(bf16))
        news.append(p_new)
        totals.append(jnp.sum(p, 1, keepdims=True) + p_new)
    for b in range(seqs):
        acc = jnp.dot(weights[b], v_ref[b], preferred_element_type=f32)
        acc = jnp.concatenate(
            [acc[g * group : (g + 1) * group, g * hd : (g + 1) * hd] for g in range(kvh)], 0
        )
        some = totals[b] > 0
        safe = jnp.where(some, totals[b], 1.0)
        value = (acc + news[b] * grouped(qh + kvh, b)) / safe
        out[b * qh : (b + 1) * qh, :] = value.astype(bf16)
        log = jnp.where(some, tops[b] + jnp.log(safe), -1e30)
        logs = jnp.where(lanes == b, log, logs)
    out[seqs * qh : (seqs + 1) * qh, :] = spread(logs, seqs)


def merged(seqs, parts):
    qh = QUERY_HEADS
    logs = [gather_terms(p[seqs * qh : (seqs + 1) * qh, :], seqs) for p in parts]
    top = jnp.maximum(jnp.maximum(logs[0], logs[1]), jnp.maximum(logs[2], logs[3]))
    weights = [jnp.exp(v - top) for v in logs]
    total = (weights[0] + weights[1]) + (weights[2] + weights[3])
    shares = [w / total for w in weights]
    values = []
    for b in range(seqs):
        v = [
            p[b * qh : (b + 1) * qh, :].astype(jnp.float32) * w[:, b : b + 1]
            for p, w in zip(parts, shares)
        ]
        values.append((v[0] + v[1]) + (v[2] + v[3]))
    return values, top + jnp.log(total)


def merge_kernel(seqs, p0, p1, p3, p2, after, out):
    qh = QUERY_HEADS
    values, log = merged(seqs, (p0, p1, p2, p3))
    for b in range(seqs):
        out[b * qh : (b + 1) * qh, :] = values[b].astype(jnp.bfloat16)
    out[seqs * qh : (seqs + 1) * qh, :] = spread(log, seqs)


def finish_kernel(seqs, p0, p1, p3, p2, tokens, placing, w_ref, context, resid, outgoing, rows):
    f32, bf16 = jnp.float32, jnp.bfloat16
    qh = QUERY_HEADS
    values, _ = merged(seqs, (p0, p1, p2, p3))
    for b in range(seqs):
        rows[pl.ds(b, qh, stride=seqs), :] = values[b]
    whole = jnp.concatenate([rows[h * seqs : (h + 1) * seqs, :] for h in range(qh)], 1).astype(bf16)
    context[...] = whole
    attn = jnp.dot(whole, w_ref[...], preferred_element_type=f32)
    after = (tokens[...].astype(f32) + attn).astype(bf16)
    resid[...] = after
    padded = jnp.concatenate(
        [after.astype(f32), jnp.zeros((placing.shape[1] - seqs, after.shape[1]), f32)], 0
    ).astype(bf16)
    outgoing[...] = jnp.dot(placing[...], padded, preferred_element_type=f32).astype(bf16)


def own_rows(capacity, per_source, n_rows, width, j):
    row = lax.broadcasted_iota(jnp.int32, (n_rows, width), 0)
    return lax.rem(row, per_source) // capacity == j


def gate_up_kernel(capacity, x_ref, gain, w_ref, *outs):
    f32, bf16 = jnp.float32, jnp.bfloat16
    n_rows, width = x_ref.shape
    experts, _, cols = w_ref.shape
    part = n_rows // len(outs)
    place = line_place()
    xf = jnp.concatenate(
        [
            x_ref[pl.ds(pl.multiple_of((place ^ s) * part, part), part), :]
            for s in range(len(outs))
        ],
        0,
    ).astype(f32)
    squares = halves(jnp.sum(xf * xf, 1, keepdims=True))
    gained = xf * gain[...]
    blocks = [
        jnp.where(own_rows(capacity, experts * capacity, n_rows, width, j), gained, 0.0).astype(bf16)
        for j in range(experts)
    ]
    for s, out in enumerate(outs):
        out[:, cols:] = squares[s * part : (s + 1) * part]
    step = 256
    for c in range(0, cols, step):
        total = jnp.dot(blocks[0], w_ref[0, :, c : c + step], preferred_element_type=f32)
        for j in range(1, experts):
            total += jnp.dot(blocks[j], w_ref[j, :, c : c + step], preferred_element_type=f32)
        total = total.astype(bf16)
        for s, out in enumerate(outs):
            out[:, c : c + step] = total[s * part : (s + 1) * part]


def activate_kernel(m0, m1, m3, m2, out):
    f32, bf16 = jnp.float32, jnp.bfloat16
    hidden = out.shape[1]

    def total(at):
        p, q, r, s = (m[:, at].astype(f32) for m in (m0, m1, m2, m3))
        return (p + q) + (r + s)

    squares = total(slice(2 * hidden, 2 * hidden + 128))
    norm = lax.rsqrt((squares + pltpu.roll(squares, 64, 1)) / D + 1e-06)[:, :1]
    gate = total(slice(0, hidden)) * norm
    up = total(slice(hidden, 2 * hidden)) * norm
    out[...] = (gate / (1.0 + jnp.exp(-gate)) * up).astype(bf16)


def down_kernel(capacity, x0, x1, x3, x2, w_ref, out):
    f32 = jnp.float32
    xf = jnp.concatenate([x[...].astype(f32) for x in (x0, x1, x2, x3)], 0)
    n_rows, width = xf.shape
    part = n_rows // 4
    experts = w_ref.shape[0]
    total = None
    for j in range(experts):
        mine = own_rows(capacity, experts * capacity, n_rows, width, j)
        block = jnp.where(mine, xf, 0.0).astype(jnp.bfloat16)
        share = jnp.dot(block, w_ref[j], preferred_element_type=f32)
        total = share if total is None else total + share
    total = total.astype(jnp.bfloat16)
    place = line_place()
    for s in range(4):
        at = pl.ds(pl.multiple_of((place ^ s) * part, part), part)
        out[at, :] = total[s * part : (s + 1) * part]


def combine_kernel(resid, weighting, returned, out):
    f32, bf16 = jnp.float32, jnp.bfloat16
    weights = weighting[...]
    seqs = weights.shape[0]
    high = weights.astype(bf16).astype(f32)
    rest = weights - high
    middle = rest.astype(bf16).astype(f32)
    low = rest - middle
    stack = jnp.concatenate([high, middle, low, jnp.zeros_like(low)], 0).astype(bf16)
    sums = jnp.dot(stack, returned[...], preferred_element_type=f32)
    moe = (sums[:seqs] + sums[seqs : 2 * seqs]) + sums[2 * seqs : 3 * seqs]
    out[...] = (resid[...].astype(f32) + moe).astype(bf16)


VM = pl.BlockSpec(memory_space=pltpu.VMEM)
ANY = pl.BlockSpec(memory_space=pl.ANY)
HBM = pl.BlockSpec(memory_space=pltpu.HBM)
SM = pl.BlockSpec(memory_space=pltpu.SMEM)


def shape(dims, dtype=jnp.bfloat16):
    return jax.ShapeDtypeStruct(dims, dtype)


def call(kernel, name, out, inputs, specs, scratch=(), mib=8):
    return pl.pallas_call(
        kernel,
        out_shape=out,
        in_specs=specs,
        out_specs=jax.tree.map(lambda _: VM, out),
        scratch_shapes=list(scratch),
        compiler_params=pltpu.CompilerParams(vmem_limit_bytes=mib << 20),
        name=name,
    )(*inputs)


def near(array):
    return pltpu.with_memory_space_constraint(array, pltpu.VMEM)


def load(after, *arrays):
    kept = [pltpu.with_memory_space_constraint(a, pltpu.HBM) for a in arrays]
    return call(
        load_kernel,
        "load",
        tuple(pltpu.VMEM(a.shape, a.dtype) for a in arrays),
        (near(after), *kept),
        [VM] + [HBM] * len(arrays),
        [pltpu.SemaphoreType.DMA((len(arrays),))],
    )


def local(
    tokens,
    attn_gain,
    w_qkv,
    w_out,
    k_cache,
    value_cache,
    lengths,
    moe_gain,
    routes,
    gates,
    w_in,
    w_down,
):
    f32, bf16 = jnp.float32, jnp.bfloat16
    seqs, slice_width = tokens.shape
    hd = HEAD_DIMENSION
    hidden = w_down.shape[1]
    local_exp = w_in.shape[0]
    n_ctx, n_exp = lax.axis_size("ctx"), lax.axis_size("exp")
    experts_all = local_exp * n_exp
    top_k = routes.shape[1]
    capacity = 2 * seqs * top_k // experts_all
    per_source = local_exp * capacity

    cols = w_qkv.shape[1]
    message = call(
        project_kernel,
        "project",
        pltpu.VMEM((seqs, cols + 128), f32),
        [
            pltpu.with_memory_space_constraint(a, pltpu.HBM)
            for a in (tokens, attn_gain[None], w_qkv)
        ],
        [HBM] * 3,
        [
            pltpu.VMEM(tokens.shape, bf16),
            pltpu.VMEM((1, slice_width), f32),
            pltpu.VMEM(w_qkv.shape, bf16),
            pltpu.SemaphoreType.DMA((2,)),
            pltpu.SemaphoreType.DMA((2,)),
        ],
    )
    whole, message = message, lax.optimization_barrier(message.astype(jnp.float16))
    got = exchange(message, 0, n_ctx, n_exp)
    keys, values = load(whole, k_cache, value_cache)
    live, owns, placing, weighting = call(
        prepare_kernel,
        "prepare",
        (
            pltpu.VMEM((seqs, 128), f32),
            pltpu.VMEM((seqs, 128), f32),
            pltpu.VMEM((128, 128), bf16),
            pltpu.VMEM((seqs, 128), f32),
        ),
        (lengths, routes, gates, near(whole)),
        [SM] + [VM] * 3,
    )
    cosine, sine = rotation(lengths, hd)
    total = added([message] + got)
    message = lax.optimization_barrier(total.astype(jnp.float16))
    shares = added([message] + exchange(message, 1, n_ctx, n_exp))
    (w_near,) = load(total, w_out)

    part = call(
        functools.partial(attend_kernel, seqs),
        "attend",
        shape(((seqs + 1) * QUERY_HEADS, hd)),
        (shares, cosine, sine, near(live), near(owns), near(keys), near(values), near(w_near)),
        [VM] * 8,
        [pltpu.VMEM((cols // hd * seqs, hd), f32)],
    )
    parts = [part] + exchange(part, 0, n_ctx, n_exp)
    (w_in_near,) = load(part, w_in)
    part = call(
        functools.partial(merge_kernel, seqs),
        "merge",
        shape(part.shape),
        parts + [near(w_in_near)],
        [VM] * 5,
    )
    context, resid, outgoing = call(
        functools.partial(finish_kernel, seqs),
        "finish",
        (
            pltpu.VMEM((seqs, QUERY_HEADS * hd), bf16),
            shape(tokens.shape),
            shape((placing.shape[0], slice_width)),
        ),
        [part] + exchange(part, 1, n_ctx, n_exp) + [tokens, near(placing), near(w_near)],
        [VM] * 7,
        [pltpu.VMEM((QUERY_HEADS * seqs, hd), f32)],
    )

    n_rows = n_exp * per_source
    rows = lax.all_to_all(
        outgoing.reshape(n_exp, per_source, slice_width), "exp", split_axis=0, concat_axis=0, tiled=True
    )
    side = 4
    wide = 2 * hidden + 128
    sent = call(
        functools.partial(gate_up_kernel, capacity),
        "gate_up",
        (shape((n_rows // side, wide)),) * side,
        (rows.reshape(n_rows, slice_width), moe_gain[None], near(w_in_near)),
        [VM] * 3,
    )
    got = [sent[0]] + exchange(sent[1:], 0, n_ctx, n_exp)[::-1]
    w_down_near, context = pl.pallas_call(
        load_kernel,
        out_shape=(pltpu.VMEM(w_down.shape, bf16), shape(context.shape)),
        in_specs=[VM, HBM, VM],
        out_specs=(VM, HBM),
        scratch_shapes=[pltpu.SemaphoreType.DMA((2,))],
        compiler_params=pltpu.CompilerParams(vmem_limit_bytes=8 << 20),
        name="settle",
    )(near(sent[0]), pltpu.with_memory_space_constraint(w_down, pltpu.HBM), near(context))
    total = call(
        add_kernel, "add_rows", shape(got[0].shape), got + [near(w_down_near)], [VM] * 5
    )
    act = call(
        activate_kernel,
        "activate",
        shape((n_rows // side, hidden)),
        [total] + exchange(total, 1, n_ctx, n_exp),
        [VM] * 4,
    )
    expert_out = call(
        functools.partial(down_kernel, capacity),
        "down",
        shape((n_rows, slice_width)),
        [act] + exchange(act, 0, n_ctx, n_exp) + [near(w_down_near)],
        [VM] * 5,
    )
    returned = lax.all_to_all(
        expert_out.reshape(n_exp, per_source, slice_width), "exp", split_axis=0, concat_axis=0, tiled=True
    )
    layer_out = call(
        combine_kernel,
        "combine",
        shape(tokens.shape),
        (resid, near(weighting), returned.reshape(n_rows, slice_width)),
        [VM] * 3,
    )
    return (context, layer_out)


def solution(mesh):
    placed = (
        P("exp", "ctx"),
        P("ctx"),
        P("ctx", None),
        P(None, "ctx"),
        P("exp", "ctx", None),
        P("exp", "ctx", None),
        P("exp"),
        P("ctx"),
        P("exp", None),
        P("exp", None),
        P("exp", "ctx", None),
        P("exp", None, "ctx"),
    )
    return jax.shard_map(
        local,
        mesh=mesh,
        in_specs=placed,
        out_specs=(P("exp", None), P("exp", "ctx")),
        check_vma=False,
    )
```

```python
import functools

import jax
import jax.numpy as jnp
from jax import lax
from jax.experimental import pallas as pl
from jax.experimental.pallas import tpu as pltpu
from jax.sharding import PartitionSpec as P

D = 4096
QUERY_HEADS = 32
KEY_VALUE_HEADS = 4
HEAD_DIMENSION = 128
AXES = ("ctx", "exp")
SQUARES = 1024.0
SHARES = 16.0


def exchange(value, stage, n_ctx, n_exp, turned=True):
    side = 4
    got = {}
    for step in (2, 3, 1) if isinstance(value, (list, tuple)) else (1, 3, 2):
        pairs = []
        for i in range(n_ctx):
            for e in range(n_exp):
                along_x = (e & 1 if turned else 1) == stage
                j = i ^ step if along_x else i ^ (side * step)
                pairs.append((i * n_exp + e, j * n_exp + e))
        sent = value[step - 1] if isinstance(value, (list, tuple)) else value
        got[step] = lax.ppermute(sent, AXES, pairs)
    return [got[step] for step in (1, 3, 2)]


def rotation(pos, size):
    half = size // 2
    freq = jnp.exp(-jnp.log(1000000.0) * jnp.arange(half).astype(jnp.float32) / half)
    angle = pos.astype(jnp.float32)[:, None] * freq[None, :]
    cosine, sine = jnp.cos(angle), jnp.sin(angle)
    return jnp.concatenate([cosine, cosine], -1), jnp.concatenate([-sine, sine], -1)


def lane_ids():
    return lax.broadcasted_iota(jnp.int32, (QUERY_HEADS, 128), 1)


def spread(log, seqs):
    log = jnp.where(lane_ids() < seqs, log, 0.0)
    high = log.astype(jnp.bfloat16).astype(jnp.float32)
    rest = log - high
    middle = rest.astype(jnp.bfloat16).astype(jnp.float32)
    low = rest - middle
    terms = high + pltpu.roll(middle, seqs, 1) + pltpu.roll(low, 2 * seqs, 1)
    return terms.astype(jnp.bfloat16)


def gather_terms(block, seqs):
    terms = block.astype(jnp.float32)
    return (terms + pltpu.roll(terms, 128 - seqs, 1)) + pltpu.roll(terms, 128 - 2 * seqs, 1)


def halves(value):
    high = value.astype(jnp.bfloat16).astype(jnp.float32)
    lane = lax.broadcasted_iota(jnp.int32, (value.shape[0], 128), 1)
    return jnp.where(lane < 64, high, value - high).astype(jnp.bfloat16)


def added(arrays):
    own, one, three, two = (a.astype(jnp.float32) for a in arrays)
    return (own + one) + (three + two)


def prepare_kernel(lengths, routes, gates, after, live, owns, placing, weighting):
    f32 = jnp.float32
    seqs, top_k = routes.shape
    lane = lax.broadcasted_iota(jnp.int32, (seqs, 128), 1)
    row = lax.broadcasted_iota(jnp.int32, (seqs, 128), 0)
    first = lax.axis_index("ctx")
    limits = jnp.zeros((seqs, 128), jnp.int32)
    for b in range(seqs):
        limits = jnp.where(row == b, lengths[b], limits)
    live[...] = jnp.where(lane + first * 128 < limits, 1.0, 0.0)
    owns[...] = jnp.where(lane * 0 + first == 0, 1.0, 0.0)
    named = jnp.zeros((seqs, 128), f32)
    weights = jnp.zeros((seqs, 128), f32)
    for k in range(top_k):
        hit = jnp.broadcast_to(routes[:, k : k + 1], (seqs, 128)) == lane // 2
        named += jnp.where(hit, 1.0, 0.0)
        weights += jnp.where(hit, jnp.broadcast_to(gates[:, k : k + 1], (seqs, 128)), 0.0)
    earlier = jnp.zeros((1, 128), f32)
    ranks = []
    for b in range(seqs):
        ranks.append(earlier)
        earlier = earlier + named[b : b + 1]
    rank = jnp.concatenate(ranks, 0)
    chosen = (named > 0.5) & (jnp.abs(rank - (lane % 2).astype(f32)) < 0.5)
    weighting[...] = jnp.where(chosen, weights, 0.0)
    square = jnp.concatenate(
        [jnp.where(chosen, 1.0, 0.0), jnp.zeros((128 - seqs, 128), f32)], 0
    )
    placing[...] = square.T.astype(jnp.bfloat16)


def line_place():
    return lax.axis_index("ctx") // 4


def project_kernel(tokens_hbm, gain_hbm, w_hbm, out, tokens, gain, w_ref, small, sems):
    f32, bf16 = jnp.float32, jnp.bfloat16
    chunks = sems.shape[0]
    cols = w_hbm.shape[1]
    width = cols // chunks
    copies = [
        pltpu.make_async_copy(
            w_hbm.at[:, pl.ds(c * width, width)], w_ref.at[:, pl.ds(c * width, width)], sems.at[c]
        )
        for c in range(chunks)
    ]
    first = [
        pltpu.make_async_copy(tokens_hbm, tokens, small.at[0]),
        pltpu.make_async_copy(gain_hbm, gain, small.at[1]),
    ]
    for copy in first + copies:
        copy.start()
    for copy in first:
        copy.wait()
    xf = tokens[...].astype(f32)
    scaled = (xf * gain[...]).astype(bf16)
    squares = jnp.sum(xf * xf, 1, keepdims=True) * (SQUARES / D)
    out[:, cols:] = halves(squares).astype(f32)
    for c, copy in enumerate(copies):
        copy.wait()
        at = slice(c * width, (c + 1) * width)
        out[:, at] = jnp.dot(scaled, w_ref[:, at], preferred_element_type=f32) * SHARES


def load_kernel(after, *refs):
    count = len(refs) // 2
    sems = refs[-1]
    copies = [
        pltpu.make_async_copy(refs[i], refs[count + i], sems.at[i]) for i in range(count)
    ]
    for copy in copies:
        copy.start()
    for copy in copies:
        copy.wait()


def add_kernel(m0, m1, m3, m2, *rest):
    f32, bf16 = jnp.float32, jnp.bfloat16
    out = rest[-1]
    cols = out.shape[1] - 128

    def total(at):
        p, q, r, s = (m[:, at].astype(f32) for m in (m0, m1, m2, m3))
        return (p + q) + (r + s)

    out[:, :cols] = total(slice(0, cols)).astype(bf16)
    squares = total(slice(cols, cols + 128))
    out[:, cols:] = halves((squares + pltpu.roll(squares, 64, 1))[:, :1])


def attend_kernel(
    seqs, shares, cosine, sine, live_ref, owns, k_ref, v_ref, after, out, rows
):
    f32, bf16 = jnp.float32, jnp.bfloat16
    qh, kvh, hd = QUERY_HEADS, KEY_VALUE_HEADS, HEAD_DIMENSION
    group = qh // kvh
    positions = k_ref.shape[1]

    def share(h):
        return shares[:, h * hd : (h + 1) * hd]

    squares = share(qh + 2 * kvh)
    norm = lax.rsqrt((squares + pltpu.roll(squares, 64, 1)) / SQUARES + 1e-06) / SHARES
    cos, sin = cosine[...] * norm, sine[...] * norm
    scale = hd**-0.5
    cos_q, sin_q = cos * scale, sin * scale
    for h in range(qh):
        v = share(h)
        rows[h * seqs : (h + 1) * seqs, :] = v * cos_q + pltpu.roll(v, hd // 2, 1) * sin_q
    for h in range(qh, qh + kvh):
        v = share(h)
        rows[h * seqs : (h + 1) * seqs, :] = v * cos + pltpu.roll(v, hd // 2, 1) * sin
    for h in range(qh + kvh, qh + 2 * kvh):
        rows[h * seqs : (h + 1) * seqs, :] = share(h) * norm

    def grouped(first, b):
        at = [(first + g) * seqs + b for g in range(kvh)]
        return jnp.concatenate(
            [jnp.broadcast_to(rows[i : i + 1, :], (group, hd)) for i in at], 0
        )

    owns_new = jnp.broadcast_to(owns[0:1, :], (qh, 128))[:, :1] > 0.5
    zero = jnp.zeros((group, hd), f32)
    lanes = lane_ids()
    logs = jnp.zeros((qh, 128), f32)
    scores, fresh = [], []
    for b in range(seqs):
        q = rows[pl.ds(b, qh, stride=seqs), :]
        fresh.append(jnp.where(owns_new, jnp.sum(q * grouped(qh, b), 1, keepdims=True), -1e30))
        wide = jnp.concatenate(
            [
                jnp.concatenate(
                    [q[g * group : (g + 1) * group] if c == g else zero for c in range(kvh)], 1
                )
                for g in range(kvh)
            ],
            0,
        )
        high = wide.astype(bf16)
        low = (wide - high.astype(f32)).astype(bf16)
        both = lax.dot_general(
            jnp.concatenate([high, low], 0),
            k_ref[b],
            (((1,), (1,)), ((), ())),
            preferred_element_type=f32,
        )
        scores.append(both[:qh] + both[qh:])
    tops, weights, news, totals = [], [], [], []
    for b in range(seqs):
        live = jnp.broadcast_to(live_ref[b : b + 1, :], (qh, positions)) > 0.5
        s = jnp.where(live, scores[b], -1e30)
        top = jnp.maximum(jnp.max(s, 1, keepdims=True), fresh[b])
        p = jnp.where(live, jnp.exp(s - top), 0.0)
        p_new = jnp.where(owns_new, jnp.exp(fresh[b] - top), 0.0)
        tops.append(top)
        weights.append(p.astype(bf16))
        news.append(p_new)
        totals.append(jnp.sum(p, 1, keepdims=True) + p_new)
    for b in range(seqs):
        acc = jnp.dot(weights[b], v_ref[b], preferred_element_type=f32)
        acc = jnp.concatenate(
            [acc[g * group : (g + 1) * group, g * hd : (g + 1) * hd] for g in range(kvh)], 0
        )
        some = totals[b] > 0
        safe = jnp.where(some, totals[b], 1.0)
        value = (acc + news[b] * grouped(qh + kvh, b)) / safe
        out[b * qh : (b + 1) * qh, :] = value.astype(bf16)
        log = jnp.where(some, tops[b] + jnp.log(safe), -1e30)
        logs = jnp.where(lanes == b, log, logs)
    out[seqs * qh : (seqs + 1) * qh, :] = spread(logs, seqs)


def merged(seqs, parts):
    qh = QUERY_HEADS
    logs = [gather_terms(p[seqs * qh : (seqs + 1) * qh, :], seqs) for p in parts]
    top = jnp.maximum(jnp.maximum(logs[0], logs[1]), jnp.maximum(logs[2], logs[3]))
    weights = [jnp.exp(v - top) for v in logs]
    total = (weights[0] + weights[1]) + (weights[2] + weights[3])
    shares = [w / total for w in weights]
    values = []
    for b in range(seqs):
        v = [
            p[b * qh : (b + 1) * qh, :].astype(jnp.float32) * w[:, b : b + 1]
            for p, w in zip(parts, shares)
        ]
        values.append((v[0] + v[1]) + (v[2] + v[3]))
    return values, top + jnp.log(total)


def merge_kernel(seqs, p0, p1, p3, p2, after, out):
    qh = QUERY_HEADS
    values, log = merged(seqs, (p0, p1, p2, p3))
    for b in range(seqs):
        out[b * qh : (b + 1) * qh, :] = values[b].astype(jnp.bfloat16)
    out[seqs * qh : (seqs + 1) * qh, :] = spread(log, seqs)


def finish_kernel(seqs, p0, p1, p3, p2, tokens, placing, w_ref, context, resid, outgoing, rows):
    f32, bf16 = jnp.float32, jnp.bfloat16
    qh = QUERY_HEADS
    values, _ = merged(seqs, (p0, p1, p2, p3))
    for b in range(seqs):
        rows[pl.ds(b, qh, stride=seqs), :] = values[b]
    whole = jnp.concatenate([rows[h * seqs : (h + 1) * seqs, :] for h in range(qh)], 1).astype(bf16)
    context[...] = whole
    attn = jnp.dot(whole, w_ref[...], preferred_element_type=f32)
    after = (tokens[...].astype(f32) + attn).astype(bf16)
    resid[...] = after
    padded = jnp.concatenate(
        [after.astype(f32), jnp.zeros((placing.shape[1] - seqs, after.shape[1]), f32)], 0
    ).astype(bf16)
    outgoing[...] = jnp.dot(placing[...], padded, preferred_element_type=f32).astype(bf16)


def own_rows(capacity, per_source, n_rows, width, j):
    row = lax.broadcasted_iota(jnp.int32, (n_rows, width), 0)
    return lax.rem(row, per_source) // capacity == j


def gate_up_kernel(capacity, x_ref, gain, w_ref, *outs):
    f32, bf16 = jnp.float32, jnp.bfloat16
    n_rows, width = x_ref.shape
    experts, _, cols = w_ref.shape
    part = n_rows // len(outs)
    place = line_place()
    xf = jnp.concatenate(
        [
            x_ref[pl.ds(pl.multiple_of((place ^ s) * part, part), part), :]
            for s in range(len(outs))
        ],
        0,
    ).astype(f32)
    squares = halves(jnp.sum(xf * xf, 1, keepdims=True))
    gained = xf * gain[...]
    blocks = [
        jnp.where(own_rows(capacity, experts * capacity, n_rows, width, j), gained, 0.0).astype(bf16)
        for j in range(experts)
    ]
    for s, out in enumerate(outs):
        out[:, cols:] = squares[s * part : (s + 1) * part]
    step = 256
    for c in range(0, cols, step):
        total = jnp.dot(blocks[0], w_ref[0, :, c : c + step], preferred_element_type=f32)
        for j in range(1, experts):
            total += jnp.dot(blocks[j], w_ref[j, :, c : c + step], preferred_element_type=f32)
        total = total.astype(bf16)
        for s, out in enumerate(outs):
            out[:, c : c + step] = total[s * part : (s + 1) * part]


def activate_kernel(m0, m1, m3, m2, out):
    f32, bf16 = jnp.float32, jnp.bfloat16
    hidden = out.shape[1]

    def total(at):
        p, q, r, s = (m[:, at].astype(f32) for m in (m0, m1, m2, m3))
        return (p + q) + (r + s)

    squares = total(slice(2 * hidden, 2 * hidden + 128))
    norm = lax.rsqrt((squares + pltpu.roll(squares, 64, 1)) / D + 1e-06)[:, :1]
    gate = total(slice(0, hidden)) * norm
    up = total(slice(hidden, 2 * hidden)) * norm
    out[...] = (gate / (1.0 + jnp.exp(-gate)) * up).astype(bf16)


def down_kernel(capacity, x0, x1, x3, x2, w_ref, out):
    f32 = jnp.float32
    xf = jnp.concatenate([x[...].astype(f32) for x in (x0, x1, x2, x3)], 0)
    n_rows, width = xf.shape
    part = n_rows // 4
    experts = w_ref.shape[0]
    total = None
    for j in range(experts):
        mine = own_rows(capacity, experts * capacity, n_rows, width, j)
        block = jnp.where(mine, xf, 0.0).astype(jnp.bfloat16)
        share = jnp.dot(block, w_ref[j], preferred_element_type=f32)
        total = share if total is None else total + share
    total = total.astype(jnp.bfloat16)
    place = line_place()
    for s in range(4):
        at = pl.ds(pl.multiple_of((place ^ s) * part, part), part)
        out[at, :] = total[s * part : (s + 1) * part]


def combine_kernel(resid, weighting, returned, out):
    f32, bf16 = jnp.float32, jnp.bfloat16
    weights = weighting[...]
    seqs = weights.shape[0]
    high = weights.astype(bf16).astype(f32)
    rest = weights - high
    middle = rest.astype(bf16).astype(f32)
    low = rest - middle
    stack = jnp.concatenate([high, middle, low, jnp.zeros_like(low)], 0).astype(bf16)
    sums = jnp.dot(stack, returned[...], preferred_element_type=f32)
    moe = (sums[:seqs] + sums[seqs : 2 * seqs]) + sums[2 * seqs : 3 * seqs]
    out[...] = (resid[...].astype(f32) + moe).astype(bf16)


VM = pl.BlockSpec(memory_space=pltpu.VMEM)
ANY = pl.BlockSpec(memory_space=pl.ANY)
HBM = pl.BlockSpec(memory_space=pltpu.HBM)
SM = pl.BlockSpec(memory_space=pltpu.SMEM)


def shape(dims, dtype=jnp.bfloat16):
    return jax.ShapeDtypeStruct(dims, dtype)


def call(kernel, name, out, inputs, specs, scratch=(), mib=8):
    return pl.pallas_call(
        kernel,
        out_shape=out,
        in_specs=specs,
        out_specs=jax.tree.map(lambda _: VM, out),
        scratch_shapes=list(scratch),
        compiler_params=pltpu.CompilerParams(vmem_limit_bytes=mib << 20),
        name=name,
    )(*inputs)


def near(array):
    return pltpu.with_memory_space_constraint(array, pltpu.VMEM)


def load(after, *arrays):
    kept = [pltpu.with_memory_space_constraint(a, pltpu.HBM) for a in arrays]
    return call(
        load_kernel,
        "load",
        tuple(pltpu.VMEM(a.shape, a.dtype) for a in arrays),
        (near(after), *kept),
        [VM] + [HBM] * len(arrays),
        [pltpu.SemaphoreType.DMA((len(arrays),))],
    )


def local(
    tokens,
    attn_gain,
    w_qkv,
    w_out,
    k_cache,
    value_cache,
    lengths,
    moe_gain,
    routes,
    gates,
    w_in,
    w_down,
):
    f32, bf16 = jnp.float32, jnp.bfloat16
    seqs, slice_width = tokens.shape
    hd = HEAD_DIMENSION
    hidden = w_down.shape[1]
    local_exp = w_in.shape[0]
    n_ctx, n_exp = lax.axis_size("ctx"), lax.axis_size("exp")
    experts_all = local_exp * n_exp
    top_k = routes.shape[1]
    capacity = 2 * seqs * top_k // experts_all
    per_source = local_exp * capacity

    cols = w_qkv.shape[1]
    message = call(
        project_kernel,
        "project",
        pltpu.VMEM((seqs, cols + 128), f32),
        [
            pltpu.with_memory_space_constraint(a, pltpu.HBM)
            for a in (tokens, attn_gain[None], w_qkv)
        ],
        [HBM] * 3,
        [
            pltpu.VMEM(tokens.shape, bf16),
            pltpu.VMEM((1, slice_width), f32),
            pltpu.VMEM(w_qkv.shape, bf16),
            pltpu.SemaphoreType.DMA((2,)),
            pltpu.SemaphoreType.DMA((2,)),
        ],
    )
    whole, message = message, lax.optimization_barrier(message.astype(jnp.float16))
    got = exchange(message, 0, n_ctx, n_exp)
    keys, values = load(whole, k_cache, value_cache)
    live, owns, placing, weighting = call(
        prepare_kernel,
        "prepare",
        (
            pltpu.VMEM((seqs, 128), f32),
            pltpu.VMEM((seqs, 128), f32),
            pltpu.VMEM((128, 128), bf16),
            pltpu.VMEM((seqs, 128), f32),
        ),
        (lengths, routes, gates, near(whole)),
        [SM] + [VM] * 3,
    )
    cosine, sine = rotation(lengths, hd)
    total = added([message] + got)
    message = lax.optimization_barrier(total.astype(jnp.float16))
    shares = added([message] + exchange(message, 1, n_ctx, n_exp))
    (w_near,) = load(total, w_out)

    part = call(
        functools.partial(attend_kernel, seqs),
        "attend",
        shape(((seqs + 1) * QUERY_HEADS, hd)),
        (shares, cosine, sine, near(live), near(owns), near(keys), near(values), near(w_near)),
        [VM] * 8,
        [pltpu.VMEM((cols // hd * seqs, hd), f32)],
    )
    parts = [part] + exchange(part, 0, n_ctx, n_exp)
    (w_in_near,) = load(part, w_in)
    part = call(
        functools.partial(merge_kernel, seqs),
        "merge",
        shape(part.shape),
        parts + [near(w_in_near)],
        [VM] * 5,
    )
    context, resid, outgoing = call(
        functools.partial(finish_kernel, seqs),
        "finish",
        (
            pltpu.VMEM((seqs, QUERY_HEADS * hd), bf16),
            shape(tokens.shape),
            shape((placing.shape[0], slice_width)),
        ),
        [part] + exchange(part, 1, n_ctx, n_exp) + [tokens, near(placing), near(w_near)],
        [VM] * 7,
        [pltpu.VMEM((QUERY_HEADS * seqs, hd), f32)],
    )

    n_rows = n_exp * per_source
    rows = lax.all_to_all(
        outgoing.reshape(n_exp, per_source, slice_width), "exp", split_axis=0, concat_axis=0, tiled=True
    )
    side = 4
    wide = 2 * hidden + 128
    sent = call(
        functools.partial(gate_up_kernel, capacity),
        "gate_up",
        (shape((n_rows // side, wide)),) * side,
        (rows.reshape(n_rows, slice_width), moe_gain[None], near(w_in_near)),
        [VM] * 3,
    )
    got = [sent[0]] + exchange(sent[1:], 0, n_ctx, n_exp, False)[::-1]
    w_down_near, context = pl.pallas_call(
        load_kernel,
        out_shape=(pltpu.VMEM(w_down.shape, bf16), shape(context.shape)),
        in_specs=[VM, HBM, VM],
        out_specs=(VM, HBM),
        scratch_shapes=[pltpu.SemaphoreType.DMA((2,))],
        compiler_params=pltpu.CompilerParams(vmem_limit_bytes=8 << 20),
        name="settle",
    )(near(sent[0]), pltpu.with_memory_space_constraint(w_down, pltpu.HBM), near(context))
    total = call(
        add_kernel, "add_rows", shape(got[0].shape), got + [near(w_down_near)], [VM] * 5
    )
    act = call(
        activate_kernel,
        "activate",
        shape((n_rows // side, hidden)),
        [total] + exchange(total, 1, n_ctx, n_exp, False),
        [VM] * 4,
    )
    expert_out = call(
        functools.partial(down_kernel, capacity),
        "down",
        shape((n_rows, slice_width)),
        [act] + exchange(act, 0, n_ctx, n_exp, False) + [near(w_down_near)],
        [VM] * 5,
    )
    returned = lax.all_to_all(
        expert_out.reshape(n_exp, per_source, slice_width), "exp", split_axis=0, concat_axis=0, tiled=True
    )
    layer_out = call(
        combine_kernel,
        "combine",
        shape(tokens.shape),
        (resid, near(weighting), returned.reshape(n_rows, slice_width)),
        [VM] * 3,
    )
    return (context, layer_out)


def solution(mesh):
    placed = (
        P("exp", "ctx"),
        P("ctx"),
        P("ctx", None),
        P(None, "ctx"),
        P("exp", "ctx", None),
        P("exp", "ctx", None),
        P("exp"),
        P("ctx"),
        P("exp", None),
        P("exp", None),
        P("exp", "ctx", None),
        P("exp", None, "ctx"),
    )
    return jax.shard_map(
        local,
        mesh=mesh,
        in_specs=placed,
        out_specs=(P("exp", None), P("exp", "ctx")),
        check_vma=False,
    )
```

```python
import functools

import jax
import jax.numpy as jnp
from jax import lax
from jax.experimental import pallas as pl
from jax.experimental.pallas import tpu as pltpu
from jax.sharding import PartitionSpec as P

D = 4096
QUERY_HEADS = 32
KEY_VALUE_HEADS = 4
HEAD_DIMENSION = 128
AXES = ("ctx", "exp")
SQUARES = 1024.0
SHARES = 16.0


def exchange(value, stage, n_ctx, n_exp):
    side = 4
    got = {}
    for step in (2, 3, 1) if isinstance(value, (list, tuple)) else (1, 3, 2):
        pairs = []
        for i in range(n_ctx):
            for e in range(n_exp):
                j = i ^ step if (e & 1) == stage else i ^ (side * step)
                pairs.append((i * n_exp + e, j * n_exp + e))
        sent = value[step - 1] if isinstance(value, (list, tuple)) else value
        got[step] = lax.ppermute(sent, AXES, pairs)
    return [got[step] for step in (1, 3, 2)]


def rotation(pos, size):
    half = size // 2
    freq = jnp.exp(-jnp.log(1000000.0) * jnp.arange(half).astype(jnp.float32) / half)
    angle = pos.astype(jnp.float32)[:, None] * freq[None, :]
    cosine, sine = jnp.cos(angle), jnp.sin(angle)
    return jnp.concatenate([cosine, cosine], -1), jnp.concatenate([-sine, sine], -1)


def lane_ids():
    return lax.broadcasted_iota(jnp.int32, (QUERY_HEADS, 128), 1)


def spread(log, seqs):
    log = jnp.where(lane_ids() < seqs, log, 0.0)
    high = log.astype(jnp.bfloat16).astype(jnp.float32)
    rest = log - high
    middle = rest.astype(jnp.bfloat16).astype(jnp.float32)
    low = rest - middle
    terms = high + pltpu.roll(middle, seqs, 1) + pltpu.roll(low, 2 * seqs, 1)
    return terms.astype(jnp.bfloat16)


def gather_terms(block, seqs):
    terms = block.astype(jnp.float32)
    return (terms + pltpu.roll(terms, 128 - seqs, 1)) + pltpu.roll(terms, 128 - 2 * seqs, 1)


def halves(value):
    high = value.astype(jnp.bfloat16).astype(jnp.float32)
    lane = lax.broadcasted_iota(jnp.int32, (value.shape[0], 128), 1)
    return jnp.where(lane < 64, high, value - high).astype(jnp.bfloat16)


def added(arrays):
    own, one, three, two = (a.astype(jnp.float32) for a in arrays)
    return (own + one) + (three + two)


def prepare_kernel(lengths, routes, gates, after, live, owns, placing, weighting):
    f32 = jnp.float32
    seqs, top_k = routes.shape
    lane = lax.broadcasted_iota(jnp.int32, (seqs, 128), 1)
    row = lax.broadcasted_iota(jnp.int32, (seqs, 128), 0)
    first = lax.axis_index("ctx")
    limits = jnp.zeros((seqs, 128), jnp.int32)
    for b in range(seqs):
        limits = jnp.where(row == b, lengths[b], limits)
    live[...] = jnp.where(lane + first * 128 < limits, 1.0, 0.0)
    owns[...] = jnp.where(lane * 0 + first == 0, 1.0, 0.0)
    named = jnp.zeros((seqs, 128), f32)
    weights = jnp.zeros((seqs, 128), f32)
    for k in range(top_k):
        hit = jnp.broadcast_to(routes[:, k : k + 1], (seqs, 128)) == lane // 2
        named += jnp.where(hit, 1.0, 0.0)
        weights += jnp.where(hit, jnp.broadcast_to(gates[:, k : k + 1], (seqs, 128)), 0.0)
    earlier = jnp.zeros((1, 128), f32)
    ranks = []
    for b in range(seqs):
        ranks.append(earlier)
        earlier = earlier + named[b : b + 1]
    rank = jnp.concatenate(ranks, 0)
    chosen = (named > 0.5) & (jnp.abs(rank - (lane % 2).astype(f32)) < 0.5)
    weights = jnp.where(chosen, weights, 0.0)
    high = weights.astype(jnp.bfloat16).astype(f32)
    rest = weights - high
    middle = rest.astype(jnp.bfloat16).astype(f32)
    low = rest - middle
    terms = jnp.concatenate([high, middle, low, jnp.zeros_like(low)], 0)
    weighting[...] = terms.astype(jnp.bfloat16)
    square = jnp.concatenate(
        [jnp.where(chosen, 1.0, 0.0), jnp.zeros((128 - seqs, 128), f32)], 0
    )
    placing[...] = square.T.astype(jnp.bfloat16)


def line_place():
    first = lax.axis_index("ctx")
    return jnp.where(lax.axis_index("exp") % 2 == 1, first // 4, first % 4)


def project_kernel(tokens_hbm, gain_hbm, w_hbm, out, tokens, gain, w_ref, small, sems):
    f32, bf16 = jnp.float32, jnp.bfloat16
    chunks = sems.shape[0]
    cols = w_hbm.shape[1]
    width = cols // chunks
    copies = [
        pltpu.make_async_copy(
            w_hbm.at[:, pl.ds(c * width, width)], w_ref.at[:, pl.ds(c * width, width)], sems.at[c]
        )
        for c in range(chunks)
    ]
    first = [
        pltpu.make_async_copy(tokens_hbm, tokens, small.at[0]),
        pltpu.make_async_copy(gain_hbm, gain, small.at[1]),
    ]
    for copy in first + copies:
        copy.start()
    for copy in first:
        copy.wait()
    xf = tokens[...].astype(f32)
    scaled = (xf * gain[...]).astype(bf16)
    squares = jnp.sum(xf * xf, 1, keepdims=True) * (SQUARES / D)
    out[:, cols:] = halves(squares).astype(f32)
    for c, copy in enumerate(copies):
        copy.wait()
        at = slice(c * width, (c + 1) * width)
        out[:, at] = jnp.dot(scaled, w_ref[:, at], preferred_element_type=f32) * SHARES


def load_kernel(after, *refs):
    count = len(refs) // 2
    sems = refs[-1]
    copies = [
        pltpu.make_async_copy(refs[i], refs[count + i], sems.at[i]) for i in range(count)
    ]
    for copy in copies:
        copy.start()
    for copy in copies:
        copy.wait()


def add_kernel(m0, m1, m3, m2, *rest):
    f32, bf16 = jnp.float32, jnp.bfloat16
    out = rest[-1]
    cols = out.shape[1] - 128

    def total(at):
        p, q, r, s = (m[:, at].astype(f32) for m in (m0, m1, m2, m3))
        return (p + q) + (r + s)

    out[:, :cols] = total(slice(0, cols)).astype(bf16)
    squares = total(slice(cols, cols + 128))
    out[:, cols:] = halves((squares + pltpu.roll(squares, 64, 1))[:, :1])


def attend_kernel(
    seqs, shares, cosine, sine, live_ref, owns, k_ref, v_ref, after, out, rows
):
    f32, bf16 = jnp.float32, jnp.bfloat16
    qh, kvh, hd = QUERY_HEADS, KEY_VALUE_HEADS, HEAD_DIMENSION
    group = qh // kvh
    positions = k_ref.shape[1]

    def share(h):
        return shares[:, h * hd : (h + 1) * hd]

    squares = share(qh + 2 * kvh)
    norm = lax.rsqrt((squares + pltpu.roll(squares, 64, 1)) / SQUARES + 1e-06) / SHARES
    cos, sin = cosine[...] * norm, sine[...] * norm
    scale = hd**-0.5
    cos_q, sin_q = cos * scale, sin * scale
    for h in range(qh):
        v = share(h)
        rows[h * seqs : (h + 1) * seqs, :] = v * cos_q + pltpu.roll(v, hd // 2, 1) * sin_q
    for h in range(qh, qh + kvh):
        v = share(h)
        rows[h * seqs : (h + 1) * seqs, :] = v * cos + pltpu.roll(v, hd // 2, 1) * sin
    for h in range(qh + kvh, qh + 2 * kvh):
        rows[h * seqs : (h + 1) * seqs, :] = share(h) * norm

    def grouped(first, b):
        at = [(first + g) * seqs + b for g in range(kvh)]
        return jnp.concatenate(
            [jnp.broadcast_to(rows[i : i + 1, :], (group, hd)) for i in at], 0
        )

    owns_new = jnp.broadcast_to(owns[0:1, :], (qh, 128))[:, :1] > 0.5
    zero = jnp.zeros((group, hd), f32)
    lanes = lane_ids()
    logs = jnp.zeros((qh, 128), f32)
    scores, fresh = [], []
    for b in range(seqs):
        q = rows[pl.ds(b, qh, stride=seqs), :]
        fresh.append(jnp.where(owns_new, jnp.sum(q * grouped(qh, b), 1, keepdims=True), -1e30))
        wide = jnp.concatenate(
            [
                jnp.concatenate(
                    [q[g * group : (g + 1) * group] if c == g else zero for c in range(kvh)], 1
                )
                for g in range(kvh)
            ],
            0,
        )
        high = wide.astype(bf16)
        low = (wide - high.astype(f32)).astype(bf16)
        both = lax.dot_general(
            jnp.concatenate([high, low], 0),
            k_ref[b],
            (((1,), (1,)), ((), ())),
            preferred_element_type=f32,
        )
        scores.append(both[:qh] + both[qh:])
    tops, weights, news, totals = [], [], [], []
    for b in range(seqs):
        live = jnp.broadcast_to(live_ref[b : b + 1, :], (qh, positions)) > 0.5
        s = jnp.where(live, scores[b], -1e30)
        top = jnp.maximum(jnp.max(s, 1, keepdims=True), fresh[b])
        p = jnp.where(live, jnp.exp(s - top), 0.0)
        p_new = jnp.where(owns_new, jnp.exp(fresh[b] - top), 0.0)
        tops.append(top)
        weights.append(p.astype(bf16))
        news.append(p_new)
        totals.append(jnp.sum(p, 1, keepdims=True) + p_new)
    for b in range(seqs):
        acc = jnp.dot(weights[b], v_ref[b], preferred_element_type=f32)
        acc = jnp.concatenate(
            [acc[g * group : (g + 1) * group, g * hd : (g + 1) * hd] for g in range(kvh)], 0
        )
        some = totals[b] > 0
        safe = jnp.where(some, totals[b], 1.0)
        value = (acc + news[b] * grouped(qh + kvh, b)) / safe
        out[b * qh : (b + 1) * qh, :] = value.astype(bf16)
        log = jnp.where(some, tops[b] + jnp.log(safe), -1e30)
        logs = jnp.where(lanes == b, log, logs)
    out[seqs * qh : (seqs + 1) * qh, :] = spread(logs, seqs)


def merged(seqs, parts):
    qh = QUERY_HEADS
    logs = [gather_terms(p[seqs * qh : (seqs + 1) * qh, :], seqs) for p in parts]
    top = jnp.maximum(jnp.maximum(logs[0], logs[1]), jnp.maximum(logs[2], logs[3]))
    weights = [jnp.exp(v - top) for v in logs]
    total = (weights[0] + weights[1]) + (weights[2] + weights[3])
    shares = [w / total for w in weights]
    values = []
    for b in range(seqs):
        v = [
            p[b * qh : (b + 1) * qh, :].astype(jnp.float32) * w[:, b : b + 1]
            for p, w in zip(parts, shares)
        ]
        values.append((v[0] + v[1]) + (v[2] + v[3]))
    return values, top + jnp.log(total)


def merge_kernel(seqs, p0, p1, p3, p2, after, out):
    qh = QUERY_HEADS
    values, log = merged(seqs, (p0, p1, p2, p3))
    for b in range(seqs):
        out[b * qh : (b + 1) * qh, :] = values[b].astype(jnp.bfloat16)
    out[seqs * qh : (seqs + 1) * qh, :] = spread(log, seqs)


def finish_kernel(seqs, p0, p1, p3, p2, tokens, placing, w_ref, context, resid, outgoing, rows):
    f32, bf16 = jnp.float32, jnp.bfloat16
    qh = QUERY_HEADS
    values, _ = merged(seqs, (p0, p1, p2, p3))
    for b in range(seqs):
        rows[pl.ds(b, qh, stride=seqs), :] = values[b]
    whole = jnp.concatenate([rows[h * seqs : (h + 1) * seqs, :] for h in range(qh)], 1).astype(bf16)
    context[...] = whole
    attn = jnp.dot(whole, w_ref[...], preferred_element_type=f32)
    after = (tokens[...].astype(f32) + attn).astype(bf16)
    resid[...] = after
    padded = jnp.concatenate(
        [after.astype(f32), jnp.zeros((placing.shape[1] - seqs, after.shape[1]), f32)], 0
    ).astype(bf16)
    outgoing[...] = jnp.dot(placing[...], padded, preferred_element_type=f32).astype(bf16)


def own_rows(capacity, per_source, n_rows, width, j):
    row = lax.broadcasted_iota(jnp.int32, (n_rows, width), 0)
    return lax.rem(row, per_source) // capacity == j


def gate_up_kernel(capacity, x_ref, gain, w_ref, *outs):
    f32, bf16 = jnp.float32, jnp.bfloat16
    n_rows, width = x_ref.shape
    experts, _, cols = w_ref.shape
    part = n_rows // len(outs)
    place = line_place()
    xf = jnp.concatenate(
        [
            x_ref[pl.ds(pl.multiple_of((place ^ s) * part, part), part), :]
            for s in range(len(outs))
        ],
        0,
    ).astype(f32)
    squares = halves(jnp.sum(xf * xf, 1, keepdims=True))
    gained = xf * gain[...]
    blocks = [
        jnp.where(own_rows(capacity, experts * capacity, n_rows, width, j), gained, 0.0).astype(bf16)
        for j in range(experts)
    ]
    for s, out in enumerate(outs):
        out[:, cols:] = squares[s * part : (s + 1) * part]
    step = 256
    for c in range(0, cols, step):
        total = jnp.dot(blocks[0], w_ref[0, :, c : c + step], preferred_element_type=f32)
        for j in range(1, experts):
            total += jnp.dot(blocks[j], w_ref[j, :, c : c + step], preferred_element_type=f32)
        total = total.astype(bf16)
        for s, out in enumerate(outs):
            out[:, c : c + step] = total[s * part : (s + 1) * part]


def activate_kernel(m0, m1, m3, m2, out):
    f32, bf16 = jnp.float32, jnp.bfloat16
    hidden = out.shape[1]

    def total(at):
        p, q, r, s = (m[:, at].astype(f32) for m in (m0, m1, m2, m3))
        return (p + q) + (r + s)

    squares = total(slice(2 * hidden, 2 * hidden + 128))
    norm = lax.rsqrt((squares + pltpu.roll(squares, 64, 1)) / D + 1e-06)[:, :1]
    gate = total(slice(0, hidden)) * norm
    up = total(slice(hidden, 2 * hidden)) * norm
    out[...] = (gate / (1.0 + jnp.exp(-gate)) * up).astype(bf16)


def down_kernel(capacity, x0, x1, x3, x2, w_ref, out):
    f32 = jnp.float32
    xf = jnp.concatenate([x[...].astype(f32) for x in (x0, x1, x2, x3)], 0)
    n_rows, width = xf.shape
    part = n_rows // 4
    experts = w_ref.shape[0]
    total = None
    for j in range(experts):
        mine = own_rows(capacity, experts * capacity, n_rows, width, j)
        block = jnp.where(mine, xf, 0.0).astype(jnp.bfloat16)
        share = jnp.dot(block, w_ref[j], preferred_element_type=f32)
        total = share if total is None else total + share
    total = total.astype(jnp.bfloat16)
    place = line_place()
    for s in range(4):
        at = pl.ds(pl.multiple_of((place ^ s) * part, part), part)
        out[at, :] = total[s * part : (s + 1) * part]


def combine_kernel(resid, weighting, returned, out):
    f32, bf16 = jnp.float32, jnp.bfloat16
    seqs = resid.shape[0]
    sums = jnp.dot(weighting[...], returned[...], preferred_element_type=f32)
    moe = (sums[:seqs] + sums[seqs : 2 * seqs]) + sums[2 * seqs : 3 * seqs]
    out[...] = (resid[...].astype(f32) + moe).astype(bf16)


VM = pl.BlockSpec(memory_space=pltpu.VMEM)
ANY = pl.BlockSpec(memory_space=pl.ANY)
HBM = pl.BlockSpec(memory_space=pltpu.HBM)
SM = pl.BlockSpec(memory_space=pltpu.SMEM)


def shape(dims, dtype=jnp.bfloat16):
    return jax.ShapeDtypeStruct(dims, dtype)


def call(kernel, name, out, inputs, specs, scratch=(), mib=8):
    return pl.pallas_call(
        kernel,
        out_shape=out,
        in_specs=specs,
        out_specs=jax.tree.map(lambda _: VM, out),
        scratch_shapes=list(scratch),
        compiler_params=pltpu.CompilerParams(vmem_limit_bytes=mib << 20),
        name=name,
    )(*inputs)


def near(array):
    return pltpu.with_memory_space_constraint(array, pltpu.VMEM)


def load(after, *arrays):
    kept = [pltpu.with_memory_space_constraint(a, pltpu.HBM) for a in arrays]
    return call(
        load_kernel,
        "load",
        tuple(pltpu.VMEM(a.shape, a.dtype) for a in arrays),
        (near(after), *kept),
        [VM] + [HBM] * len(arrays),
        [pltpu.SemaphoreType.DMA((len(arrays),))],
    )


def local(
    tokens,
    attn_gain,
    w_qkv,
    w_out,
    k_cache,
    value_cache,
    lengths,
    moe_gain,
    routes,
    gates,
    w_in,
    w_down,
):
    f32, bf16 = jnp.float32, jnp.bfloat16
    seqs, slice_width = tokens.shape
    hd = HEAD_DIMENSION
    hidden = w_down.shape[1]
    local_exp = w_in.shape[0]
    n_ctx, n_exp = lax.axis_size("ctx"), lax.axis_size("exp")
    experts_all = local_exp * n_exp
    top_k = routes.shape[1]
    capacity = 2 * seqs * top_k // experts_all
    per_source = local_exp * capacity

    cols = w_qkv.shape[1]
    message = call(
        project_kernel,
        "project",
        pltpu.VMEM((seqs, cols + 128), f32),
        [
            pltpu.with_memory_space_constraint(a, pltpu.HBM)
            for a in (tokens, attn_gain[None], w_qkv)
        ],
        [HBM] * 3,
        [
            pltpu.VMEM(tokens.shape, bf16),
            pltpu.VMEM((1, slice_width), f32),
            pltpu.VMEM(w_qkv.shape, bf16),
            pltpu.SemaphoreType.DMA((2,)),
            pltpu.SemaphoreType.DMA((2,)),
        ],
    )
    whole, message = message, lax.optimization_barrier(message.astype(jnp.float16))
    got = exchange(message, 0, n_ctx, n_exp)
    keys, values = load(whole, k_cache, value_cache)
    live, owns, placing, weighting = call(
        prepare_kernel,
        "prepare",
        (
            pltpu.VMEM((seqs, 128), f32),
            pltpu.VMEM((seqs, 128), f32),
            pltpu.VMEM((128, 128), bf16),
            pltpu.VMEM((4 * seqs, 128), bf16),
        ),
        (lengths, routes, gates, near(whole)),
        [SM] + [VM] * 3,
    )
    cosine, sine = rotation(lengths, hd)
    total = added([message] + got)
    message = lax.optimization_barrier(total.astype(jnp.float16))
    shares = added([message] + exchange(message, 1, n_ctx, n_exp))
    (w_near,) = load(total, w_out)

    part = call(
        functools.partial(attend_kernel, seqs),
        "attend",
        shape(((seqs + 1) * QUERY_HEADS, hd)),
        (shares, cosine, sine, near(live), near(owns), near(keys), near(values), near(w_near)),
        [VM] * 8,
        [pltpu.VMEM((cols // hd * seqs, hd), f32)],
    )
    parts = [part] + exchange(part, 0, n_ctx, n_exp)
    (w_in_near,) = load(part, w_in)
    part = call(
        functools.partial(merge_kernel, seqs),
        "merge",
        shape(part.shape),
        parts + [near(w_in_near)],
        [VM] * 5,
    )
    context, resid, outgoing = call(
        functools.partial(finish_kernel, seqs),
        "finish",
        (
            pltpu.VMEM((seqs, QUERY_HEADS * hd), bf16),
            shape(tokens.shape),
            shape((placing.shape[0], slice_width)),
        ),
        [part] + exchange(part, 1, n_ctx, n_exp) + [tokens, near(placing), near(w_near)],
        [VM] * 7,
        [pltpu.VMEM(((QUERY_HEADS + 1) * seqs, hd), f32)],
    )

    n_rows = n_exp * per_source
    rows = lax.all_to_all(
        outgoing.reshape(n_exp, per_source, slice_width), "exp", split_axis=0, concat_axis=0, tiled=True
    )
    side = 4
    wide = 2 * hidden + 128
    sent = call(
        functools.partial(gate_up_kernel, capacity),
        "gate_up",
        (shape((n_rows // side, wide)),) * side,
        (rows.reshape(n_rows, slice_width), moe_gain[None], near(w_in_near)),
        [VM] * 3,
    )
    got = [sent[0]] + exchange(sent[1:], 0, n_ctx, n_exp)[::-1]
    w_down_near, context = pl.pallas_call(
        load_kernel,
        out_shape=(pltpu.VMEM(w_down.shape, bf16), shape(context.shape)),
        in_specs=[VM, HBM, VM],
        out_specs=(VM, HBM),
        scratch_shapes=[pltpu.SemaphoreType.DMA((2,))],
        compiler_params=pltpu.CompilerParams(vmem_limit_bytes=8 << 20),
        name="settle",
    )(near(sent[0]), pltpu.with_memory_space_constraint(w_down, pltpu.HBM), near(context))
    total = call(
        add_kernel, "add_rows", shape(got[0].shape), got + [near(w_down_near)], [VM] * 5
    )
    act = call(
        activate_kernel,
        "activate",
        shape((n_rows // side, hidden)),
        [total] + exchange(total, 1, n_ctx, n_exp),
        [VM] * 4,
    )
    expert_out = call(
        functools.partial(down_kernel, capacity),
        "down",
        shape((n_rows, slice_width)),
        [act] + exchange(act, 0, n_ctx, n_exp) + [near(w_down_near)],
        [VM] * 5,
    )
    returned = lax.all_to_all(
        expert_out.reshape(n_exp, per_source, slice_width), "exp", split_axis=0, concat_axis=0, tiled=True
    )
    layer_out = call(
        combine_kernel,
        "combine",
        shape(tokens.shape),
        (resid, near(weighting), returned.reshape(n_rows, slice_width)),
        [VM] * 3,
    )
    return (context, layer_out)


def solution(mesh):
    placed = (
        P("exp", "ctx"),
        P("ctx"),
        P("ctx", None),
        P(None, "ctx"),
        P("exp", "ctx", None),
        P("exp", "ctx", None),
        P("exp"),
        P("ctx"),
        P("exp", None),
        P("exp", None),
        P("exp", "ctx", None),
        P("exp", None, "ctx"),
    )
    return jax.shard_map(
        local,
        mesh=mesh,
        in_specs=placed,
        out_specs=(P("exp", None), P("exp", "ctx")),
        check_vma=False,
    )
```

```python
import functools

import jax
import jax.numpy as jnp
from jax import lax
from jax.experimental import pallas as pl
from jax.experimental.pallas import tpu as pltpu
from jax.sharding import PartitionSpec as P

D = 4096
QUERY_HEADS = 32
KEY_VALUE_HEADS = 4
HEAD_DIMENSION = 128
AXES = ("ctx", "exp")
SQUARES = 1024.0
SHARES = 16.0


def exchange(value, stage, n_ctx, n_exp):
    side = 4
    got = {}
    for step in (2, 3, 1) if isinstance(value, (list, tuple)) else (1, 3, 2):
        pairs = []
        for i in range(n_ctx):
            for e in range(n_exp):
                j = i ^ step if (e & 1) == stage else i ^ (side * step)
                pairs.append((i * n_exp + e, j * n_exp + e))
        sent = value[step - 1] if isinstance(value, (list, tuple)) else value
        got[step] = lax.ppermute(sent, AXES, pairs)
    return [got[step] for step in (1, 3, 2)]


def rotation(pos, size):
    half = size // 2
    freq = jnp.exp(-jnp.log(1000000.0) * jnp.arange(half).astype(jnp.float32) / half)
    angle = pos.astype(jnp.float32)[:, None] * freq[None, :]
    cosine, sine = jnp.cos(angle), jnp.sin(angle)
    return jnp.concatenate([cosine, cosine], -1), jnp.concatenate([-sine, sine], -1)


def lane_ids():
    return lax.broadcasted_iota(jnp.int32, (QUERY_HEADS, 128), 1)


def spread(log, seqs):
    log = jnp.where(lane_ids() < seqs, log, 0.0)
    high = log.astype(jnp.bfloat16).astype(jnp.float32)
    rest = log - high
    middle = rest.astype(jnp.bfloat16).astype(jnp.float32)
    low = rest - middle
    terms = high + pltpu.roll(middle, seqs, 1) + pltpu.roll(low, 2 * seqs, 1)
    return terms.astype(jnp.bfloat16)


def gather_terms(block, seqs):
    terms = block.astype(jnp.float32)
    return (terms + pltpu.roll(terms, 128 - seqs, 1)) + pltpu.roll(terms, 128 - 2 * seqs, 1)


def halves(value):
    high = value.astype(jnp.bfloat16).astype(jnp.float32)
    lane = lax.broadcasted_iota(jnp.int32, (value.shape[0], 128), 1)
    return jnp.where(lane < 64, high, value - high).astype(jnp.bfloat16)


def added(arrays):
    own, one, three, two = (a.astype(jnp.float32) for a in arrays)
    return (own + one) + (three + two)


def prepare_kernel(lengths, routes, gates, after, live, owns, placing, weighting):
    f32 = jnp.float32
    seqs, top_k = routes.shape
    lane = lax.broadcasted_iota(jnp.int32, (seqs, 128), 1)
    row = lax.broadcasted_iota(jnp.int32, (seqs, 128), 0)
    first = lax.axis_index("ctx")
    limits = jnp.zeros((seqs, 128), jnp.int32)
    for b in range(seqs):
        limits = jnp.where(row == b, lengths[b], limits)
    live[...] = jnp.where(lane + first * 128 < limits, 1.0, 0.0)
    owns[...] = jnp.where(lane * 0 + first == 0, 1.0, 0.0)
    named = jnp.zeros((seqs, 128), f32)
    weights = jnp.zeros((seqs, 128), f32)
    for k in range(top_k):
        hit = jnp.broadcast_to(routes[:, k : k + 1], (seqs, 128)) == lane // 2
        named += jnp.where(hit, 1.0, 0.0)
        weights += jnp.where(hit, jnp.broadcast_to(gates[:, k : k + 1], (seqs, 128)), 0.0)
    earlier = jnp.zeros((1, 128), f32)
    ranks = []
    for b in range(seqs):
        ranks.append(earlier)
        earlier = earlier + named[b : b + 1]
    rank = jnp.concatenate(ranks, 0)
    chosen = (named > 0.5) & (jnp.abs(rank - (lane % 2).astype(f32)) < 0.5)
    weights = jnp.where(chosen, weights, 0.0)
    high = weights.astype(jnp.bfloat16).astype(f32)
    rest = weights - high
    middle = rest.astype(jnp.bfloat16).astype(f32)
    low = rest - middle
    terms = jnp.concatenate([high, middle, low, jnp.zeros_like(low)], 0)
    weighting[...] = terms.astype(jnp.bfloat16)
    square = jnp.concatenate(
        [jnp.where(chosen, 1.0, 0.0), jnp.zeros((128 - seqs, 128), f32)], 0
    )
    placing[...] = square.T.astype(jnp.bfloat16)


def line_place():
    first = lax.axis_index("ctx")
    return jnp.where(lax.axis_index("exp") % 2 == 1, first // 4, first % 4)


def project_kernel(tokens_hbm, gain_hbm, w_hbm, out, tokens, gain, w_ref, small, sems):
    f32, bf16 = jnp.float32, jnp.bfloat16
    chunks = sems.shape[0]
    cols = w_hbm.shape[1]
    width = cols // chunks
    copies = [
        pltpu.make_async_copy(
            w_hbm.at[:, pl.ds(c * width, width)], w_ref.at[:, pl.ds(c * width, width)], sems.at[c]
        )
        for c in range(chunks)
    ]
    first = [
        pltpu.make_async_copy(tokens_hbm, tokens, small.at[0]),
        pltpu.make_async_copy(gain_hbm, gain, small.at[1]),
    ]
    for copy in copies[:1] + first + copies[1:]:
        copy.start()
    for copy in first:
        copy.wait()
    xf = tokens[...].astype(f32)
    scaled = (xf * gain[...]).astype(bf16)
    squares = jnp.sum(xf * xf, 1, keepdims=True) * (SQUARES / D)
    out[:, cols:] = halves(squares).astype(f32)
    for c, copy in enumerate(copies):
        copy.wait()
        at = slice(c * width, (c + 1) * width)
        out[:, at] = jnp.dot(scaled, w_ref[:, at], preferred_element_type=f32) * SHARES


def load_kernel(after, *refs):
    count = len(refs) // 2
    sems = refs[-1]
    copies = [
        pltpu.make_async_copy(refs[i], refs[count + i], sems.at[i]) for i in range(count)
    ]
    for copy in copies:
        copy.start()
    for copy in copies:
        copy.wait()


def add_kernel(m0, m1, m3, m2, *rest):
    f32, bf16 = jnp.float32, jnp.bfloat16
    out = rest[-1]
    cols = out.shape[1] - 128

    def total(at):
        p, q, r, s = (m[:, at].astype(f32) for m in (m0, m1, m2, m3))
        return (p + q) + (r + s)

    out[:, :cols] = total(slice(0, cols)).astype(bf16)
    squares = total(slice(cols, cols + 128))
    out[:, cols:] = halves((squares + pltpu.roll(squares, 64, 1))[:, :1])


def attend_kernel(
    seqs, shares, cosine, sine, live_ref, owns, k_ref, v_ref, after, out, rows
):
    f32, bf16 = jnp.float32, jnp.bfloat16
    qh, kvh, hd = QUERY_HEADS, KEY_VALUE_HEADS, HEAD_DIMENSION
    group = qh // kvh
    positions = k_ref.shape[1]

    def share(h):
        return shares[:, h * hd : (h + 1) * hd]

    squares = share(qh + 2 * kvh)
    norm = lax.rsqrt((squares + pltpu.roll(squares, 64, 1)) / SQUARES + 1e-06) / SHARES
    cos, sin = cosine[...] * norm, sine[...] * norm
    scale = hd**-0.5
    cos_q, sin_q = cos * scale, sin * scale
    for h in range(qh):
        v = share(h)
        rows[h * seqs : (h + 1) * seqs, :] = v * cos_q + pltpu.roll(v, hd // 2, 1) * sin_q
    for h in range(qh, qh + kvh):
        v = share(h)
        rows[h * seqs : (h + 1) * seqs, :] = v * cos + pltpu.roll(v, hd // 2, 1) * sin
    for h in range(qh + kvh, qh + 2 * kvh):
        rows[h * seqs : (h + 1) * seqs, :] = share(h) * norm

    def grouped(first, b):
        at = [(first + g) * seqs + b for g in range(kvh)]
        return jnp.concatenate(
            [jnp.broadcast_to(rows[i : i + 1, :], (group, hd)) for i in at], 0
        )

    owns_new = jnp.broadcast_to(owns[0:1, :], (qh, 128))[:, :1] > 0.5
    zero = jnp.zeros((group, hd), f32)
    lanes = lane_ids()
    logs = jnp.zeros((qh, 128), f32)
    scores, fresh = [], []
    for b in range(seqs):
        q = rows[pl.ds(b, qh, stride=seqs), :]
        fresh.append(jnp.where(owns_new, jnp.sum(q * grouped(qh, b), 1, keepdims=True), -1e30))
        wide = jnp.concatenate(
            [
                jnp.concatenate(
                    [q[g * group : (g + 1) * group] if c == g else zero for c in range(kvh)], 1
                )
                for g in range(kvh)
            ],
            0,
        )
        high = wide.astype(bf16)
        low = (wide - high.astype(f32)).astype(bf16)
        both = lax.dot_general(
            jnp.concatenate([high, low], 0),
            k_ref[b],
            (((1,), (1,)), ((), ())),
            preferred_element_type=f32,
        )
        scores.append(both[:qh] + both[qh:])
    tops, weights, news, totals = [], [], [], []
    for b in range(seqs):
        live = jnp.broadcast_to(live_ref[b : b + 1, :], (qh, positions)) > 0.5
        s = jnp.where(live, scores[b], -1e30)
        top = jnp.maximum(jnp.max(s, 1, keepdims=True), fresh[b])
        p = jnp.where(live, jnp.exp(s - top), 0.0)
        p_new = jnp.where(owns_new, jnp.exp(fresh[b] - top), 0.0)
        tops.append(top)
        weights.append(p.astype(bf16))
        news.append(p_new)
        totals.append(jnp.sum(p, 1, keepdims=True) + p_new)
    for b in range(seqs):
        acc = jnp.dot(weights[b], v_ref[b], preferred_element_type=f32)
        acc = jnp.concatenate(
            [acc[g * group : (g + 1) * group, g * hd : (g + 1) * hd] for g in range(kvh)], 0
        )
        some = totals[b] > 0
        safe = jnp.where(some, totals[b], 1.0)
        value = (acc + news[b] * grouped(qh + kvh, b)) / safe
        out[b * qh : (b + 1) * qh, :] = value.astype(bf16)
        log = jnp.where(some, tops[b] + jnp.log(safe), -1e30)
        logs = jnp.where(lanes == b, log, logs)
    out[seqs * qh : (seqs + 1) * qh, :] = spread(logs, seqs)


def merged(seqs, parts):
    qh = QUERY_HEADS
    logs = [gather_terms(p[seqs * qh : (seqs + 1) * qh, :], seqs) for p in parts]
    top = jnp.maximum(jnp.maximum(logs[0], logs[1]), jnp.maximum(logs[2], logs[3]))
    weights = [jnp.exp(v - top) for v in logs]
    total = (weights[0] + weights[1]) + (weights[2] + weights[3])
    shares = [w / total for w in weights]
    values = []
    for b in range(seqs):
        v = [
            p[b * qh : (b + 1) * qh, :].astype(jnp.float32) * w[:, b : b + 1]
            for p, w in zip(parts, shares)
        ]
        values.append((v[0] + v[1]) + (v[2] + v[3]))
    return values, top + jnp.log(total)


def merge_kernel(seqs, p0, p1, p3, p2, after, out):
    qh = QUERY_HEADS
    values, log = merged(seqs, (p0, p1, p2, p3))
    for b in range(seqs):
        out[b * qh : (b + 1) * qh, :] = values[b].astype(jnp.bfloat16)
    out[seqs * qh : (seqs + 1) * qh, :] = spread(log, seqs)


def finish_kernel(seqs, p0, p1, p3, p2, tokens, placing, w_ref, context, resid, outgoing, rows):
    f32, bf16 = jnp.float32, jnp.bfloat16
    qh = QUERY_HEADS
    values, _ = merged(seqs, (p0, p1, p2, p3))
    for b in range(seqs):
        rows[pl.ds(b, qh, stride=seqs), :] = values[b]
    whole = jnp.concatenate([rows[h * seqs : (h + 1) * seqs, :] for h in range(qh)], 1).astype(bf16)
    context[...] = whole
    attn = jnp.dot(whole, w_ref[...], preferred_element_type=f32)
    after = (tokens[...].astype(f32) + attn).astype(bf16)
    resid[...] = after
    padded = jnp.concatenate(
        [after.astype(f32), jnp.zeros((placing.shape[1] - seqs, after.shape[1]), f32)], 0
    ).astype(bf16)
    outgoing[...] = jnp.dot(placing[...], padded, preferred_element_type=f32).astype(bf16)


def own_rows(capacity, per_source, n_rows, width, j):
    row = lax.broadcasted_iota(jnp.int32, (n_rows, width), 0)
    return lax.rem(row, per_source) // capacity == j


def gate_up_kernel(capacity, x_ref, gain, w_ref, *outs):
    f32, bf16 = jnp.float32, jnp.bfloat16
    n_rows, width = x_ref.shape
    experts, _, cols = w_ref.shape
    part = n_rows // len(outs)
    place = line_place()
    xf = jnp.concatenate(
        [
            x_ref[pl.ds(pl.multiple_of((place ^ s) * part, part), part), :]
            for s in range(len(outs))
        ],
        0,
    ).astype(f32)
    squares = halves(jnp.sum(xf * xf, 1, keepdims=True))
    gained = xf * gain[...]
    blocks = [
        jnp.where(own_rows(capacity, experts * capacity, n_rows, width, j), gained, 0.0).astype(bf16)
        for j in range(experts)
    ]
    for s, out in enumerate(outs):
        out[:, cols:] = squares[s * part : (s + 1) * part]
    step = 256
    for c in range(0, cols, step):
        total = jnp.dot(blocks[0], w_ref[0, :, c : c + step], preferred_element_type=f32)
        for j in range(1, experts):
            total += jnp.dot(blocks[j], w_ref[j, :, c : c + step], preferred_element_type=f32)
        total = total.astype(bf16)
        for s, out in enumerate(outs):
            out[:, c : c + step] = total[s * part : (s + 1) * part]


def activate_kernel(m0, m1, m3, m2, out):
    f32, bf16 = jnp.float32, jnp.bfloat16
    hidden = out.shape[1]

    def total(at):
        p, q, r, s = (m[:, at].astype(f32) for m in (m0, m1, m2, m3))
        return (p + q) + (r + s)

    squares = total(slice(2 * hidden, 2 * hidden + 128))
    norm = lax.rsqrt((squares + pltpu.roll(squares, 64, 1)) / D + 1e-06)[:, :1]
    gate = total(slice(0, hidden)) * norm
    up = total(slice(hidden, 2 * hidden)) * norm
    out[...] = (gate / (1.0 + jnp.exp(-gate)) * up).astype(bf16)


def down_kernel(capacity, x0, x1, x3, x2, w_ref, out):
    f32 = jnp.float32
    xf = jnp.concatenate([x[...].astype(f32) for x in (x0, x1, x2, x3)], 0)
    n_rows, width = xf.shape
    part = n_rows // 4
    experts = w_ref.shape[0]
    total = None
    for j in range(experts):
        mine = own_rows(capacity, experts * capacity, n_rows, width, j)
        block = jnp.where(mine, xf, 0.0).astype(jnp.bfloat16)
        share = jnp.dot(block, w_ref[j], preferred_element_type=f32)
        total = share if total is None else total + share
    total = total.astype(jnp.bfloat16)
    place = line_place()
    for s in range(4):
        at = pl.ds(pl.multiple_of((place ^ s) * part, part), part)
        out[at, :] = total[s * part : (s + 1) * part]


def combine_kernel(resid, weighting, returned, out):
    f32, bf16 = jnp.float32, jnp.bfloat16
    seqs = resid.shape[0]
    sums = jnp.dot(weighting[...], returned[...], preferred_element_type=f32)
    moe = (sums[:seqs] + sums[seqs : 2 * seqs]) + sums[2 * seqs : 3 * seqs]
    out[...] = (resid[...].astype(f32) + moe).astype(bf16)


VM = pl.BlockSpec(memory_space=pltpu.VMEM)
ANY = pl.BlockSpec(memory_space=pl.ANY)
HBM = pl.BlockSpec(memory_space=pltpu.HBM)
SM = pl.BlockSpec(memory_space=pltpu.SMEM)


def shape(dims, dtype=jnp.bfloat16):
    return jax.ShapeDtypeStruct(dims, dtype)


def call(kernel, name, out, inputs, specs, scratch=(), mib=8):
    return pl.pallas_call(
        kernel,
        out_shape=out,
        in_specs=specs,
        out_specs=jax.tree.map(lambda _: VM, out),
        scratch_shapes=list(scratch),
        compiler_params=pltpu.CompilerParams(vmem_limit_bytes=mib << 20),
        name=name,
    )(*inputs)


def near(array):
    return pltpu.with_memory_space_constraint(array, pltpu.VMEM)


def load(after, *arrays):
    kept = [pltpu.with_memory_space_constraint(a, pltpu.HBM) for a in arrays]
    return call(
        load_kernel,
        "load",
        tuple(pltpu.VMEM(a.shape, a.dtype) for a in arrays),
        (near(after), *kept),
        [VM] + [HBM] * len(arrays),
        [pltpu.SemaphoreType.DMA((len(arrays),))],
    )


def local(
    tokens,
    attn_gain,
    w_qkv,
    w_out,
    k_cache,
    value_cache,
    lengths,
    moe_gain,
    routes,
    gates,
    w_in,
    w_down,
):
    f32, bf16 = jnp.float32, jnp.bfloat16
    seqs, slice_width = tokens.shape
    hd = HEAD_DIMENSION
    hidden = w_down.shape[1]
    local_exp = w_in.shape[0]
    n_ctx, n_exp = lax.axis_size("ctx"), lax.axis_size("exp")
    experts_all = local_exp * n_exp
    top_k = routes.shape[1]
    capacity = 2 * seqs * top_k // experts_all
    per_source = local_exp * capacity

    cols = w_qkv.shape[1]
    message = call(
        project_kernel,
        "project",
        pltpu.VMEM((seqs, cols + 128), f32),
        [
            pltpu.with_memory_space_constraint(a, pltpu.HBM)
            for a in (tokens, attn_gain[None], w_qkv)
        ],
        [HBM] * 3,
        [
            pltpu.VMEM(tokens.shape, bf16),
            pltpu.VMEM((1, slice_width), f32),
            pltpu.VMEM(w_qkv.shape, bf16),
            pltpu.SemaphoreType.DMA((2,)),
            pltpu.SemaphoreType.DMA((2,)),
        ],
    )
    whole, message = message, lax.optimization_barrier(message.astype(jnp.float16))
    got = exchange(message, 0, n_ctx, n_exp)
    keys, values = load(whole, k_cache, value_cache)
    live, owns, placing, weighting = call(
        prepare_kernel,
        "prepare",
        (
            pltpu.VMEM((seqs, 128), f32),
            pltpu.VMEM((seqs, 128), f32),
            pltpu.VMEM((128, 128), bf16),
            pltpu.VMEM((4 * seqs, 128), bf16),
        ),
        (lengths, routes, gates, near(whole)),
        [SM] + [VM] * 3,
    )
    cosine, sine = rotation(lengths, hd)
    total = added([message] + got)
    message = lax.optimization_barrier(total.astype(jnp.float16))
    shares = added([message] + exchange(message, 1, n_ctx, n_exp))
    (w_near,) = load(total, w_out)

    part = call(
        functools.partial(attend_kernel, seqs),
        "attend",
        shape(((seqs + 1) * QUERY_HEADS, hd)),
        (shares, cosine, sine, near(live), near(owns), near(keys), near(values), near(w_near)),
        [VM] * 8,
        [pltpu.VMEM((cols // hd * seqs, hd), f32)],
    )
    parts = [part] + exchange(part, 0, n_ctx, n_exp)
    (w_in_near,) = load(part, w_in)
    part = call(
        functools.partial(merge_kernel, seqs),
        "merge",
        shape(part.shape),
        parts + [near(w_in_near)],
        [VM] * 5,
    )
    context, resid, outgoing = call(
        functools.partial(finish_kernel, seqs),
        "finish",
        (
            pltpu.VMEM((seqs, QUERY_HEADS * hd), bf16),
            shape(tokens.shape),
            shape((placing.shape[0], slice_width)),
        ),
        [part] + exchange(part, 1, n_ctx, n_exp) + [tokens, near(placing), near(w_near)],
        [VM] * 7,
        [pltpu.VMEM(((QUERY_HEADS + 1) * seqs, hd), f32)],
    )

    n_rows = n_exp * per_source
    rows = lax.all_to_all(
        outgoing.reshape(n_exp, per_source, slice_width), "exp", split_axis=0, concat_axis=0, tiled=True
    )
    side = 4
    wide = 2 * hidden + 128
    sent = call(
        functools.partial(gate_up_kernel, capacity),
        "gate_up",
        (shape((n_rows // side, wide)),) * side,
        (rows.reshape(n_rows, slice_width), moe_gain[None], near(w_in_near)),
        [VM] * 3,
    )
    got = [sent[0]] + exchange(sent[1:], 0, n_ctx, n_exp)[::-1]
    w_down_near, context = pl.pallas_call(
        load_kernel,
        out_shape=(pltpu.VMEM(w_down.shape, bf16), shape(context.shape)),
        in_specs=[VM, HBM, VM],
        out_specs=(VM, HBM),
        scratch_shapes=[pltpu.SemaphoreType.DMA((2,))],
        compiler_params=pltpu.CompilerParams(vmem_limit_bytes=8 << 20),
        name="settle",
    )(near(sent[0]), pltpu.with_memory_space_constraint(w_down, pltpu.HBM), near(context))
    total = call(
        add_kernel, "add_rows", shape(got[0].shape), got + [near(w_down_near)], [VM] * 5
    )
    act = call(
        activate_kernel,
        "activate",
        shape((n_rows // side, hidden)),
        [total] + exchange(total, 1, n_ctx, n_exp),
        [VM] * 4,
    )
    expert_out = call(
        functools.partial(down_kernel, capacity),
        "down",
        shape((n_rows, slice_width)),
        [act] + exchange(act, 0, n_ctx, n_exp) + [near(w_down_near)],
        [VM] * 5,
    )
    returned = lax.all_to_all(
        expert_out.reshape(n_exp, per_source, slice_width), "exp", split_axis=0, concat_axis=0, tiled=True
    )
    layer_out = call(
        combine_kernel,
        "combine",
        shape(tokens.shape),
        (resid, near(weighting), returned.reshape(n_rows, slice_width)),
        [VM] * 3,
    )
    return (context, layer_out)


def solution(mesh):
    placed = (
        P("exp", "ctx"),
        P("ctx"),
        P("ctx", None),
        P(None, "ctx"),
        P("exp", "ctx", None),
        P("exp", "ctx", None),
        P("exp"),
        P("ctx"),
        P("exp", None),
        P("exp", None),
        P("exp", "ctx", None),
        P("exp", None, "ctx"),
    )
    return jax.shard_map(
        local,
        mesh=mesh,
        in_specs=placed,
        out_specs=(P("exp", None), P("exp", "ctx")),
        check_vma=False,
    )
```

```python
import functools

import jax
import jax.numpy as jnp
from jax import lax
from jax.experimental import pallas as pl
from jax.experimental.pallas import tpu as pltpu
from jax.sharding import PartitionSpec as P

D = 4096
QUERY_HEADS = 32
KEY_VALUE_HEADS = 4
HEAD_DIMENSION = 128
AXES = ("ctx", "exp")
SQUARES = 1024.0
SHARES = 16.0


def exchange(value, stage, n_ctx, n_exp, first=0):
    side = 4
    got = {}
    for step in (2, 3, 1) if isinstance(value, (list, tuple)) else (1, 3, 2):
        pairs = []
        for i in range(n_ctx):
            for e in range(n_exp):
                j = i ^ step if (e & 1) == stage ^ first else i ^ (side * step)
                pairs.append((i * n_exp + e, j * n_exp + e))
        sent = value[step - 1] if isinstance(value, (list, tuple)) else value
        got[step] = lax.ppermute(sent, AXES, pairs)
    return [got[step] for step in (1, 3, 2)]


def rotation(pos, size):
    half = size // 2
    freq = jnp.exp(-jnp.log(1000000.0) * jnp.arange(half).astype(jnp.float32) / half)
    angle = pos.astype(jnp.float32)[:, None] * freq[None, :]
    cosine, sine = jnp.cos(angle), jnp.sin(angle)
    return jnp.concatenate([cosine, cosine], -1), jnp.concatenate([-sine, sine], -1)


def lane_ids():
    return lax.broadcasted_iota(jnp.int32, (QUERY_HEADS, 128), 1)


def spread(log, seqs):
    log = jnp.where(lane_ids() < seqs, log, 0.0)
    high = log.astype(jnp.bfloat16).astype(jnp.float32)
    rest = log - high
    middle = rest.astype(jnp.bfloat16).astype(jnp.float32)
    low = rest - middle
    terms = high + pltpu.roll(middle, seqs, 1) + pltpu.roll(low, 2 * seqs, 1)
    return terms.astype(jnp.bfloat16)


def gather_terms(block, seqs):
    terms = block.astype(jnp.float32)
    return (terms + pltpu.roll(terms, 128 - seqs, 1)) + pltpu.roll(terms, 128 - 2 * seqs, 1)


def halves(value):
    high = value.astype(jnp.bfloat16).astype(jnp.float32)
    lane = lax.broadcasted_iota(jnp.int32, (value.shape[0], 128), 1)
    return jnp.where(lane < 64, high, value - high).astype(jnp.bfloat16)


def added(arrays):
    own, one, three, two = (a.astype(jnp.float32) for a in arrays)
    return (own + one) + (three + two)


def prepare_kernel(lengths, routes, gates, after, live, owns, placing, weighting):
    f32 = jnp.float32
    seqs, top_k = routes.shape
    lane = lax.broadcasted_iota(jnp.int32, (seqs, 128), 1)
    row = lax.broadcasted_iota(jnp.int32, (seqs, 128), 0)
    first = lax.axis_index("ctx")
    limits = jnp.zeros((seqs, 128), jnp.int32)
    for b in range(seqs):
        limits = jnp.where(row == b, lengths[b], limits)
    live[...] = jnp.where(lane + first * 128 < limits, 1.0, 0.0)
    owns[...] = jnp.where(lane * 0 + first == 0, 1.0, 0.0)
    named = jnp.zeros((seqs, 128), f32)
    weights = jnp.zeros((seqs, 128), f32)
    for k in range(top_k):
        hit = jnp.broadcast_to(routes[:, k : k + 1], (seqs, 128)) == lane // 2
        named += jnp.where(hit, 1.0, 0.0)
        weights += jnp.where(hit, jnp.broadcast_to(gates[:, k : k + 1], (seqs, 128)), 0.0)
    earlier = jnp.zeros((1, 128), f32)
    ranks = []
    for b in range(seqs):
        ranks.append(earlier)
        earlier = earlier + named[b : b + 1]
    rank = jnp.concatenate(ranks, 0)
    chosen = (named > 0.5) & (jnp.abs(rank - (lane % 2).astype(f32)) < 0.5)
    weights = jnp.where(chosen, weights, 0.0)
    high = weights.astype(jnp.bfloat16).astype(f32)
    rest = weights - high
    middle = rest.astype(jnp.bfloat16).astype(f32)
    low = rest - middle
    terms = jnp.concatenate([high, middle, low, jnp.zeros_like(low)], 0)
    weighting[...] = terms.astype(jnp.bfloat16)
    square = jnp.concatenate(
        [jnp.where(chosen, 1.0, 0.0), jnp.zeros((128 - seqs, 128), f32)], 0
    )
    placing[...] = square.T.astype(jnp.bfloat16)


def line_place():
    first = lax.axis_index("ctx")
    return jnp.where(lax.axis_index("exp") % 2 == 1, first % 4, first // 4)


def project_kernel(tokens_hbm, gain_hbm, w_hbm, out, tokens, gain, w_ref, small, sems):
    f32, bf16 = jnp.float32, jnp.bfloat16
    chunks = sems.shape[0]
    cols = w_hbm.shape[1]
    width = cols // chunks
    copies = [
        pltpu.make_async_copy(
            w_hbm.at[:, pl.ds(c * width, width)], w_ref.at[:, pl.ds(c * width, width)], sems.at[c]
        )
        for c in range(chunks)
    ]
    first = [
        pltpu.make_async_copy(tokens_hbm, tokens, small.at[0]),
        pltpu.make_async_copy(gain_hbm, gain, small.at[1]),
    ]
    for copy in copies[:1] + first + copies[1:]:
        copy.start()
    for copy in first:
        copy.wait()
    xf = tokens[...].astype(f32)
    scaled = (xf * gain[...]).astype(bf16)
    squares = jnp.sum(xf * xf, 1, keepdims=True) * (SQUARES / D)
    out[:, cols:] = halves(squares).astype(f32)
    for c, copy in enumerate(copies):
        copy.wait()
        at = slice(c * width, (c + 1) * width)
        out[:, at] = jnp.dot(scaled, w_ref[:, at], preferred_element_type=f32) * SHARES


def load_kernel(after, *refs):
    count = len(refs) // 2
    sems = refs[-1]
    copies = [
        pltpu.make_async_copy(refs[i], refs[count + i], sems.at[i]) for i in range(count)
    ]
    for copy in copies:
        copy.start()
    for copy in copies:
        copy.wait()


def add_kernel(m0, m1, m3, m2, *rest):
    f32, bf16 = jnp.float32, jnp.bfloat16
    out = rest[-1]
    cols = out.shape[1] - 128

    def total(at):
        p, q, r, s = (m[:, at].astype(f32) for m in (m0, m1, m2, m3))
        return (p + q) + (r + s)

    out[:, :cols] = total(slice(0, cols)).astype(bf16)
    squares = total(slice(cols, cols + 128))
    out[:, cols:] = halves((squares + pltpu.roll(squares, 64, 1))[:, :1])


def attend_kernel(
    seqs, shares, cosine, sine, live_ref, owns, k_ref, v_ref, after, out, rows
):
    f32, bf16 = jnp.float32, jnp.bfloat16
    qh, kvh, hd = QUERY_HEADS, KEY_VALUE_HEADS, HEAD_DIMENSION
    group = qh // kvh
    positions = k_ref.shape[1]

    def share(h):
        return shares[:, h * hd : (h + 1) * hd]

    squares = share(qh + 2 * kvh)
    norm = lax.rsqrt((squares + pltpu.roll(squares, 64, 1)) / SQUARES + 1e-06) / SHARES
    cos, sin = cosine[...] * norm, sine[...] * norm
    scale = hd**-0.5
    cos_q, sin_q = cos * scale, sin * scale
    for h in range(qh):
        v = share(h)
        rows[h * seqs : (h + 1) * seqs, :] = v * cos_q + pltpu.roll(v, hd // 2, 1) * sin_q
    for h in range(qh, qh + kvh):
        v = share(h)
        rows[h * seqs : (h + 1) * seqs, :] = v * cos + pltpu.roll(v, hd // 2, 1) * sin
    for h in range(qh + kvh, qh + 2 * kvh):
        rows[h * seqs : (h + 1) * seqs, :] = share(h) * norm

    def grouped(first, b):
        at = [(first + g) * seqs + b for g in range(kvh)]
        return jnp.concatenate(
            [jnp.broadcast_to(rows[i : i + 1, :], (group, hd)) for i in at], 0
        )

    owns_new = jnp.broadcast_to(owns[0:1, :], (qh, 128))[:, :1] > 0.5
    zero = jnp.zeros((group, hd), f32)
    lanes = lane_ids()
    logs = jnp.zeros((qh, 128), f32)
    scores, fresh = [], []
    for b in range(seqs):
        q = rows[pl.ds(b, qh, stride=seqs), :]
        fresh.append(jnp.where(owns_new, jnp.sum(q * grouped(qh, b), 1, keepdims=True), -1e30))
        wide = jnp.concatenate(
            [
                jnp.concatenate(
                    [q[g * group : (g + 1) * group] if c == g else zero for c in range(kvh)], 1
                )
                for g in range(kvh)
            ],
            0,
        )
        high = wide.astype(bf16)
        low = (wide - high.astype(f32)).astype(bf16)
        both = lax.dot_general(
            jnp.concatenate([high, low], 0),
            k_ref[b],
            (((1,), (1,)), ((), ())),
            preferred_element_type=f32,
        )
        scores.append(both[:qh] + both[qh:])
    tops, weights, news, totals = [], [], [], []
    for b in range(seqs):
        live = jnp.broadcast_to(live_ref[b : b + 1, :], (qh, positions)) > 0.5
        s = jnp.where(live, scores[b], -1e30)
        top = jnp.maximum(jnp.max(s, 1, keepdims=True), fresh[b])
        p = jnp.where(live, jnp.exp(s - top), 0.0)
        p_new = jnp.where(owns_new, jnp.exp(fresh[b] - top), 0.0)
        tops.append(top)
        weights.append(p.astype(bf16))
        news.append(p_new)
        totals.append(jnp.sum(p, 1, keepdims=True) + p_new)
    for b in range(seqs):
        acc = jnp.dot(weights[b], v_ref[b], preferred_element_type=f32)
        acc = jnp.concatenate(
            [acc[g * group : (g + 1) * group, g * hd : (g + 1) * hd] for g in range(kvh)], 0
        )
        some = totals[b] > 0
        safe = jnp.where(some, totals[b], 1.0)
        value = (acc + news[b] * grouped(qh + kvh, b)) / safe
        out[b * qh : (b + 1) * qh, :] = value.astype(bf16)
        log = jnp.where(some, tops[b] + jnp.log(safe), -1e30)
        logs = jnp.where(lanes == b, log, logs)
    out[seqs * qh : (seqs + 1) * qh, :] = spread(logs, seqs)


def merged(seqs, parts):
    qh = QUERY_HEADS
    logs = [gather_terms(p[seqs * qh : (seqs + 1) * qh, :], seqs) for p in parts]
    top = jnp.maximum(jnp.maximum(logs[0], logs[1]), jnp.maximum(logs[2], logs[3]))
    weights = [jnp.exp(v - top) for v in logs]
    total = (weights[0] + weights[1]) + (weights[2] + weights[3])
    shares = [w / total for w in weights]
    values = []
    for b in range(seqs):
        v = [
            p[b * qh : (b + 1) * qh, :].astype(jnp.float32) * w[:, b : b + 1]
            for p, w in zip(parts, shares)
        ]
        values.append((v[0] + v[1]) + (v[2] + v[3]))
    return values, top + jnp.log(total)


def merge_kernel(seqs, p0, p1, p3, p2, after, out):
    qh = QUERY_HEADS
    values, log = merged(seqs, (p0, p1, p2, p3))
    for b in range(seqs):
        out[b * qh : (b + 1) * qh, :] = values[b].astype(jnp.bfloat16)
    out[seqs * qh : (seqs + 1) * qh, :] = spread(log, seqs)


def finish_kernel(seqs, p0, p1, p3, p2, tokens, placing, w_ref, context, resid, outgoing, rows):
    f32, bf16 = jnp.float32, jnp.bfloat16
    qh = QUERY_HEADS
    values, _ = merged(seqs, (p0, p1, p2, p3))
    for b in range(seqs):
        rows[pl.ds(b, qh, stride=seqs), :] = values[b]
    whole = jnp.concatenate([rows[h * seqs : (h + 1) * seqs, :] for h in range(qh)], 1).astype(bf16)
    context[...] = whole
    attn = jnp.dot(whole, w_ref[...], preferred_element_type=f32)
    after = (tokens[...].astype(f32) + attn).astype(bf16)
    resid[...] = after
    padded = jnp.concatenate(
        [after.astype(f32), jnp.zeros((placing.shape[1] - seqs, after.shape[1]), f32)], 0
    ).astype(bf16)
    outgoing[...] = jnp.dot(placing[...], padded, preferred_element_type=f32).astype(bf16)


def own_rows(capacity, per_source, n_rows, width, j):
    row = lax.broadcasted_iota(jnp.int32, (n_rows, width), 0)
    return lax.rem(row, per_source) // capacity == j


def gate_up_kernel(capacity, x_ref, gain, w_ref, *outs):
    f32, bf16 = jnp.float32, jnp.bfloat16
    n_rows, width = x_ref.shape
    experts, _, cols = w_ref.shape
    part = n_rows // len(outs)
    place = line_place()
    xf = jnp.concatenate(
        [
            x_ref[pl.ds(pl.multiple_of((place ^ s) * part, part), part), :]
            for s in range(len(outs))
        ],
        0,
    ).astype(f32)
    squares = halves(jnp.sum(xf * xf, 1, keepdims=True))
    gained = xf * gain[...]
    blocks = [
        jnp.where(own_rows(capacity, experts * capacity, n_rows, width, j), gained, 0.0).astype(bf16)
        for j in range(experts)
    ]
    for s, out in enumerate(outs):
        out[:, cols:] = squares[s * part : (s + 1) * part]
    step = 256
    for c in range(0, cols, step):
        total = jnp.dot(blocks[0], w_ref[0, :, c : c + step], preferred_element_type=f32)
        for j in range(1, experts):
            total += jnp.dot(blocks[j], w_ref[j, :, c : c + step], preferred_element_type=f32)
        total = total.astype(bf16)
        for s, out in enumerate(outs):
            out[:, c : c + step] = total[s * part : (s + 1) * part]


def activate_kernel(m0, m1, m3, m2, out):
    f32, bf16 = jnp.float32, jnp.bfloat16
    hidden = out.shape[1]

    def total(at):
        p, q, r, s = (m[:, at].astype(f32) for m in (m0, m1, m2, m3))
        return (p + q) + (r + s)

    squares = total(slice(2 * hidden, 2 * hidden + 128))
    norm = lax.rsqrt((squares + pltpu.roll(squares, 64, 1)) / D + 1e-06)[:, :1]
    gate = total(slice(0, hidden)) * norm
    up = total(slice(hidden, 2 * hidden)) * norm
    out[...] = (gate / (1.0 + jnp.exp(-gate)) * up).astype(bf16)


def down_kernel(capacity, x0, x1, x3, x2, w_ref, out):
    f32 = jnp.float32
    xf = jnp.concatenate([x[...].astype(f32) for x in (x0, x1, x2, x3)], 0)
    n_rows, width = xf.shape
    part = n_rows // 4
    experts = w_ref.shape[0]
    total = None
    for j in range(experts):
        mine = own_rows(capacity, experts * capacity, n_rows, width, j)
        block = jnp.where(mine, xf, 0.0).astype(jnp.bfloat16)
        share = jnp.dot(block, w_ref[j], preferred_element_type=f32)
        total = share if total is None else total + share
    total = total.astype(jnp.bfloat16)
    place = line_place()
    for s in range(4):
        at = pl.ds(pl.multiple_of((place ^ s) * part, part), part)
        out[at, :] = total[s * part : (s + 1) * part]


def combine_kernel(resid, weighting, returned, out):
    f32, bf16 = jnp.float32, jnp.bfloat16
    seqs = resid.shape[0]
    sums = jnp.dot(weighting[...], returned[...], preferred_element_type=f32)
    moe = (sums[:seqs] + sums[seqs : 2 * seqs]) + sums[2 * seqs : 3 * seqs]
    out[...] = (resid[...].astype(f32) + moe).astype(bf16)


VM = pl.BlockSpec(memory_space=pltpu.VMEM)
ANY = pl.BlockSpec(memory_space=pl.ANY)
HBM = pl.BlockSpec(memory_space=pltpu.HBM)
SM = pl.BlockSpec(memory_space=pltpu.SMEM)


def shape(dims, dtype=jnp.bfloat16):
    return jax.ShapeDtypeStruct(dims, dtype)


def call(kernel, name, out, inputs, specs, scratch=(), mib=8):
    return pl.pallas_call(
        kernel,
        out_shape=out,
        in_specs=specs,
        out_specs=jax.tree.map(lambda _: VM, out),
        scratch_shapes=list(scratch),
        compiler_params=pltpu.CompilerParams(vmem_limit_bytes=mib << 20),
        name=name,
    )(*inputs)


def near(array):
    return pltpu.with_memory_space_constraint(array, pltpu.VMEM)


def load(after, *arrays):
    kept = [pltpu.with_memory_space_constraint(a, pltpu.HBM) for a in arrays]
    return call(
        load_kernel,
        "load",
        tuple(pltpu.VMEM(a.shape, a.dtype) for a in arrays),
        (near(after), *kept),
        [VM] + [HBM] * len(arrays),
        [pltpu.SemaphoreType.DMA((len(arrays),))],
    )


def local(
    tokens,
    attn_gain,
    w_qkv,
    w_out,
    k_cache,
    value_cache,
    lengths,
    moe_gain,
    routes,
    gates,
    w_in,
    w_down,
):
    f32, bf16 = jnp.float32, jnp.bfloat16
    seqs, slice_width = tokens.shape
    hd = HEAD_DIMENSION
    hidden = w_down.shape[1]
    local_exp = w_in.shape[0]
    n_ctx, n_exp = lax.axis_size("ctx"), lax.axis_size("exp")
    experts_all = local_exp * n_exp
    top_k = routes.shape[1]
    capacity = 2 * seqs * top_k // experts_all
    per_source = local_exp * capacity

    cols = w_qkv.shape[1]
    message = call(
        project_kernel,
        "project",
        pltpu.VMEM((seqs, cols + 128), f32),
        [
            pltpu.with_memory_space_constraint(a, pltpu.HBM)
            for a in (tokens, attn_gain[None], w_qkv)
        ],
        [HBM] * 3,
        [
            pltpu.VMEM(tokens.shape, bf16),
            pltpu.VMEM((1, slice_width), f32),
            pltpu.VMEM(w_qkv.shape, bf16),
            pltpu.SemaphoreType.DMA((2,)),
            pltpu.SemaphoreType.DMA((2,)),
        ],
    )
    whole, message = message, lax.optimization_barrier(message.astype(jnp.float16))
    got = exchange(message, 0, n_ctx, n_exp)
    keys, values = load(whole, k_cache, value_cache)
    live, owns, placing, weighting = call(
        prepare_kernel,
        "prepare",
        (
            pltpu.VMEM((seqs, 128), f32),
            pltpu.VMEM((seqs, 128), f32),
            pltpu.VMEM((128, 128), bf16),
            pltpu.VMEM((4 * seqs, 128), bf16),
        ),
        (lengths, routes, gates, near(whole)),
        [SM] + [VM] * 3,
    )
    cosine, sine = rotation(lengths, hd)
    total = added([message] + got)
    message = lax.optimization_barrier(total.astype(jnp.float16))
    shares = added([message] + exchange(message, 1, n_ctx, n_exp))
    (w_near,) = load(total, w_out)

    part = call(
        functools.partial(attend_kernel, seqs),
        "attend",
        shape(((seqs + 1) * QUERY_HEADS, hd)),
        (shares, cosine, sine, near(live), near(owns), near(keys), near(values), near(w_near)),
        [VM] * 8,
        [pltpu.VMEM((cols // hd * seqs, hd), f32)],
    )
    parts = [part] + exchange(part, 0, n_ctx, n_exp)
    (w_in_near,) = load(part, w_in)
    part = call(
        functools.partial(merge_kernel, seqs),
        "merge",
        shape(part.shape),
        parts + [near(w_in_near)],
        [VM] * 5,
    )
    context, resid, outgoing = call(
        functools.partial(finish_kernel, seqs),
        "finish",
        (
            pltpu.VMEM((seqs, QUERY_HEADS * hd), bf16),
            shape(tokens.shape),
            shape((placing.shape[0], slice_width)),
        ),
        [part] + exchange(part, 1, n_ctx, n_exp) + [tokens, near(placing), near(w_near)],
        [VM] * 7,
        [pltpu.VMEM(((QUERY_HEADS + 1) * seqs, hd), f32)],
    )

    n_rows = n_exp * per_source
    rows = lax.all_to_all(
        outgoing.reshape(n_exp, per_source, slice_width), "exp", split_axis=0, concat_axis=0, tiled=True
    )
    side = 4
    wide = 2 * hidden + 128
    sent = call(
        functools.partial(gate_up_kernel, capacity),
        "gate_up",
        (shape((n_rows // side, wide)),) * side,
        (rows.reshape(n_rows, slice_width), moe_gain[None], near(w_in_near)),
        [VM] * 3,
    )
    got = [sent[0]] + exchange(sent[1:], 0, n_ctx, n_exp, 1)[::-1]
    w_down_near, context = pl.pallas_call(
        load_kernel,
        out_shape=(pltpu.VMEM(w_down.shape, bf16), shape(context.shape)),
        in_specs=[VM, HBM, VM],
        out_specs=(VM, HBM),
        scratch_shapes=[pltpu.SemaphoreType.DMA((2,))],
        compiler_params=pltpu.CompilerParams(vmem_limit_bytes=8 << 20),
        name="settle",
    )(near(sent[0]), pltpu.with_memory_space_constraint(w_down, pltpu.HBM), near(context))
    total = call(
        add_kernel, "add_rows", shape(got[0].shape), got + [near(w_down_near)], [VM] * 5
    )
    act = call(
        activate_kernel,
        "activate",
        shape((n_rows // side, hidden)),
        [total] + exchange(total, 1, n_ctx, n_exp, 1),
        [VM] * 4,
    )
    expert_out = call(
        functools.partial(down_kernel, capacity),
        "down",
        shape((n_rows, slice_width)),
        [act] + exchange(act, 0, n_ctx, n_exp, 1) + [near(w_down_near)],
        [VM] * 5,
    )
    returned = lax.all_to_all(
        expert_out.reshape(n_exp, per_source, slice_width), "exp", split_axis=0, concat_axis=0, tiled=True
    )
    layer_out = call(
        combine_kernel,
        "combine",
        shape(tokens.shape),
        (resid, near(weighting), returned.reshape(n_rows, slice_width)),
        [VM] * 3,
    )
    return (context, layer_out)


def solution(mesh):
    placed = (
        P("exp", "ctx"),
        P("ctx"),
        P("ctx", None),
        P(None, "ctx"),
        P("exp", "ctx", None),
        P("exp", "ctx", None),
        P("exp"),
        P("ctx"),
        P("exp", None),
        P("exp", None),
        P("exp", "ctx", None),
        P("exp", None, "ctx"),
    )
    return jax.shard_map(
        local,
        mesh=mesh,
        in_specs=placed,
        out_specs=(P("exp", None), P("exp", "ctx")),
        check_vma=False,
    )
```
